32 devices in a mesh: dp: 8 (over z, x), inner: 4 (over y, core).
Axes of the slice: x: 2, y: 2, z: 4, core: 2. Of those that a mesh axis runs over, the one named last changes fastest.
Arguments:
- tokens: bfloat16 [20480, 768], P(('dp', 'inner')), may hold values from -6 to 6
- lengths: int32 [8, 3], P('dp'), may hold values from 1 to 2558, as said below
- w_qkv: bfloat16 [768, 2304], P('dp', 'inner'), may hold values from -0.3125 to 0.3125
- bias_qv: bfloat16 [1536], P(('dp', 'inner')), may hold values from -4 to 4
- w_out: bfloat16 [768, 768], P('dp', 'inner'), may hold values from -1.75 to 1.75
- bias_out: bfloat16 [768], P(('dp', 'inner')), may hold values from -3 to 3
- w_up: bfloat16 [768, 3072], P('dp', 'inner'), may hold values from -0.21875 to 0.21875
- bias_up: bfloat16 [3072], P(('dp', 'inner')), may hold values from -4 to 4
- w_down: bfloat16 [3072, 768], P('dp', 'inner'), may hold values from -0.109375 to 0.109375
- bias_down: bfloat16 [768], P(('dp', 'inner')), may hold values from -3 to 3
- gain_one: bfloat16 [768], P(('dp', 'inner')), may hold values from 0.099609375 to 1.8984375
- shift_one: bfloat16 [768], P(('dp', 'inner')), may hold values from -3 to 3
- gain_two: bfloat16 [768], P(('dp', 'inner')), may hold values from 0.099609375 to 1.8984375
- shift_two: bfloat16 [768], P(('dp', 'inner')), may hold values from -3 to 3
- cotangent: bfloat16 [20480, 768], P(('dp', 'inner')), may hold values from -6 to 6
Outputs:
- output: bfloat16 [20480, 768], P(('dp', 'inner'))
- grad_tokens: bfloat16 [20480, 768], P(('dp', 'inner'))
- grad_w_qkv: float32 [768, 2304], P('dp', 'inner')
- grad_bias_qv: float32 [1536], P(('dp', 'inner'))
- grad_w_out: float32 [768, 768], P('dp', 'inner')
- grad_bias_out: float32 [768], P(('dp', 'inner'))
- grad_w_up: float32 [768, 3072], P('dp', 'inner')
- grad_bias_up: float32 [3072], P(('dp', 'inner'))
- grad_w_down: float32 [3072, 768], P('dp', 'inner')
- grad_bias_down: float32 [768], P(('dp', 'inner'))
- grad_gain_one: float32 [768], P(('dp', 'inner'))
- grad_shift_one: float32 [768], P(('dp', 'inner'))
- grad_gain_two: float32 [768], P(('dp', 'inner'))
- grad_shift_two: float32 [768], P(('dp', 'inner'))
The draws below stay inside these ranges and needn't reach their ends.
Inputs may be any that keep to these rules, and one draw needn't show every extreme that they name: `lengths`: row d holds the token counts of the 3 items of group d in order, and they sum to 2560. In every row one item, at a place drawn from the seed, begins within the first 640 tokens of the group and ends within the last 640; each other item has fewer than 320 tokens. In row 0 every other item has one token.
All inputs are finite; a program needn't handle non-finite values.
Results may differ from the reference program's by a relative error of at most 0.015.
The reference program's roundings to bfloat16 on the way count: a program that leaves them out, or rounds other values in their place, can miss the bound.
Values may be sent and summed in bfloat16 or wider, within the bound.
A program may use at most 192 MiB of HBM per device.

```python
import jax
import jax.numpy as jnp
from jax import lax

D = 768
HEADS = 12
HEAD_DIM = 64
FF = 3072
TOK_DEV = 640
ITEMS = 3
GROUP_TOK = 2560
TOKENS = 20480
N_DP = 8


def draw_lengths(key, part):
    key = jax.random.fold_in(key, 11)
    key_short, key_place = jax.random.split(key)
    shorts = jax.random.randint(key_short, (N_DP, ITEMS - 1), 1, TOK_DEV // (ITEMS - 1), dtype=jnp.int32)
    row = jnp.arange(N_DP, dtype=jnp.int32)[:, None]
    shorts = jnp.where(row == 0, jnp.ones_like(shorts), shorts).astype(jnp.int32)
    place = jax.random.randint(key_place, (N_DP, 1), 0, ITEMS, dtype=jnp.int32)
    longest = GROUP_TOK - jnp.sum(shorts, axis=1, keepdims=True)
    slot = jnp.arange(ITEMS, dtype=jnp.int32)[None, :]
    index = jnp.clip(slot - (slot > place).astype(jnp.int32), 0, ITEMS - 2)
    picked = jnp.take_along_axis(shorts, index, axis=1)
    return jnp.where(slot == place, longest, picked).astype(jnp.int32)


def spiked(values, key, source, target, blocks, factor):
    def block_of(dim):
        return (jnp.arange(values.shape[dim]) // (values.shape[dim] // blocks)).reshape((-1,) + (1,) * (values.ndim - 1 - dim))

    first = jax.random.permutation(key, blocks)[block_of(target)]
    second = (block_of(target) + blocks // 2) % blocks
    return jnp.where((block_of(source) == first) | (block_of(source) == second), factor * values, values)


def level_of(key, dims, shards, low, high):
    factor_of, own = 1.0, jax.random.fold_in(key, 6)
    for dim, blocks in shards:
        heights = jnp.exp(jax.random.uniform(jax.random.fold_in(own, dim), (blocks,), jnp.float32, low / len(shards), high / len(shards)))
        factor_of = factor_of * jnp.repeat(heights, dims[dim] // blocks).reshape([-1 if axis == dim else 1 for axis in range(len(dims))])
    return factor_of


def scatter_about(key, shape, width, bound, cuts=(), kind=jnp.bfloat16):
    entries = jax.random.normal(key, shape, jnp.float32) * width
    if len(cuts) > 0:
        entries = level_of(key, shape, cuts, -0.22, 0.18) * entries
    return jnp.clip(entries, min=-bound, max=bound).astype(kind)


def gaussian_with(stream_key, shape, width, limit, shards, heavy, kind=jnp.bfloat16):
    values = width * jax.random.normal(stream_key, shape, jnp.float32)
    if shards:
        values = values * level_of(stream_key, shape, shards, -0.22, 0.18)
    return jnp.clip(spiked(values, jax.random.fold_in(stream_key, 3), *heavy), -limit, limit).astype(kind)


def setup_inputs(seed: int = 0) -> dict:
    arg_keys = jax.random.split(jax.random.key(seed), 16)
    return {
        "tokens": gaussian_with(arg_keys[0], (TOKENS, D), 1.0, 6.0, ((0, 32),), (0, 1, 32, 2.75)),
        "lengths": draw_lengths(jax.random.fold_in(arg_keys[15], 71), 0),
        "w_qkv": scatter_about(arg_keys[2], (D, 3 * D), (D // 2) ** -0.5, 0.3125, ((0, 8), (1, 4))),
        "bias_qv": scatter_about(arg_keys[3], (2 * D,), 0.8, 4.0, ((0, 32),)),
        "w_out": scatter_about(arg_keys[4], (D, D), (max(D // 64, 4)) ** -0.5, 1.75, ((0, 8), (1, 4))),
        "bias_out": scatter_about(arg_keys[5], (D,), 0.5, 3.0, ((0, 32),)),
        "w_up": scatter_about(arg_keys[6], (D, FF), D ** -0.5, 0.21875, ((0, 8), (1, 4))),
        "bias_up": scatter_about(arg_keys[7], (FF,), 0.8, 4.0, ((0, 32),)),
        "w_down": scatter_about(arg_keys[8], (FF, D), FF ** -0.5, 0.109375, ((0, 8), (1, 4))),
        "bias_down": scatter_about(arg_keys[9], (D,), 0.5, 3.0, ((0, 32),)),
        "gain_one": jnp.clip(1.0 + 0.18 * jax.random.normal(arg_keys[10], (D,), jnp.float32), 0.099609375, 1.8984375).astype(jnp.bfloat16),
        "shift_one": scatter_about(arg_keys[11], (D,), 0.5, 3.0, ((0, 32),)),
        "gain_two": jnp.clip(1.0 + 0.18 * jax.random.normal(arg_keys[12], (D,), jnp.float32), 0.099609375, 1.8984375).astype(jnp.bfloat16),
        "shift_two": scatter_about(arg_keys[13], (D,), 0.5, 3.0, ((0, 32),)),
        "cotangent": gaussian_with(arg_keys[14], (TOKENS, D), 1.0, 6.0, ((0, 32),), (0, 1, 32, 2.75)),
    }


EPS = 1e-06
NEG = -1e+30

@jax.custom_vjp
def low(v):
    return lax.optimization_barrier(v.astype(jnp.bfloat16)).astype(jnp.float32)

@jax.custom_vjp
def low_back(v):
    return v

def low_keep(v):
    return (low(v), None)

def low_pass(kept, grad):
    return (grad,)

def back_keep(v):
    return (v, None)

def back_low(kept, grad):
    return (low(grad),)
low.defvjp(low_keep, low_pass)
low_back.defvjp(back_keep, back_low)

def product(a, b):
    return jnp.dot(a, b, precision=lax.Precision.HIGHEST, preferred_element_type=jnp.float32)

def layer_norm(value, gain, shift):
    mean = lax.optimization_barrier(jnp.mean(value, axis=-1, keepdims=True))
    centred = value - mean
    spread = lax.optimization_barrier(jnp.mean(centred * centred, axis=-1, keepdims=True))
    return centred * lax.rsqrt(spread + EPS) * gain + shift

def head_attend(query, key_rows, value_rows, same):
    scores = low_back(product(query, key_rows.T)) * HEAD_DIM ** (-0.5)
    scores = jnp.where(same, scores, NEG)
    top = lax.optimization_barrier(jnp.max(scores, axis=-1, keepdims=True))
    expo = jnp.exp(scores - top)
    probs = expo / lax.optimization_barrier(jnp.sum(expo, axis=-1, keepdims=True))
    return product(low(probs), value_rows)

def group_layer(inputs, segment, params):
    w_qkv, bias_qv, w_out, bias_out, w_up, bias_up, w_down, bias_down, gain_one, shift_one, gain_two, shift_two = params
    h_one = low(layer_norm(inputs, gain_one, shift_one))
    qkv_bias = jnp.concatenate([bias_qv[:D], jnp.zeros((D,), jnp.float32), bias_qv[D:]])
    qkv = low(low_back(product(h_one, w_qkv) + qkv_bias))
    query = qkv[:, :D].reshape(GROUP_TOK, HEADS, HEAD_DIM).transpose(1, 0, 2)
    keys = qkv[:, D:2 * D].reshape(GROUP_TOK, HEADS, HEAD_DIM).transpose(1, 0, 2)
    values = qkv[:, 2 * D:].reshape(GROUP_TOK, HEADS, HEAD_DIM).transpose(1, 0, 2)
    same = segment[:, None] == segment[None, :]

    def one_head(parts):
        return head_attend(parts[0], parts[1], parts[2], same)
    heads_out = lax.map(jax.checkpoint(one_head), (query, keys, values))
    attended = low(low_back(heads_out.transpose(1, 0, 2).reshape(GROUP_TOK, D)))
    mixed = low_back(product(attended, w_out) + bias_out)
    residual = inputs + mixed
    h_two = low(layer_norm(residual, gain_two, shift_two))
    up = low_back(product(h_two, w_up) + bias_up)
    act = low(jax.nn.gelu(up, approximate=False))
    down = low_back(product(act, w_down) + bias_down)
    return residual + down

def reference(tokens, lengths, w_qkv, bias_qv, w_out, bias_out, w_up, bias_up, w_down, bias_down, gain_one, shift_one, gain_two, shift_two, cotangent):
    params = tuple((a.astype(jnp.float32) for a in (w_qkv, bias_qv, w_out, bias_out, w_up, bias_up, w_down, bias_down, gain_one, shift_one, gain_two, shift_two)))
    groups = tokens.astype(jnp.float32).reshape(N_DP, GROUP_TOK, D)
    ends = jnp.cumsum(lengths, axis=1).astype(jnp.int32)
    place = jnp.arange(GROUP_TOK, dtype=jnp.int32)
    segment = lax.optimization_barrier(jnp.sum((place[None, :, None] >= ends[:, None, :]).astype(jnp.int32), axis=2)).astype(jnp.int32)

    def forward(group_inputs, weights):

        def one_group(parts):
            return group_layer(parts[0], parts[1], weights)
        return lax.map(jax.checkpoint(one_group), (group_inputs, segment))
    result, pull = jax.vjp(forward, groups, params)
    upstream = cotangent.astype(jnp.float32).reshape(N_DP, GROUP_TOK, D)
    grad_groups, grads = pull(upstream)
    output = result.reshape(TOKENS, D).astype(jnp.bfloat16)
    grad_tokens = grad_groups.reshape(TOKENS, D).astype(jnp.bfloat16)
    return (output, grad_tokens, grads[0], grads[1], grads[2], grads[3], grads[4], grads[5], grads[6], grads[7], grads[8], grads[9], grads[10], grads[11])
```

```python
import functools

import jax
import jax.numpy as jnp
from jax import lax
from jax.experimental import pallas as pl
from jax.experimental.pallas import tpu as pltpu
from jax.sharding import PartitionSpec as P

D = 768
HEADS = 12
HEAD_DIM = 64
EPS = 1e-06
NEG = -1e30
LANES = 128
N_Z = 4
N_IN = 4
HP = HEADS // N_IN
CW = HP * HEAD_DIM
MESH = pl.DeviceIdType.MESH
NT = (((1,), (1,)), ((), ()))
TN = (((0,), (0,)), ((), ()))
F32, BF16 = jnp.float32, jnp.bfloat16
ANY = pl.BlockSpec(memory_space=pl.ANY)
VMEM = pl.BlockSpec(memory_space=pltpu.VMEM)
SMEM = pl.BlockSpec(memory_space=pltpu.SMEM)
VMEM_LIMIT = 60 << 20


def product(left, right):
    return jnp.dot(left, right, preferred_element_type=F32)


def product_tn(left, right):
    return lax.dot_general(left, right, TN, preferred_element_type=F32)


def product_nt(left, right):
    return lax.dot_general(left, right, NT, preferred_element_type=F32)


class Place:
    def __init__(self, n_dp):
        self.n_x = n_dp // N_Z
        self.dp = lax.axis_index("dp")
        self.inn = lax.axis_index("inner")
        self.x, self.z = self.dp % self.n_x, self.dp // self.n_x
        self.c, self.y = self.inn % 2, self.inn // 2

    def size(self, axis):
        return {"z": N_Z, "x": self.n_x, "y": 2, "c": 2}[axis]

    def peer(self, axis, k):
        if axis == "z":
            at = (self.z + k) % N_Z
            return at, (at * self.n_x + self.x, self.inn)
        if axis == "x":
            at = (self.x + k) % self.n_x
            return at, (self.z * self.n_x + at, self.inn)
        if axis == "y":
            return 1 - self.y, (self.dp, (1 - self.y) * 2 + self.c)
        return 1 - self.c, (self.dp, self.y * 2 + 1 - self.c)

    def peers(self, axis):
        return [self.peer(axis, k) + (k,) for k in range(1, self.size(axis))]


class Sems:
    def __init__(self, send, recv, local):
        self.send, self.recv, self.local = send, recv, local
        self.n = self.m = 0

    def remote(self, src, dst, device):
        i = self.n
        self.n += 1
        return pltpu.make_async_remote_copy(
            src_ref=src,
            dst_ref=dst,
            send_sem=self.send.at[i],
            recv_sem=self.recv.at[i],
            device_id=device,
            device_id_type=MESH,
        )

    def copy(self, src, dst):
        i = self.m
        self.m += 1
        return pltpu.make_async_copy(src, dst, self.local.at[i])


def sem_shapes(n_remote, n_local):
    return [
        pltpu.SemaphoreType.DMA((n_remote,)),
        pltpu.SemaphoreType.DMA((n_remote,)),
        pltpu.SemaphoreType.DMA((n_local,)),
    ]


def greet(place, axes, diagonal=False):
    devices = [device for axis in axes for _, device, _ in place.peers(axis)]
    if diagonal:
        devices.append((place.dp, (1 - place.y) * 2 + 1 - place.c))
    barrier = pltpu.get_barrier_semaphore()
    for device in devices:
        pl.semaphore_signal(barrier, inc=1, device_id=device, device_id_type=MESH)
    pl.semaphore_wait(barrier, len(devices))


def start(copies):
    for copy in copies:
        copy.start()


def wait_recv(copies):
    for copy in copies:
        copy.wait_recv()


def wait_send(copies):
    for copy in copies:
        copy.wait_send()


def params(collective_id):
    return pltpu.CompilerParams(
        collective_id=collective_id, has_side_effects=True, vmem_limit_bytes=VMEM_LIMIT
    )


class Gather:
    def __init__(self, place, sems, source, out, view, order, z_done=False):
        self.place, self.sems, self.order = place, sems, order
        p = place

        def at(inn, z, x):
            return view(out.at[inn, z, x])

        everything = slice(None)
        zs, xs = (everything if z_done else p.z), p.x
        self.own = sems.copy(source, at(p.inn, zs, xs))
        inns = [p.inn]
        self.stages = []
        for number, axis in enumerate(order):
            copies = []
            for _, device, _ in p.peers(axis):
                for inn in inns:
                    target = at(inn, zs, xs)
                    copies.append(sems.remote(source if number == 0 else target, target, device))
            self.stages.append(copies)
            if axis == "z":
                zs = everything
            elif axis == "x":
                xs = everything
            elif axis == "y":
                inns = [p.inn, (1 - p.y) * 2 + p.c]

    def step(self, number):
        if number == 0:
            self.own.start()
        else:
            if number == 1:
                self.own.wait()
            wait_recv(self.stages[number - 1])
        if number < len(self.stages):
            start(self.stages[number])

    def finish(self):
        for copies in self.stages:
            wait_send(copies)


def add_into(total, part, lead):
    shape = total.shape[:lead]
    count = 1
    for size in shape:
        count *= size

    def one(i, _):
        index, rest = [], i
        for size in reversed(shape):
            index.insert(0, rest % size)
            rest = rest // size
        index = tuple(index)
        total[index] = total[index] + part[index]
        return 0

    lax.fori_loop(0, count, one, 0)


class Scatter:
    def __init__(self, place, sems, grads, view, order, buffers, out):
        self.place, self.sems, self.order, self.out = place, sems, order, out
        p = place
        self.total, self.from_core, self.from_x, self.from_y, self.from_z = buffers
        total = self.total
        self.own = [sems.copy(view(grads.at[2 * yy + p.c]), total.at[yy]) for yy in range(2)]
        _, device, _ = p.peers("c")[0]
        self.core = [
            sems.remote(view(grads.at[2 * yy + 1 - p.c]), self.from_core.at[yy], device)
            for yy in range(2)
        ]
        self.copies = {}
        for axis in order:
            copies = []
            for at, device, k in p.peers(axis):
                if axis == "x":
                    if order[0] == "x":
                        pairs = [
                            (total.at[yy, :, at], self.from_x.at[k - 1, yy]) for yy in range(2)
                        ]
                    else:
                        pairs = [(total.at[p.y, :, at], self.from_x.at[k - 1, 0])]
                elif axis == "y":
                    if order[0] == "y":
                        pairs = [(total.at[at], self.from_y)]
                    else:
                        pairs = [(total.at[at, :, p.x], self.from_y.at[:, 0])]
                else:
                    pairs = [(total.at[p.y, at, p.x], self.from_z.at[k - 1])]
                copies += [sems.remote(src, dst, device) for src, dst in pairs]
            self.copies[axis] = copies

    def step(self, number):
        p, total, order = self.place, self.total, self.order
        if number == 0:
            start(self.own)
            start(self.core)
            return
        if number == 1:
            for copy in self.own:
                copy.wait()
            wait_recv(self.core)
            add_into(total, self.from_core, 3)
        else:
            axis = order[number - 2]
            wait_recv(self.copies[axis])
            if axis == "x":
                for k in range(self.from_x.shape[0]):
                    if order[0] == "x":
                        for yy in range(2):
                            add_into(total.at[yy, :, p.x], self.from_x.at[k, yy], 1)
                    else:
                        add_into(total.at[p.y, :, p.x], self.from_x.at[k, 0], 1)
            elif axis == "y":
                if order[0] == "y":
                    add_into(total.at[p.y], self.from_y, 2)
                else:
                    add_into(total.at[p.y, :, p.x], self.from_y.at[:, 0], 1)
            else:
                value = total[p.y, p.z, p.x].astype(F32)
                for k in range(N_Z - 1):
                    value = value + self.from_z[k].astype(F32)
                self.out[...] = value
        if number - 1 < len(order):
            start(self.copies[order[number - 1]])

    def finish(self):
        wait_send(self.core)
        for axis in self.order:
            wait_send(self.copies[axis])


def scatter_buffers(n_x, rows, cols, order):
    if order[0] == "x":
        x_shape, y_shape = (n_x - 1, 2, N_Z, rows, cols), (N_Z, 1, rows, cols)
    else:
        x_shape, y_shape = (n_x - 1, 1, N_Z, rows, cols), (N_Z, n_x, rows, cols)
    return [
        pltpu.VMEM((2, N_Z, n_x, rows, cols), BF16),
        pltpu.VMEM((2, N_Z, n_x, rows, cols), BF16),
        pltpu.VMEM(x_shape, BF16),
        pltpu.VMEM(y_shape, BF16),
        pltpu.VMEM((N_Z - 1, rows, cols), BF16),
    ]


def slot_of(device, receiver):
    return (device - receiver + N_IN - 1) % N_IN


def head_kernel(n_dp, tokens, w_units, vecs, tok_all, wq_all, vec_all, send, recv, local):
    p = Place(n_dp)
    sems = Sems(send, recv, local)
    inn, sib, far = p.inn, p.y * 2 + 1 - p.c, (1 - p.y) * 2 + p.c
    diag = (1 - p.y) * 2 + 1 - p.c
    own_tok = sems.copy(tokens, tok_all.at[N_IN - 1])
    tok_far = sems.remote(tokens, tok_all.at[slot_of(inn, far)], (p.dp, far))
    tok_sib = sems.remote(tokens, tok_all.at[slot_of(inn, sib)], (p.dp, sib))
    tok_on = sems.remote(
        tok_all.at[slot_of(far, inn)], tok_all.at[slot_of(far, sib)], (p.dp, sib)
    )
    own_vec = sems.copy(vecs, vec_all.at[p.z, p.x, inn])
    vec_in = [
        sems.remote(vecs, vec_all.at[p.z, p.x, inn], (p.dp, other)) for other in (sib, far, diag)
    ]
    mine = vec_all.at[p.z, p.x]
    vec_x = [sems.remote(mine, mine, device) for _, device, _ in p.peers("x")]
    column = vec_all.at[p.z]
    vec_z = [sems.remote(column, column, device) for _, device, _ in p.peers("z")]
    unit_base = sems.n
    sems.n += 3
    own_unit = sems.copy(w_units.at[0], w_units.at[0])

    def unit(r):
        u = 3 * inn + r
        target = u % N_IN
        spot = wq_all.at[u // N_IN, p.z, p.x]
        away = pltpu.make_async_remote_copy(
            src_ref=w_units.at[r],
            dst_ref=spot,
            send_sem=send.at[unit_base + r],
            recv_sem=recv.at[unit_base + u // N_IN],
            device_id=(p.dp, target),
            device_id_type=MESH,
        )
        stay = pltpu.make_async_copy(w_units.at[r], spot, local.at[sems.m - 1])
        return target == inn, stay, away

    def arrival(t):
        u = inn + N_IN * t
        spot = wq_all.at[t, p.z, p.x]
        bring = pltpu.make_async_remote_copy(
            src_ref=w_units.at[0],
            dst_ref=spot,
            send_sem=send.at[unit_base],
            recv_sem=recv.at[unit_base + t],
            device_id=(p.dp, far),
            device_id_type=MESH,
        )
        return u // 3 == inn, bring

    block = wq_all.at[:, p.z, p.x]
    wq_z = [sems.remote(block, block, device) for _, device, _ in p.peers("z")]
    line = wq_all.at[:, :, p.x]
    wq_x = [sems.remote(line, line, device) for _, device, _ in p.peers("x")]

    greet(p, "zxyc", diagonal=True)
    start(vec_in)
    own_vec.start()
    for r in range(3):
        stays, stay, away = unit(r)

        @pl.when(stays)
        def _():
            stay.start()

        @pl.when(jnp.logical_not(stays))
        def _():
            away.start()

    tok_far.start()
    tok_sib.start()
    own_tok.start()
    for t in range(3):
        stays, bring = arrival(t)

        @pl.when(jnp.logical_not(stays))
        def _():
            bring.wait_recv()

    unit(0)[1].wait()
    start(wq_z)
    own_vec.wait()
    wait_recv(vec_in)
    start(vec_x)
    wait_recv(vec_x)
    start(vec_z)
    wait_recv(wq_z)
    start(wq_x)
    wait_recv(vec_z)
    wait_recv(wq_x)
    tok_far.wait_recv()
    tok_on.start()
    tok_sib.wait_recv()
    tok_on.wait_recv()
    own_tok.wait()
    for r in range(3):
        stays, _, away = unit(r)

        @pl.when(jnp.logical_not(stays))
        def _():
            away.wait_send()

    wait_send([tok_far, tok_sib, tok_on] + vec_in + vec_x + vec_z + wq_z + wq_x)


def head(n_dp, tokens, w_units, vecs):
    n_x = n_dp // N_Z
    rows, width = tokens.shape
    _, w_rows, w_cols = w_units.shape
    n_remote = 3 + 3 + 3 + 2 * (n_x - 1) + 2 * (N_Z - 1)
    return pl.pallas_call(
        functools.partial(head_kernel, n_dp),
        out_shape=(
            jax.ShapeDtypeStruct((N_IN, rows, width), BF16),
            jax.ShapeDtypeStruct((3, N_Z, n_x, w_rows, w_cols), BF16),
            jax.ShapeDtypeStruct((N_Z, n_x, N_IN, 1, vecs.shape[-1]), F32),
        ),
        in_specs=[ANY] * 3,
        out_specs=(ANY,) * 3,
        scratch_shapes=sem_shapes(n_remote, 3),
        compiler_params=params(0),
        name="head",
    )(tokens, w_units, vecs)


BQ = 640
CK = 256


def segment_columns(place, lengths, rows, first):
    end_one = lengths[0, 0]
    end_two = end_one + lengths[0, 1]
    index = lax.broadcasted_iota(jnp.int32, (rows, HEAD_DIM), 0) + first
    lane = lax.broadcasted_iota(jnp.int32, (rows, HEAD_DIM), 1)
    item = jnp.where(index >= end_one, 1, 0) + jnp.where(index >= end_two, 1, 0)
    return item, lane


def forward_kernel(
    n_dp,
    tokens,
    lengths,
    w_qkv,
    norm_vecs,
    bias,
    w_out,
    w_up,
    w_down,
    h_one,
    q_out,
    v_out,
    kt_out,
    att_out,
    e_out,
    mixed,
    all_out,
    all_up,
    all_down,
    k_ref,
    vt_ref,
    s_ref,
    e_ref,
    low_ref,
    e_sem,
    send,
    recv,
    local,
):
    p = Place(n_dp)
    sems = Sems(send, recv, local)
    rows = tokens.shape[1]
    total = N_IN * rows
    half_down = w_down.shape[0] // 2
    half_up = w_up.shape[1] // 2

    def part(ref, first, size, axis):
        cut = pl.ds(first, size)
        lead = (slice(None),) * (len(ref.shape) - 2)
        return ref.at[lead + ((cut, slice(None)) if axis == 0 else (slice(None), cut))]

    pieces = []
    for which, (ref, out, size, axis) in enumerate(
        ((w_down, all_down, half_down, 0), (w_up, all_up, half_up, 1))
    ):
        for half in range(2):
            view = functools.partial(part, first=half * size, size=size, axis=axis)
            order = "zxyc" if (which, half) == (0, 0) else "zyxc"
            pieces.append(Gather(p, sems, view(ref), out, view, order))
    down0, down1, up0, up1 = pieces
    small = Gather(p, sems, w_out, all_out, lambda ref: ref, "xyzc")
    swap = []
    for s in range(N_IN - 1):
        device = (p.inn + 1 + s) % N_IN
        swap.append(sems.remote(low_ref.at[s], mixed.at[p.inn], (p.dp, device)))
    swap_own = sems.copy(low_ref.at[N_IN - 1], mixed.at[p.inn])

    greet(p, "zxyc", diagonal=True)
    small.step(0)
    up0.step(0)
    down0.step(0)
    up1.step(0)
    down1.step(0)

    gain, shift = norm_vecs[0:1], norm_vecs[1:2]
    for s in range(N_IN):
        value = tokens[s].astype(F32)
        mean = jnp.mean(value, axis=-1, keepdims=True)
        centred = value - mean
        spread = jnp.mean(centred * centred, axis=-1, keepdims=True)
        normed = centred * lax.rsqrt(spread + EPS)
        low = (normed * gain + shift).astype(BF16)
        here = pl.ds(s * rows, rows)
        h_one[here, :] = low
        first = (p.inn + 1 + s) % N_IN * rows
        item, lane = segment_columns(p, lengths, rows, first)
        same = jnp.where(lane == item, 1.0, 0.0).astype(BF16)
        other = jnp.where(jnp.logical_and(lane != item, lane < 3), NEG, 0.0).astype(BF16)
        ones = jnp.where(lane < 2, 1.0, 0.0).astype(BF16)
        q = (product(low, w_qkv[0]) + bias[0:1]).astype(BF16) * BF16(HEAD_DIM**-0.5)
        k = product(low, w_qkv[1]).astype(BF16)
        v = (product(low, w_qkv[2]) + bias[1:2]).astype(BF16)
        for h in range(HP):
            cols = slice(h * HEAD_DIM, (h + 1) * HEAD_DIM)
            q_out[h, here, :] = jnp.concatenate([q[:, cols], same], axis=1)
            k_ref[h, here, :] = jnp.concatenate([k[:, cols], other], axis=1)
            v_aug = jnp.concatenate([v[:, cols], ones], axis=1)
            v_out[h, here, :] = v_aug
            vt_ref[h, :, here] = v_aug.T
            kt_out[h, :, here] = k[:, cols].T

    items = N_IN * HP

    def spill(it, slot):
        h, qb = it % HP, it // HP
        return pltpu.make_async_copy(
            e_ref.at[slot],
            e_out.at[h, :, pl.ds(pl.multiple_of(qb * BQ, BQ), BQ)],
            e_sem.at[slot],
        )

    actions = {
        1: [lambda: small.step(1), lambda: up0.step(1), lambda: down0.step(1)],
        3: [lambda: small.step(2), lambda: up1.step(1), lambda: down1.step(1)],
        5: [lambda: up0.step(2), lambda: down0.step(2)],
        6: [lambda: small.step(3)],
        8: [lambda: up1.step(2), lambda: down1.step(2)],
        10: [lambda: up0.step(3), lambda: down0.step(3)],
    }

    def body(it, _):
        slot = it % 2
        h, qb = it % HP, it // HP
        here = pl.ds(pl.multiple_of(qb * BQ, BQ), BQ)

        @pl.when(it >= 2)
        def _():
            spill(it - 2, slot).wait()

        q = q_out[h, here, :]
        top = None
        for c in range(total // CK):
            cs = slice(c * CK, (c + 1) * CK)
            scores = product_nt(k_ref[h, cs, :], q)
            s_ref[cs, :] = scores
            peak = jnp.max(scores, axis=0, keepdims=True)
            top = peak if top is None else jnp.maximum(top, peak)
        acc = None
        for c in range(total // CK):
            cs = slice(c * CK, (c + 1) * CK)
            expo = jnp.exp(s_ref[cs, :] - top).astype(BF16)
            e_ref[slot, cs, :] = expo
            term = product(vt_ref[h, :, cs], expo)
            acc = term if acc is None else acc + term
        spill(it, slot).start()
        wide = acc.T
        sums = wide[:, HEAD_DIM : HEAD_DIM + 1]
        lane = lax.broadcasted_iota(jnp.int32, wide.shape, 1)
        att_out[h, here, :] = jnp.where(lane < HEAD_DIM, wide / sums, wide)

        @pl.when(h == HP - 1)
        def _():
            low_ref[qb] = jnp.concatenate(
                [att_out[i, here, 0:HEAD_DIM] for i in range(HP)], axis=1
            ).astype(BF16)

        for s in range(N_IN - 1):

            @pl.when(it == s * HP + HP - 1)
            def _():
                swap[s].start()

        for when, acts in actions.items():

            @pl.when(it == when)
            def _():
                for act in acts:
                    act()

        return 0

    lax.fori_loop(0, items, body, 0)
    swap_own.start()
    small.step(4)
    up0.step(4)
    down0.step(4)
    up1.step(3)
    down1.step(3)
    up1.step(4)
    down1.step(4)
    for copy in swap:
        copy.wait()
    swap_own.wait()
    for it in (items - 2, items - 1):
        spill(it, it % 2).wait()
    for piece in pieces + [small]:
        piece.finish()


def forward(n_dp, tokens, lengths, w_qkv, norm_vecs, bias, w_out, w_up, w_down):
    n_x = n_dp // N_Z
    rows = tokens.shape[1]
    total = N_IN * rows
    wide = jax.ShapeDtypeStruct((HP, total, LANES), BF16)

    def whole(block):
        return jax.ShapeDtypeStruct((N_IN, N_Z, n_x) + block.shape, BF16)

    n_big = (N_Z - 1) + max(1 + 2 * (n_x - 1), 1 + (n_x - 1)) + 2
    n_small = (n_x - 1) + 1 + 2 * (N_Z - 1) + 2
    return pl.pallas_call(
        functools.partial(forward_kernel, n_dp),
        out_shape=(
            jax.ShapeDtypeStruct((total, D), BF16),
            wide,
            wide,
            jax.ShapeDtypeStruct((HP, HEAD_DIM, total), BF16),
            jax.ShapeDtypeStruct((HP, total, LANES), F32),
            jax.ShapeDtypeStruct((HP, total, total), BF16),
            jax.ShapeDtypeStruct((N_IN, rows, CW), BF16),
            whole(w_out),
            whole(w_up),
            whole(w_down),
        ),
        in_specs=[VMEM, SMEM, VMEM, VMEM, VMEM, ANY, ANY, ANY],
        out_specs=(VMEM,) * 5 + (ANY,) * 5,
        scratch_shapes=[
            pltpu.VMEM((HP, total, LANES), BF16),
            pltpu.VMEM((HP, LANES, total), BF16),
            pltpu.VMEM((total, BQ), F32),
            pltpu.VMEM((2, total, BQ), BF16),
            pltpu.VMEM((N_IN, rows, CW), BF16),
            pltpu.SemaphoreType.DMA((2,)),
        ]
        + sem_shapes(4 * n_big + n_small + 3, 6),
        compiler_params=params(1),
        name="forward",
    )(tokens, lengths, w_qkv, norm_vecs, bias, w_out, w_up, w_down)


BK = 640
CQ = 1280


def backward_kernel(
    n_dp,
    d_att,
    att,
    e_all,
    q_ref,
    v_ref,
    kt_ref,
    g_out,
    g_up,
    g_down,
    d_qkv,
    s_out,
    s_up,
    s_down,
    seen,
    do_ref,
    dqt_ref,
    e_ref,
    *rest,
):
    buffers, (e_sem, send, recv, local) = rest[:25], rest[25:]
    p = Place(n_dp)
    sems = Sems(send, recv, local)
    rows = d_att.shape[1]
    total = N_IN * rows
    half_down = g_down.shape[3] // 2
    half_up = g_up.shape[4] // 2

    def part(ref, first, size, axis):
        cut = pl.ds(first, size)
        lead = (slice(None),) * (len(ref.shape) - 2)
        return ref.at[lead + ((cut, slice(None)) if axis == 0 else (slice(None), cut))]

    pieces = []
    number = 0
    for which, (ref, out, size, axis) in enumerate(
        ((g_down, s_down, half_down, 0), (g_up, s_up, half_up, 1))
    ):
        for half in range(2):
            view = functools.partial(part, first=half * size, size=size, axis=axis)
            order = ORDERS[number]
            pieces.append(
                Scatter(p, sems, ref, view, order, buffers[5 * number : 5 * number + 5], view(out))
            )
            number += 1
    down0, down1, up0, up1 = pieces
    small = Scatter(p, sems, g_out, lambda ref: ref, ORDERS[4], buffers[20:25], s_out)
    swap = []
    for s in range(N_IN - 1):
        device = (p.inn + 1 + s) % N_IN
        swap.append(sems.remote(d_att.at[device], seen.at[N_IN - 2 - s], (p.dp, device)))
    swap_own = sems.copy(d_att.at[p.inn], seen.at[N_IN - 1])

    items = (total // BK) * HP

    def fetch(it, slot):
        h, kb = it % HP, it // HP
        return pltpu.make_async_copy(
            e_all.at[h, pl.ds(pl.multiple_of(kb * BK, BK), BK), :], e_ref.at[slot], e_sem.at[slot]
        )

    fetch(0, 0).start()
    greet(p, "zxyc", diagonal=True)
    start(swap)
    swap_own.start()
    for piece in (up0, down0, small, up1, down1):
        piece.step(0)
    dqt_ref[...] = jnp.zeros_like(dqt_ref)
    swap_own.wait()
    wait_recv(swap)
    for s in range(N_IN):
        here = pl.ds(s * rows, rows)
        for h in range(HP):
            grad = seen[s, :, h * HEAD_DIM : (h + 1) * HEAD_DIM].astype(F32)
            both = att[h, here, :]
            scale = HEAD_DIM**-0.5 / both[:, HEAD_DIM : HEAD_DIM + 1]
            delta = jnp.sum(grad * both[:, 0:HEAD_DIM], axis=-1, keepdims=True) * -scale
            high = delta.astype(BF16)
            rest_low = (delta - high.astype(F32)).astype(BF16)
            lane = lax.broadcasted_iota(jnp.int32, (rows, HEAD_DIM), 1)
            tail = jnp.where(
                lane == 0, high.astype(F32), jnp.where(lane == 1, rest_low.astype(F32), 0.0)
            ).astype(BF16)
            do_ref[h, here, :] = jnp.concatenate([(grad * scale).astype(BF16), tail], axis=1)

    actions = {
        0: [lambda: up0.step(1), lambda: down0.step(1)],
        1: [lambda: small.step(1), lambda: up1.step(1), lambda: down1.step(1)],
        4: [lambda: up0.step(2), lambda: down0.step(2), lambda: small.step(2)],
        7: [lambda: up1.step(2), lambda: down1.step(2), lambda: small.step(3)],
        8: [lambda: up0.step(3), lambda: down0.step(3)],
        11: [lambda: up0.step(4), lambda: down0.step(4), lambda: small.step(4)],
    }

    def body(it, _):
        slot = it % 2

        @pl.when(it + 1 < items)
        def _():
            fetch(it + 1, 1 - slot).start()

        fetch(it, slot).wait()
        h, kb = it % HP, it // HP
        here = pl.ds(pl.multiple_of(kb * BK, BK), BK)
        va, kt = v_ref[h, here, :], kt_ref[h, :, here]
        dv = dk = None
        for c in range(total // CQ):
            cs = slice(c * CQ, (c + 1) * CQ)
            expo = e_ref[slot, :, cs]
            do = do_ref[h, cs, :]
            ds = (expo.astype(F32) * product_nt(va, do)).astype(BF16)
            dv_term, dk_term = product(expo, do), product(ds, q_ref[h, cs, :])
            dv = dv_term if dv is None else dv + dv_term
            dk = dk_term if dk is None else dk + dk_term
            dqt_ref[h, :, cs] += product(kt, ds)
        d_qkv[1, h, here, :] = dk[:, 0:HEAD_DIM].astype(BF16) * BF16(HEAD_DIM**0.5)
        d_qkv[2, h, here, :] = dv[:, 0:HEAD_DIM].astype(BF16) * BF16(HEAD_DIM**0.5)
        for when, acts in actions.items():

            @pl.when(it == when)
            def _():
                for act in acts:
                    act()

        return 0

    lax.fori_loop(0, items, body, 0)
    up1.step(3)
    down1.step(3)
    for h in range(HP):
        d_qkv[0, h, :, :] = dqt_ref[h].T.astype(BF16)
    up1.step(4)
    down1.step(4)
    wait_send(swap)
    for piece in pieces + [small]:
        piece.finish()


ORDERS = ("yxz", "xyz", "xyz", "xyz", "yxz")


def backward(n_dp, d_att, att, e_all, q, v, kt, g_out, g_up, g_down):
    n_x = n_dp // N_Z
    rows = d_att.shape[1]
    total = N_IN * rows

    def mine(grads):
        return jax.ShapeDtypeStruct(grads.shape[3:], F32)

    scratch = [
        pltpu.VMEM((N_IN, rows, CW), BF16),
        pltpu.VMEM((HP, total, LANES), BF16),
        pltpu.VMEM((HP, HEAD_DIM, total), F32),
        pltpu.VMEM((2, BK, total), BF16),
    ]
    r_down, c_down = g_down.shape[3:]
    r_up, c_up = g_up.shape[3:]
    sizes = [(r_down // 2, c_down)] * 2 + [(r_up, c_up // 2)] * 2 + [g_out.shape[3:]]
    n_remote = 3
    for (r, c), order in zip(sizes, ORDERS):
        scratch += scatter_buffers(n_x, r, c, order)
        n_remote += 2 + (2 if order[0] == "x" else 1) * (n_x - 1) + 1 + N_Z - 1
    return pl.pallas_call(
        functools.partial(backward_kernel, n_dp),
        out_shape=(
            jax.ShapeDtypeStruct((3, HP, total, HEAD_DIM), BF16),
            mine(g_out),
            mine(g_up),
            mine(g_down),
        ),
        in_specs=[ANY, VMEM, ANY, VMEM, VMEM, VMEM, ANY, ANY, ANY],
        out_specs=(VMEM,) * 4,
        scratch_shapes=scratch + [pltpu.SemaphoreType.DMA((2,))] + sem_shapes(n_remote, 11),
        compiler_params=params(2),
        name="backward",
    )(d_att, att, e_all, q, v, kt, g_out, g_up, g_down)


def tail_kernel(
    n_dp,
    dh,
    g_w,
    vecs,
    dh_sum,
    w_sum,
    vec_sum,
    t_own,
    t_core,
    t_far,
    w_own,
    w_x,
    w_z,
    w_mine,
    v_own,
    v_x,
    v_z,
    v_y,
    v_c,
    send,
    recv,
    local,
):
    p = Place(n_dp)
    n_x = n_dp // N_Z
    sems = Sems(send, recv, local)
    inn, sib, far = p.inn, p.y * 2 + 1 - p.c, (1 - p.y) * 2 + p.c
    diag = (1 - p.y) * 2 + 1 - p.c
    here, there = (p.dp, sib), (p.dp, far)
    keep = [
        sems.copy(dh.at[slot_of(inn, inn)], t_own.at[0]),
        sems.copy(dh.at[slot_of(far, inn)], t_own.at[1]),
    ]
    give = [
        sems.remote(dh.at[slot_of(sib, inn)], t_core.at[0], here),
        sems.remote(dh.at[slot_of(diag, inn)], t_core.at[1], here),
    ]
    across = sems.remote(t_own.at[1], t_far, there)
    w_load = sems.copy(g_w.at[:, :, p.x], w_own)
    w_to_x = [
        sems.remote(g_w.at[:, :, at], w_x.at[k - 1], device) for at, device, k in p.peers("x")
    ]
    w_to_z = [
        sems.remote(w_own.at[:, at], w_z.at[k - 1], device) for at, device, k in p.peers("z")
    ]
    v_load = sems.copy(vecs.at[:, p.x], v_own)
    v_to_x = [
        sems.remote(vecs.at[:, at], v_x.at[k - 1], device) for at, device, k in p.peers("x")
    ]
    v_to_z = [sems.remote(v_own.at[at], v_z.at[k - 1], device) for at, device, k in p.peers("z")]
    v_to_y = sems.remote(v_own.at[p.z, pl.ds((1 - p.y) * 2, 2)], v_y, there)
    v_to_c = sems.remote(v_own.at[p.z, sib], v_c, here)
    unit_base = sems.n

    def unit(t):
        u = inn + N_IN * t
        owner, r = u // 3, u % 3
        away = pltpu.make_async_remote_copy(
            src_ref=w_mine.at[t],
            dst_ref=w_sum.at[r],
            send_sem=send.at[unit_base + t],
            recv_sem=recv.at[unit_base + r],
            device_id=(p.dp, owner),
            device_id_type=MESH,
        )
        return owner == inn, r, away

    def arrival(r):
        u = 3 * inn + r
        bring = pltpu.make_async_remote_copy(
            src_ref=w_mine.at[0],
            dst_ref=w_sum.at[r],
            send_sem=send.at[unit_base],
            recv_sem=recv.at[unit_base + r],
            device_id=(p.dp, far),
            device_id_type=MESH,
        )
        return u % N_IN == inn, bring

    greet(p, "zxyc", diagonal=True)
    start(give)
    start(keep)
    start(w_to_x)
    start(v_to_x)
    w_load.start()
    v_load.start()
    for copy in keep:
        copy.wait()
    rows = t_own.shape[1]
    step = 128

    give[1].wait_recv()

    def add_far(i, _):
        at = pl.ds(pl.multiple_of(i * step, step), step)
        t_own[1, at, :] = t_own[1, at, :] + t_core[1, at, :]
        return 0

    lax.fori_loop(0, rows // step, add_far, 0)
    across.start()
    give[0].wait_recv()

    v_load.wait()
    wait_recv(v_to_x)
    for k in range(n_x - 1):
        v_own[...] = v_own[...] + v_x[k]
    start(v_to_z)
    w_load.wait()
    wait_recv(w_to_x)
    for k in range(n_x - 1):
        add_into(w_own, w_x.at[k], 2)
    start(w_to_z)
    wait_recv(v_to_z)
    for k in range(N_Z - 1):
        v_own[p.z] = v_own[p.z] + v_z[k]
    v_to_y.start()
    v_to_y.wait_recv()
    v_own[p.z, pl.ds(p.y * 2, 2)] = v_own[p.z, pl.ds(p.y * 2, 2)] + v_y[...]
    v_to_c.start()
    wait_recv(w_to_z)
    for t in range(3):
        value = w_own[t, p.z].astype(F32)
        for k in range(N_Z - 1):
            value = value + w_z[k, t].astype(F32)
        w_mine[t] = value
        stays, r, away = unit(t)

        @pl.when(jnp.logical_not(stays))
        def _():
            away.start()

        @pl.when(stays)
        def _():
            w_sum[r] = value

    v_to_c.wait_recv()
    vec_sum[...] = v_own[p.z, inn] + v_c[...]
    across.wait_recv()

    def add_near(i, _):
        at = pl.ds(pl.multiple_of(i * step, step), step)
        dh_sum[at, :] = (
            t_own[0, at, :].astype(F32) + t_core[0, at, :].astype(F32) + t_far[at, :].astype(F32)
        )
        return 0

    lax.fori_loop(0, rows // step, add_near, 0)
    for r in range(3):
        stays, bring = arrival(r)

        @pl.when(jnp.logical_not(stays))
        def _():
            bring.wait_recv()

    for t in range(3):
        stays, _, away = unit(t)

        @pl.when(jnp.logical_not(stays))
        def _():
            away.wait_send()

    wait_send(give + [across, v_to_y, v_to_c] + w_to_x + w_to_z + v_to_x + v_to_z)


def tail(n_dp, dh, g_w, vecs):
    n_x = n_dp // N_Z
    _, rows, width = dh.shape
    w_rows, w_cols = g_w.shape[3:]
    v_len = vecs.shape[-1]
    n_remote = 2 + 1 + 2 * (n_x - 1) + 2 * (N_Z - 1) + 2 + 3
    return pl.pallas_call(
        functools.partial(tail_kernel, n_dp),
        out_shape=(
            jax.ShapeDtypeStruct((rows, width), F32),
            jax.ShapeDtypeStruct((3, w_rows, w_cols), F32),
            jax.ShapeDtypeStruct((1, v_len), F32),
        ),
        in_specs=[ANY] * 3,
        out_specs=(VMEM,) * 3,
        scratch_shapes=[
            pltpu.VMEM((2, rows, width), BF16),
            pltpu.VMEM((2, rows, width), BF16),
            pltpu.VMEM((rows, width), BF16),
            pltpu.VMEM((3, N_Z, w_rows, w_cols), BF16),
            pltpu.VMEM((n_x - 1, 3, N_Z, w_rows, w_cols), BF16),
            pltpu.VMEM((N_Z - 1, 3, w_rows, w_cols), BF16),
            pltpu.VMEM((3, w_rows, w_cols), F32),
            pltpu.VMEM((N_Z, N_IN, 1, v_len), F32),
            pltpu.VMEM((n_x - 1, N_Z, N_IN, 1, v_len), F32),
            pltpu.VMEM((N_Z - 1, N_IN, 1, v_len), F32),
            pltpu.VMEM((2, 1, v_len), F32),
            pltpu.VMEM((1, v_len), F32),
        ]
        + sem_shapes(n_remote, 4),
        compiler_params=params(3),
        name="tail",
    )(dh, g_w, vecs)


def norm_parts(value):
    mean = jnp.mean(value, axis=-1, keepdims=True)
    centred = value - mean
    spread = jnp.mean(centred * centred, axis=-1, keepdims=True)
    factor = lax.rsqrt(spread + EPS)
    return centred * factor, factor


def norm_backward(grad, normed, factor, gain):
    scaled = grad * gain
    inner_mean = jnp.mean(scaled, axis=-1, keepdims=True)
    cross_mean = jnp.mean(scaled * normed, axis=-1, keepdims=True)
    return factor * (scaled - inner_mean - normed * cross_mean)


def gelu_slope(value):
    return (
        0.5 * (1.0 + lax.erf(value * 0.7071067811865476))
        + value * jnp.exp(-0.5 * value * value) * 0.3989422804014327
    )


def on_device(
    tokens,
    lengths,
    w_qkv,
    bias_qv,
    w_out,
    bias_out,
    w_up,
    bias_up,
    w_down,
    bias_down,
    gain_one,
    shift_one,
    gain_two,
    shift_two,
    cotangent,
):
    n_dp = lax.axis_size("dp")
    n_dev = n_dp * N_IN
    n_x = n_dp // N_Z
    rows = tokens.shape[0]
    inn = lax.axis_index("inner")
    w_rows = w_qkv.shape[0]
    vectors = (
        bias_qv,
        bias_out,
        bias_up,
        bias_down,
        gain_one,
        shift_one,
        gain_two,
        shift_two,
    )
    lens = [v.shape[0] for v in vectors]
    used = sum(lens)
    padded = -(-used // LANES) * LANES
    packed = jnp.concatenate([v.astype(F32) for v in vectors] + [jnp.zeros((padded - used,), F32)])
    units = w_qkv.reshape(w_rows, 3, CW).transpose(1, 0, 2)
    tok_all, wq_all, vec_all = head(n_dp, tokens, units, packed.reshape(1, padded))
    vec_all = vec_all.reshape(n_dev, padded)
    whole, at = [], 0
    for size in lens:
        whole.append(vec_all[:, at : at + size].reshape(-1))
        at += size
    f_bqv, f_bout, f_bup, f_bdown, f_g1, f_s1, f_g2, f_s2 = whole
    wq = wq_all.reshape(3, D, CW)
    norm_vecs = jnp.stack([f_g1, f_s1])
    bias = jnp.stack(
        [
            lax.dynamic_slice_in_dim(f_bqv, inn * CW, CW),
            lax.dynamic_slice_in_dim(f_bqv, D + inn * CW, CW),
        ]
    )
    h_one, q, v, kt, att, e_all, mixed, a_out, a_up, a_down = forward(
        n_dp, tok_all, lengths, wq, norm_vecs, bias, w_out, w_up, w_down
    )
    full_out = a_out.reshape(N_IN, D, -1).transpose(1, 0, 2).reshape(D, D)
    full_up = a_up.reshape(N_IN, D, -1).transpose(1, 0, 2).reshape(D, -1)
    full_down = a_down.reshape(N_IN, -1, D // N_IN).transpose(1, 0, 2).reshape(-1, D)

    inputs = tokens.astype(F32)
    attended = mixed.transpose(1, 0, 2).reshape(rows, D)
    residual = inputs + product(attended, full_out) + f_bout
    n_two, r_two = norm_parts(residual)
    h_two = (n_two * f_g2 + f_s2).astype(BF16)
    up = product(h_two, full_up) + f_bup
    act = jax.nn.gelu(up, approximate=False).astype(BF16)
    output = (residual + product(act, full_down) + f_bdown).astype(BF16)
    upstream = cotangent.astype(F32)
    grad_w_down = product_tn(act, cotangent)
    grad_bias_down = jnp.sum(upstream, axis=0)
    d_up = (product_nt(cotangent, full_down) * gelu_slope(up)).astype(BF16)
    grad_w_up = product_tn(h_two, d_up)
    grad_bias_up = jnp.sum(d_up.astype(F32), axis=0)
    dh_two = product_nt(d_up, full_up)
    grad_gain_two = jnp.sum(dh_two * n_two, axis=0)
    grad_shift_two = jnp.sum(dh_two, axis=0)
    d_res = upstream + norm_backward(dh_two, n_two, r_two, f_g2)
    d_mixed = d_res.astype(BF16)
    grad_w_out = product_tn(attended, d_mixed)
    grad_bias_out = jnp.sum(d_mixed.astype(F32), axis=0)
    d_att = product_nt(d_mixed, full_out).astype(BF16)

    def blocks(grad):
        low = grad.astype(BF16).reshape(grad.shape[0], N_IN, grad.shape[1] // N_IN)
        low = low.transpose(1, 0, 2)
        return low.reshape(N_IN, N_Z, n_x, low.shape[1] // n_dp, low.shape[2])

    d_qkv, s_out, s_up, s_down = backward(
        n_dp,
        d_att.reshape(rows, N_IN, CW).transpose(1, 0, 2),
        att,
        e_all,
        q,
        v,
        kt,
        blocks(grad_w_out),
        blocks(grad_w_up),
        blocks(grad_w_down),
    )
    d_all = d_qkv.transpose(0, 2, 1, 3).reshape(3, N_IN * rows, CW)
    sums = jnp.sum(d_all.astype(F32), axis=1)
    g_w = lax.dot_general(
        jnp.broadcast_to(h_one[None], (3,) + h_one.shape),
        d_all,
        (((1,), (1,)), ((0,), (0,))),
        preferred_element_type=F32,
    ).astype(BF16)
    dh = product_nt(d_all[0], wq[0]) + product_nt(d_all[1], wq[1]) + product_nt(d_all[2], wq[2])
    n_all, _ = norm_parts(tok_all.reshape(N_IN * rows, D).astype(F32))
    grad_gain_one = jnp.sum(dh * n_all, axis=0)
    grad_shift_one = jnp.sum(dh, axis=0)
    grad_bias_qv = jnp.zeros((2 * D,), F32)
    grad_bias_qv = lax.dynamic_update_slice_in_dim(grad_bias_qv, sums[0], inn * CW, 0)
    grad_bias_qv = lax.dynamic_update_slice_in_dim(grad_bias_qv, sums[2], D + inn * CW, 0)
    vec_grads = (
        grad_bias_qv,
        grad_bias_out,
        grad_bias_up,
        grad_bias_down,
        grad_gain_one,
        grad_shift_one,
        grad_gain_two,
        grad_shift_two,
    )
    packed = jnp.concatenate(
        [g.reshape(n_dev, -1) for g in vec_grads] + [jnp.zeros((n_dev, padded - used), F32)], axis=1
    )
    dh_sum, w_sum, vec_sum = tail(
        n_dp,
        dh.astype(BF16).reshape(N_IN, rows, D),
        g_w.reshape(3, N_Z, n_x, w_rows, CW),
        packed.reshape(N_Z, n_x, N_IN, 1, padded),
    )
    n_one, r_one = norm_parts(inputs)
    grad_tokens = (d_res + norm_backward(dh_sum, n_one, r_one, f_g1)).astype(BF16)
    grad_w_qkv = w_sum.transpose(1, 0, 2).reshape(w_rows, 3 * CW)
    vecs, at = [], 0
    for size in lens:
        vecs.append(vec_sum[0, at : at + size])
        at += size
    return (
        output,
        grad_tokens,
        grad_w_qkv,
        vecs[0],
        s_out,
        vecs[1],
        s_up,
        vecs[2],
        s_down,
        vecs[3],
        vecs[4],
        vecs[5],
        vecs[6],
        vecs[7],
    )


def solution(mesh):
    rows = P(("dp", "inner"), None)
    mat = P("dp", "inner")
    vec = P(("dp", "inner"))
    return jax.shard_map(
        on_device,
        mesh=mesh,
        in_specs=(
            rows,
            P("dp", None),
            mat,
            vec,
            mat,
            vec,
            mat,
            vec,
            mat,
            vec,
            vec,
            vec,
            vec,
            vec,
            rows,
        ),
        out_specs=(rows, rows, mat, vec, mat, vec, mat, vec, mat, vec, vec, vec, vec, vec),
        check_vma=False,
    )
```

```python
import functools

import jax
import jax.numpy as jnp
from jax import lax
from jax.experimental import pallas as pl
from jax.experimental.pallas import tpu as pltpu
from jax.sharding import PartitionSpec as P

D = 768
HEADS = 12
HEAD_DIM = 64
EPS = 1e-06
NEG = -1e30
LANES = 128
HC = 256
N_Z = 4
N_IN = 4
HP = HEADS // N_IN
CW = HP * HEAD_DIM
SCALE = HEAD_DIM**-0.5
MESH = pl.DeviceIdType.MESH
NT = (((1,), (1,)), ((), ()))
TN = (((0,), (0,)), ((), ()))
F32, BF16 = jnp.float32, jnp.bfloat16
ANY = pl.BlockSpec(memory_space=pl.ANY)
VMEM = pl.BlockSpec(memory_space=pltpu.VMEM)
SMEM = pl.BlockSpec(memory_space=pltpu.SMEM)
VMEM_LIMIT = 62 << 20
BIAS_QV, BIAS_OUT, BIAS_UP, BIAS_DOWN, GAIN_ONE, SHIFT_ONE, GAIN_TWO, SHIFT_TWO = range(8)


def product(left, right):
    return jnp.dot(left, right, preferred_element_type=F32)


def product_tn(left, right):
    return lax.dot_general(left, right, TN, preferred_element_type=F32)


def product_nt(left, right):
    return lax.dot_general(left, right, NT, preferred_element_type=F32)


class Place:
    def __init__(self, n_dp):
        self.n_x = n_dp // N_Z
        self.dp = lax.axis_index("dp")
        self.inn = lax.axis_index("inner")
        self.x, self.z = self.dp % self.n_x, self.dp // self.n_x
        self.c, self.y = self.inn % 2, self.inn // 2
        self.sib = self.y * 2 + 1 - self.c
        self.far = (1 - self.y) * 2 + self.c
        self.diag = (1 - self.y) * 2 + 1 - self.c

    def size(self, axis):
        return {"z": N_Z, "x": self.n_x, "y": 2, "c": 2}[axis]

    def peer(self, axis, k):
        if axis == "z":
            at = (self.z + k) % N_Z
            return at, (at * self.n_x + self.x, self.inn)
        if axis == "x":
            at = (self.x + k) % self.n_x
            return at, (self.z * self.n_x + at, self.inn)
        if axis == "y":
            return 1 - self.y, (self.dp, self.far)
        return 1 - self.c, (self.dp, self.sib)

    def peers(self, axis):
        return [self.peer(axis, k) + (k,) for k in range(1, self.size(axis))]


class Sems:
    def __init__(self, send, recv, local):
        self.send, self.recv, self.local = send, recv, local
        self.n = self.m = 0

    def remote(self, src, dst, device):
        i = self.n
        self.n += 1
        return pltpu.make_async_remote_copy(
            src_ref=src,
            dst_ref=dst,
            send_sem=self.send.at[i],
            recv_sem=self.recv.at[i],
            device_id=device,
            device_id_type=MESH,
        )

    def copy(self, src, dst):
        i = self.m
        self.m += 1
        return pltpu.make_async_copy(src, dst, self.local.at[i])


def sem_shapes(n_remote, n_local):
    return [
        pltpu.SemaphoreType.DMA((n_remote,)),
        pltpu.SemaphoreType.DMA((n_remote,)),
        pltpu.SemaphoreType.DMA((n_local,)),
    ]


def greet(place, axes, diagonal=False):
    devices = [device for axis in axes for _, device, _ in place.peers(axis)]
    if diagonal:
        devices.append((place.dp, place.diag))
    barrier = pltpu.get_barrier_semaphore()
    for device in devices:
        pl.semaphore_signal(barrier, inc=1, device_id=device, device_id_type=MESH)
    pl.semaphore_wait(barrier, len(devices))


def start(copies):
    for copy in copies:
        copy.start()


def wait_recv(copies):
    for copy in copies:
        copy.wait_recv()


def wait_send(copies):
    for copy in copies:
        copy.wait_send()


def wait(copies):
    for copy in copies:
        copy.wait()


def params(collective_id):
    return pltpu.CompilerParams(
        collective_id=collective_id, has_side_effects=True, vmem_limit_bytes=VMEM_LIMIT
    )


def part(ref, first, size, axis):
    cut = pl.ds(first, size)
    lead = (slice(None),) * (len(ref.shape) - 2)
    return ref.at[lead + ((cut, slice(None)) if axis == 0 else (slice(None), cut))]


def slot_of(device, receiver):
    return (device - receiver + N_IN - 1) % N_IN


def place_mask(n_dev, length, size, first):
    column = lax.broadcasted_iota(jnp.int32, (n_dev * 8, size), 1) + first
    row = lax.broadcasted_iota(jnp.int32, (n_dev * 8, size), 0)
    begin = (row // 8) * length
    owned = jnp.logical_and(column >= begin, column < begin + length)
    column = lax.broadcasted_iota(jnp.int32, (LANES, size), 1) + first
    lane = lax.broadcasted_iota(jnp.int32, (LANES, size), 0)
    return owned, jnp.where(column % length == lane, 1.0, 0.0).astype(BF16)


def spread(blocks, length, size, first=0):
    n_dev = blocks.shape[0] // 8
    owned, lanes = place_mask(n_dev, length, size, first)
    wide = jnp.where(owned, product(blocks.astype(BF16), lanes), 0.0)
    return jnp.sum(wide.reshape(n_dev, 8, size), axis=0)


def unspread(rows, n_dev, length, first=0):
    size = rows.shape[1]
    if size > HC and n_dev * size > 32 * D:
        cut = size // 3
        parts = [
            unspread(rows[:, at : at + cut], n_dev, length, first + at)
            for at in range(0, size, cut)
        ]
        return parts[0] + parts[1] + parts[2]
    owned, lanes = place_mask(n_dev, length, size, first)
    total = None
    for _ in range(3):
        low = rows.astype(BF16)
        rows = rows - low.astype(F32)
        many = jnp.broadcast_to(low.astype(F32)[None], (n_dev,) + low.shape)
        many = jnp.where(owned, many.reshape(n_dev * 8, low.shape[1]), 0.0).astype(BF16)
        term = product_nt(many, lanes)
        total = term if total is None else total + term
    return total


def norm_parts(value):
    mean = jnp.mean(value, axis=-1, keepdims=True)
    centred = value - mean
    spread_of = jnp.mean(centred * centred, axis=-1, keepdims=True)
    factor = lax.rsqrt(spread_of + EPS)
    return centred * factor, factor


def norm_backward(grad, normed, factor, gain):
    scaled = grad * gain
    inner_mean = jnp.mean(scaled, axis=-1, keepdims=True)
    cross_mean = jnp.mean(scaled * normed, axis=-1, keepdims=True)
    return factor * (scaled - inner_mean - normed * cross_mean)


class Gather:
    def __init__(self, place, sems, source, out, view, order):
        p = place

        def at(inn, z, x):
            return view(out.at[inn, z, x])

        everything = slice(None)
        zs, xs = p.z, p.x
        self.own = sems.copy(source, at(p.inn, zs, xs))
        inns = [p.inn]
        self.stages = []
        for number, axis in enumerate(order):
            copies = []
            for _, device, _ in p.peers(axis):
                for inn in inns:
                    target = at(inn, zs, xs)
                    copies.append(sems.remote(source if number == 0 else target, target, device))
            self.stages.append(copies)
            if axis == "z":
                zs = everything
            elif axis == "x":
                xs = everything
            elif axis == "y":
                inns = [p.inn, p.far]

    def step(self, number):
        if number == 0:
            self.own.start()
        else:
            if number == 1:
                self.own.wait()
            wait_recv(self.stages[number - 1])
        if number < len(self.stages):
            start(self.stages[number])

    def finish(self):
        for copies in self.stages:
            wait_send(copies)


def gather_count(n_x, order):
    count, inns = 0, 1
    for axis in order:
        count += inns * {"z": N_Z - 1, "x": n_x - 1, "y": 1, "c": 1}[axis]
        inns = 2 if axis == "y" else inns
    return count


BQ = 640
CK = 256
GATHER_ORDERS = {"down0": "xyzc", "down1": "zxyc", "up0": "zyxc", "up1": "zyxc", "out": "zyxc"}


def forward_kernel(
    n_dp,
    lens,
    tokens,
    lengths,
    w_qkv,
    *rest,
):
    vec_in, rest = rest[:8], rest[8:]
    (
        w_out,
        w_up,
        w_down,
        h_out,
        n_out,
        q_out,
        v_out,
        kt_out,
        att_out,
        e_out,
        mixed,
        all_out,
        all_up,
        all_down,
        vec_all,
        wq_full,
        tok,
        h_ref,
        n_ref,
        q_ref,
        v_ref,
        kt_ref,
        att_ref,
        k_ref,
        vt_ref,
        s_ref,
        e_ref,
        low_ref,
        units,
        wq_all,
        vec_own,
        e_sem,
        send,
        recv,
        local,
    ) = rest
    p = Place(n_dp)
    n_dev = n_dp * N_IN
    sems = Sems(send, recv, local)
    rows = tokens.shape[0]
    total = N_IN * rows
    half_down = w_down.shape[0] // 2
    half_up = w_up.shape[1] // 2

    def piece(name, ref, out, first, size, axis):
        view = functools.partial(part, first=first, size=size, axis=axis)
        return Gather(p, sems, view(ref), out, view, GATHER_ORDERS[name])

    down0 = piece("down0", w_down, all_down, 0, half_down, 0)
    down1 = piece("down1", w_down, all_down, half_down, half_down, 0)
    up0 = piece("up0", w_up, all_up, 0, half_up, 1)
    up1 = piece("up1", w_up, all_up, half_up, half_up, 1)
    small = Gather(p, sems, w_out, all_out, lambda ref: ref, GATHER_ORDERS["out"])
    pieces = [down0, down1, up0, up1, small]

    own_tok = sems.copy(tokens, tok.at[N_IN - 1])
    tok_far = sems.remote(tokens, tok.at[slot_of(p.inn, p.far)], (p.dp, p.far))
    tok_sib = sems.remote(tokens, tok.at[slot_of(p.inn, p.sib)], (p.dp, p.sib))
    tok_on = sems.remote(
        tok.at[slot_of(p.far, p.inn)], tok.at[slot_of(p.far, p.sib)], (p.dp, p.sib)
    )
    block = vec_all.at[p.z, p.x, p.inn]
    vec_i = [
        sems.remote(vec_own, block, (p.dp, other)) for other in (p.sib, p.far, p.diag)
    ]
    mine = vec_all.at[p.z, p.x]
    vec_x = [sems.remote(mine, mine, device) for _, device, _ in p.peers("x")]
    column = vec_all.at[p.z]
    vec_z = [sems.remote(column, column, device) for _, device, _ in p.peers("z")]
    unit_base = sems.n
    sems.n += 3

    def unit(r):
        u = 3 * p.inn + r
        away = pltpu.make_async_remote_copy(
            src_ref=units.at[r],
            dst_ref=wq_all.at[u // N_IN, p.z, p.x],
            send_sem=send.at[unit_base + r],
            recv_sem=recv.at[unit_base + u // N_IN],
            device_id=(p.dp, u % N_IN),
            device_id_type=MESH,
        )
        return u % N_IN == p.inn, u // N_IN, away

    def arrival(t):
        u = p.inn + N_IN * t
        bring = pltpu.make_async_remote_copy(
            src_ref=units.at[0],
            dst_ref=wq_all.at[t, p.z, p.x],
            send_sem=send.at[unit_base],
            recv_sem=recv.at[unit_base + t],
            device_id=(p.dp, p.far),
            device_id_type=MESH,
        )
        return u // 3 == p.inn, bring

    wq_block = wq_all.at[:, p.z, p.x]
    wq_z = [sems.remote(wq_block, wq_block, device) for _, device, _ in p.peers("z")]
    wq_line = wq_all.at[:, :, p.x]
    wq_x = [sems.remote(wq_line, wq_line, device) for _, device, _ in p.peers("x")]
    swap = []
    for s in range(N_IN - 1):
        device = (p.inn + 1 + s) % N_IN
        swap.append(sems.remote(low_ref.at[s], mixed.at[p.inn], (p.dp, device)))
    swap_own = sems.copy(low_ref.at[N_IN - 1], mixed.at[p.inn])
    saves = [
        sems.copy(ref, out)
        for ref, out in (
            (h_ref, h_out),
            (n_ref, n_out),
            (q_ref, q_out),
            (v_ref, v_out),
            (kt_ref, kt_out),
        )
    ]
    att_save = sems.copy(att_ref, att_out)

    own_tok.start()
    vec_own[...] = jnp.zeros_like(vec_own)
    for r, length in enumerate(lens):
        vec_own[r : r + 1, 0:length] = vec_in[r][...].astype(F32)
    for r in range(3):
        units[r] = w_qkv[:, r * CW : (r + 1) * CW]

    greet(p, "zxyc", diagonal=True)
    start(vec_i)
    for r in range(3):
        stays, t, away = unit(r)

        @pl.when(jnp.logical_not(stays))
        def _():
            away.start()

        @pl.when(stays)
        def _():
            wq_all[t, p.z, p.x] = units[r]

    tok_far.start()
    tok_sib.start()
    vec_all[p.z, p.x, p.inn] = vec_own[...]
    down0.step(0)
    wait_recv(vec_i)
    start(vec_x)
    for t in range(3):
        stays, bring = arrival(t)

        @pl.when(jnp.logical_not(stays))
        def _():
            bring.wait_recv()

    start(wq_z)
    small.step(0)
    wait_recv(vec_x)
    start(vec_z)
    down1.step(0)
    wait_recv(vec_z)

    blocks = vec_all[...].reshape(n_dev * 8, LANES)
    shared = spread(blocks, lens[GAIN_ONE], D)
    gain, shift = shared[GAIN_ONE : GAIN_ONE + 1], shared[SHIFT_ONE : SHIFT_ONE + 1]
    bias_q = spread(blocks, lens[BIAS_QV], CW, p.inn * CW)[BIAS_QV : BIAS_QV + 1]
    bias_v = spread(blocks, lens[BIAS_QV], CW, D + p.inn * CW)[BIAS_QV : BIAS_QV + 1]

    def norm(s):
        here = pl.ds(pl.multiple_of(s * rows, rows), rows)
        normed, _ = norm_parts(tok[s].astype(F32))
        h_ref[here, :] = (normed * gain + shift).astype(BF16)
        n_ref[here, :] = normed.astype(BF16)

    def heads(s):
        here = pl.ds(pl.multiple_of(s * rows, rows), rows)
        first = (p.inn + 1 + s) % N_IN * rows
        end_one = lengths[0, 0]
        end_two = end_one + lengths[0, 1]
        index = lax.broadcasted_iota(jnp.int32, (rows, HEAD_DIM), 0) + first
        lane = lax.broadcasted_iota(jnp.int32, (rows, HEAD_DIM), 1)
        item = jnp.where(index >= end_one, 1, 0) + jnp.where(index >= end_two, 1, 0)
        same = jnp.where(lane == item, 1.0, 0.0).astype(BF16)
        other = jnp.where(jnp.logical_and(lane != item, lane < 3), NEG, 0.0).astype(BF16)
        ones = jnp.where(lane < 2, 1.0, 0.0).astype(BF16)
        qkv = product(h_ref[here, :], wq_full[...])
        q = (qkv[:, 0:CW] + bias_q).astype(BF16) * BF16(SCALE)
        k = qkv[:, CW : 2 * CW].astype(BF16)
        v = (qkv[:, 2 * CW :] + bias_v).astype(BF16)
        for h in range(HP):
            cols = slice(h * HEAD_DIM, (h + 1) * HEAD_DIM)
            q_ref[h, here, :] = jnp.concatenate([q[:, cols], same], axis=1)
            k_aug = jnp.concatenate([k[:, cols], other], axis=1)
            k_ref[h, here, :] = k_aug
            v_aug = jnp.concatenate([v[:, cols], ones], axis=1)
            v_ref[h, here, :] = v_aug
            vt_ref[h, :, here] = v_aug.T
            kt_ref[h, :, here] = k_aug.T[0:HEAD_DIM]

    own_tok.wait()
    norm(N_IN - 1)
    wait_recv(wq_z)
    start(wq_x)
    up0.step(0)
    tok_sib.wait_recv()
    norm(slot_of(p.sib, p.inn))
    tok_far.wait_recv()
    tok_on.start()
    down0.step(1)
    small.step(1)
    norm(slot_of(p.far, p.inn))
    wait_recv(wq_x)
    for t in range(3):
        if w_qkv.shape[0] % 16 == 0:
            value = wq_all[t].reshape(D, CW)
        else:
            rows_of = [wq_all[t, z, x].astype(F32) for z in range(N_Z) for x in range(p.n_x)]
            value = jnp.concatenate(rows_of, axis=0).astype(BF16)
        wq_full[:, t * CW : (t + 1) * CW] = value
    down1.step(1)
    heads(N_IN - 1)
    tok_on.wait_recv()
    up0.step(1)
    up1.step(0)
    norm(slot_of(p.diag, p.inn))
    for s in range(N_IN - 1):
        heads(s)
    start(saves)

    items = N_IN * HP

    def spill(it, slot):
        h, qb = it % HP, it // HP
        return pltpu.make_async_copy(
            e_ref.at[slot],
            e_out.at[h, :, pl.ds(pl.multiple_of(qb * BQ, BQ), BQ)],
            e_sem.at[slot],
        )

    actions = {
        0: [(down0, 2), (small, 2)],
        1: [(up0, 2), (up1, 1)],
        2: [(down1, 2)],
        4: [(up1, 2), (small, 3)],
        6: [(up0, 3)],
        9: [(down1, 3), (small, 4)],
        10: [(up0, 4)],
    }

    def body(it, _):
        slot = it % 2
        h, qb = it % HP, it // HP
        here = pl.ds(pl.multiple_of(qb * BQ, BQ), BQ)

        @pl.when(it >= 2)
        def _():
            spill(it - 2, slot).wait()

        q = q_ref[h, here, :]
        top = None
        for c in range(total // CK):
            cs = slice(c * CK, (c + 1) * CK)
            scores = product_nt(k_ref[h, cs, :], q)
            s_ref[cs, :] = scores
            peak = jnp.max(scores, axis=0, keepdims=True)
            top = peak if top is None else jnp.maximum(top, peak)
        acc = None
        for c in range(total // CK):
            cs = slice(c * CK, (c + 1) * CK)
            expo = jnp.exp(s_ref[cs, :] - top).astype(BF16)
            e_ref[slot, cs, :] = expo
            term = product(vt_ref[h, :, cs], expo)
            acc = term if acc is None else acc + term
        spill(it, slot).start()
        wide = acc.T
        sums = wide[:, HEAD_DIM : HEAD_DIM + 1]
        lane = lax.broadcasted_iota(jnp.int32, wide.shape, 1)
        att_ref[h, here, :] = jnp.where(lane < HEAD_DIM, wide / sums, wide)

        @pl.when(h == HP - 1)
        def _():
            low_ref[qb] = jnp.concatenate(
                [att_ref[i, here, 0:HEAD_DIM] for i in range(HP)], axis=1
            ).astype(BF16)

        for s in range(N_IN - 1):

            @pl.when(it == s * HP + HP - 1)
            def _():
                swap[s].start()

        for when, acts in actions.items():

            @pl.when(it == when)
            def _():
                for which, number in acts:
                    which.step(number)

        return 0

    lax.fori_loop(0, items, body, 0)
    swap_own.start()
    att_save.start()
    down0.step(3)
    up1.step(3)
    down1.step(4)
    down0.step(4)
    up1.step(4)
    wait(swap)
    swap_own.wait()
    wait(saves)
    att_save.wait()
    for it in (items - 2, items - 1):
        spill(it, it % 2).wait()
    for item in pieces:
        item.finish()
    for r in range(3):
        stays, _, away = unit(r)

        @pl.when(jnp.logical_not(stays))
        def _():
            away.wait_send()

    wait_send([tok_far, tok_sib, tok_on] + vec_i + vec_x + vec_z + wq_z + wq_x)


def forward(n_dp, tokens, lengths, w_qkv, vectors, w_out, w_up, w_down):
    n_x = n_dp // N_Z
    rows = tokens.shape[0]
    total = N_IN * rows
    lens = tuple(v.shape[0] for v in vectors)
    w_rows = w_qkv.shape[0]
    wide = (HP, total, LANES)

    def whole(block):
        return jax.ShapeDtypeStruct((N_IN, N_Z, n_x) + block.shape, BF16)

    n_remote = 3 + 3 + 3 + 2 * (n_x - 1) + 2 * (N_Z - 1) + 3
    n_remote += sum(gather_count(n_x, order) for order in GATHER_ORDERS.values())
    return pl.pallas_call(
        functools.partial(forward_kernel, n_dp, lens),
        out_shape=(
            jax.ShapeDtypeStruct((total, D), BF16),
            jax.ShapeDtypeStruct((total, D), BF16),
            jax.ShapeDtypeStruct(wide, BF16),
            jax.ShapeDtypeStruct(wide, BF16),
            jax.ShapeDtypeStruct((HP, HEAD_DIM, total), BF16),
            jax.ShapeDtypeStruct(wide, F32),
            jax.ShapeDtypeStruct((HP, total, total), BF16),
            jax.ShapeDtypeStruct((N_IN, rows, CW), BF16),
            whole(w_out),
            whole(w_up),
            whole(w_down),
            jax.ShapeDtypeStruct((N_Z, n_x, N_IN, 8, LANES), F32),
            jax.ShapeDtypeStruct((D, 3 * CW), BF16),
        ),
        in_specs=[ANY, SMEM, VMEM] + [VMEM] * 8 + [ANY] * 3,
        out_specs=(ANY,) * 11 + (VMEM,) * 2,
        scratch_shapes=[
            pltpu.VMEM((N_IN, rows, D), BF16),
            pltpu.VMEM((total, D), BF16),
            pltpu.VMEM((total, D), BF16),
            pltpu.VMEM(wide, BF16),
            pltpu.VMEM(wide, BF16),
            pltpu.VMEM((HP, HEAD_DIM, total), BF16),
            pltpu.VMEM(wide, F32),
            pltpu.VMEM(wide, BF16),
            pltpu.VMEM((HP, LANES, total), BF16),
            pltpu.VMEM((total, BQ), F32),
            pltpu.VMEM((2, total, BQ), BF16),
            pltpu.VMEM((N_IN, rows, CW), BF16),
            pltpu.VMEM((3, w_rows, CW), BF16),
            pltpu.VMEM((3, N_Z, n_x, w_rows, CW), BF16),
            pltpu.VMEM((8, LANES), F32),
            pltpu.SemaphoreType.DMA((2,)),
        ]
        + sem_shapes(n_remote, 13),
        compiler_params=params(0),
        name="forward",
    )(tokens, lengths, w_qkv, *[v.reshape(1, -1) for v in vectors], w_out, w_up, w_down)


def add_rows(total, terms, out=None):
    step = 128

    def one(i, _):
        at = pl.ds(pl.multiple_of(i * step, step), step)
        if out is None:
            value = total[at, :]
            for term in terms:
                value = value + term[at, :]
            total[at, :] = value
        else:
            value = total[at, :].astype(F32)
            for term in terms:
                value = value + term[at, :].astype(F32)
            out[at, :] = value
        return 0

    lax.fori_loop(0, total.shape[0] // step, one, 0)


def middle_kernel(
    n_dp,
    lens,
    tokens,
    mixed,
    a_out,
    a_up,
    a_down,
    vec_all,
    cotangent,
    output,
    d_res_out,
    seen,
    t_out,
    t_up,
    t_down,
    sums,
    sum_up,
    tok,
    mix,
    po,
    pu,
    pd,
    cot,
    fo,
    fd,
    att,
    res,
    n_two,
    h_two,
    act,
    d_up,
    b_up,
    d_mixed,
    d_res,
    out_ref,
    d_att,
    co,
    cu,
    cd,
    send,
    recv,
    local,
):
    p = Place(n_dp)
    n_dev = n_dp * N_IN
    sems = Sems(send, recv, local)
    rows = tokens.shape[0]
    ff = a_down.shape[1]
    loads = {
        name: sems.copy(src, dst)
        for name, src, dst in (
            ("out", a_out, po),
            ("mix", mixed, mix),
            ("tok", tokens, tok),
            ("up", a_up, pu),
            ("cot", cotangent, cot),
            ("down", a_down, pd),
        )
    }
    for load in loads.values():
        load.start()
    swap = []
    for s in range(N_IN - 1):
        device = (p.inn + 1 + s) % N_IN
        swap.append(sems.remote(d_att.at[device], seen.at[N_IN - 2 - s], (p.dp, device)))
    swap_own = sems.copy(d_att.at[p.inn], seen.at[N_IN - 1])

    def across(parts, buffer):
        return [
            sems.remote(parts.at[2 * yy + 1 - p.c], buffer.at[yy], (p.dp, p.sib))
            for yy in range(2)
        ]

    core_up, core_down, core_out = across(pu, cu), across(pd, cd), across(po, co)
    keeps = {
        name: [sems.copy(parts.at[2 * yy + p.c], out.at[yy]) for yy in range(2)]
        for name, parts, out in (("up", pu, t_up), ("down", pd, t_down), ("out", po, t_out))
    }
    out_save = sems.copy(out_ref, output)
    res_save = sems.copy(d_res, d_res_out)

    greet(p, "yc", diagonal=True)
    blocks = vec_all[...].reshape(n_dev * 8, LANES)
    shared = spread(blocks, lens[BIAS_OUT], D)
    for c in range(ff // D):
        b_up[:, c * D : (c + 1) * D] = spread(blocks, lens[BIAS_UP], D, c * D)[
            BIAS_UP : BIAS_UP + 1
        ]

    loads["out"].wait()
    loads["mix"].wait()
    for i in range(N_IN):
        cols = slice(i * CW, (i + 1) * CW)
        fo[:, cols] = po[i]
        att[:, cols] = mix[i]
    loads["tok"].wait()
    residual = (
        tok[...].astype(F32) + product(att[...], fo[...]) + shared[BIAS_OUT : BIAS_OUT + 1]
    )
    res[...] = residual
    normed, factor = norm_parts(residual)
    n_two[...] = normed
    gain = shared[GAIN_TWO : GAIN_TWO + 1]
    h_two[...] = (normed * gain + shared[SHIFT_TWO : SHIFT_TWO + 1]).astype(BF16)
    loads["down"].wait()
    for i in range(N_IN):
        fd[:, i * CW : (i + 1) * CW] = pd[i]
    loads["up"].wait()
    loads["cot"].wait()

    def hidden(it, _):
        hid = pl.ds(pl.multiple_of(it * HC, HC), HC)
        inside = pl.ds(pl.multiple_of(it % (D // HC) * HC, HC), HC)
        up = product(h_two[...], pu[it // (D // HC), :, inside]) + b_up[:, hid]
        d_act = product_nt(cot[...], fd[hid, :])
        cdf = 0.5 * (1.0 + lax.erf(up * 0.7071067811865476))
        pdf = jnp.exp(-0.5 * up * up) * 0.3989422804014327
        act[:, hid] = (up * cdf).astype(BF16)
        grad = (d_act * (cdf + up * pdf)).astype(BF16)
        d_up[:, hid] = grad
        sum_up[:, hid] = jnp.sum(grad.astype(F32), axis=0, keepdims=True)
        return 0

    lax.fori_loop(0, ff // HC, hidden, 0)

    dh_two = None
    for i in range(N_IN):
        term = product_nt(d_up[:, i * D : (i + 1) * D], pu[i])
        dh_two = term if dh_two is None else dh_two + term
    normed = n_two[...]
    upstream = cot[...].astype(F32)
    value = upstream + norm_backward(dh_two, normed, factor, gain)
    d_res[...] = value
    res_save.start()
    low = value.astype(BF16)
    d_mixed[...] = low
    grad_att = product_nt(low, fo[...]).astype(BF16)
    for i in range(N_IN):
        d_att[i] = grad_att[:, i * CW : (i + 1) * CW]
    start(swap)
    swap_own.start()

    sums[...] = jnp.zeros_like(sums)
    sums[BIAS_OUT : BIAS_OUT + 1, :] = jnp.sum(low.astype(F32), axis=0, keepdims=True)
    sums[BIAS_DOWN : BIAS_DOWN + 1, :] = jnp.sum(upstream, axis=0, keepdims=True)
    sums[GAIN_TWO : GAIN_TWO + 1, :] = jnp.sum(dh_two * normed, axis=0, keepdims=True)
    sums[SHIFT_TWO : SHIFT_TWO + 1, :] = jnp.sum(dh_two, axis=0, keepdims=True)

    def output_part(n, _):
        cols = pl.ds(pl.multiple_of(n * HC, HC), HC)
        value = product(act[...], fd[:, cols]) + res[:, cols]
        out_ref[:, cols] = value.astype(BF16)
        return 0

    res[...] = res[...] + shared[BIAS_DOWN : BIAS_DOWN + 1]
    lax.fori_loop(0, D // HC, output_part, 0)
    out_save.start()

    def grad_up(i):
        cols = pl.ds(pl.multiple_of(i * D, D), D)
        pu[i] = product_tn(h_two[...], d_up[:, cols]).astype(BF16)

    for yy in range(2):
        grad_up(2 * yy + 1 - p.c)
    start(core_up)

    def grad_down(it, _):
        hid = pl.ds(pl.multiple_of(it * HC, HC), HC)
        value = product_tn(act[:, hid], cot[...]).astype(BF16)
        for i in range(N_IN):
            pd[i, hid, :] = value[:, i * CW : (i + 1) * CW]
        return 0

    lax.fori_loop(0, ff // HC, grad_down, 0)
    start(core_down)
    value = product_tn(att[...], d_mixed[...]).astype(BF16)
    for i in range(N_IN):
        po[i] = value[:, i * CW : (i + 1) * CW]
    start(core_out)
    for yy in range(2):
        grad_up(2 * yy + p.c)
    for copies, parts, buffer, name in (
        (core_up, pu, cu, "up"),
        (core_down, pd, cd, "down"),
        (core_out, po, co, "out"),
    ):
        wait_recv(copies)
        for yy in range(2):
            add_rows(parts.at[2 * yy + p.c], [buffer.at[yy]])
        start(keeps[name])
    wait(swap)
    swap_own.wait()
    for copies in (core_up, core_down, core_out):
        wait_send(copies)
    for copies in keeps.values():
        wait(copies)
    out_save.wait()
    res_save.wait()


def middle(n_dp, lens, tokens, mixed, a_out, a_up, a_down, vec_all, cotangent):
    rows = tokens.shape[0]
    ff = a_down.shape[1]
    out_parts, up_parts, down_parts = (D, CW), (D, D), (ff, CW)
    return pl.pallas_call(
        functools.partial(middle_kernel, n_dp, lens),
        out_shape=(
            jax.ShapeDtypeStruct((rows, D), BF16),
            jax.ShapeDtypeStruct((rows, D), F32),
            jax.ShapeDtypeStruct((N_IN, rows, CW), BF16),
            jax.ShapeDtypeStruct((2,) + out_parts, BF16),
            jax.ShapeDtypeStruct((2,) + up_parts, BF16),
            jax.ShapeDtypeStruct((2,) + down_parts, BF16),
            jax.ShapeDtypeStruct((8, D), F32),
            jax.ShapeDtypeStruct((1, ff), F32),
        ),
        in_specs=[ANY] * 5 + [VMEM, ANY],
        out_specs=(ANY,) * 6 + (VMEM,) * 2,
        scratch_shapes=[
            pltpu.VMEM((rows, D), BF16),
            pltpu.VMEM((N_IN, rows, CW), BF16),
            pltpu.VMEM((N_IN,) + out_parts, BF16),
            pltpu.VMEM((N_IN,) + up_parts, BF16),
            pltpu.VMEM((N_IN,) + down_parts, BF16),
            pltpu.VMEM((rows, D), BF16),
            pltpu.VMEM((D, D), BF16),
            pltpu.VMEM((ff, D), BF16),
            pltpu.VMEM((rows, D), BF16),
            pltpu.VMEM((rows, D), F32),
            pltpu.VMEM((rows, D), F32),
            pltpu.VMEM((rows, D), BF16),
            pltpu.VMEM((rows, ff), BF16),
            pltpu.VMEM((rows, ff), BF16),
            pltpu.VMEM((1, ff), F32),
            pltpu.VMEM((rows, D), BF16),
            pltpu.VMEM((rows, D), F32),
            pltpu.VMEM((rows, D), BF16),
            pltpu.VMEM((N_IN, rows, CW), BF16),
            pltpu.VMEM((2,) + out_parts, BF16),
            pltpu.VMEM((2,) + up_parts, BF16),
            pltpu.VMEM((2,) + down_parts, BF16),
        ]
        + sem_shapes(9, 15),
        compiler_params=params(1),
        name="middle",
    )(tokens, mixed, a_out, a_up, a_down, vec_all, cotangent)


BK = 640
CQ = 1280
SCATTER_ORDERS = ("yxz", "xyz", "yxz", "xyz", "zyx")


class Scatter:
    def __init__(self, place, sems, blocks, order, buffers, out):
        self.order, self.out = order, out
        p = place
        self.total, self.buffers = buffers[0], dict(zip(order, buffers[1:]))
        self.load = sems.copy(blocks, self.total)
        _, _, n_x, _, _ = self.total.shape
        where = {"y": pl.ds(0, 2), "z": pl.ds(0, N_Z), "x": pl.ds(0, n_x)}
        own = {"y": p.y, "z": p.z, "x": p.x}
        self.copies, self.regions = {}, {}
        for axis in order:
            copies = []
            for at, device, k in p.peers(axis):
                there = dict(where)
                there[axis] = pl.ds(at, 1)
                src = self.total.at[there["y"], there["z"], there["x"]]
                copies.append(sems.remote(src, self.buffers[axis].at[k - 1], device))
            self.copies[axis] = copies
            where[axis] = pl.ds(own[axis], 1)
            self.regions[axis] = (where["y"], where["z"], where["x"])

    def step(self, number):
        if number == 0:
            self.load.start()
            return
        if number == 1:
            self.load.wait()
        else:
            axis = self.order[number - 2]
            wait_recv(self.copies[axis])
            region, buffer = self.total.at[self.regions[axis]], self.buffers[axis]
            if number - 1 == len(self.order):
                value = region[0, 0, 0].astype(F32)
                for k in range(buffer.shape[0]):
                    value = value + buffer[k, 0, 0, 0].astype(F32)
                self.out[...] = value
                return
            _, n_y, n_z, n_x, _, _ = buffer.shape

            def one(i, _):
                for y in range(n_y):
                    for x in range(n_x):
                        value = region[y, i, x]
                        for k in range(buffer.shape[0]):
                            value = value + buffer[k, y, i, x]
                        region[y, i, x] = value
                return 0

            lax.fori_loop(0, n_z, one, 0)
        start(self.copies[self.order[number - 1]])

    def finish(self):
        for axis in self.order:
            wait_send(self.copies[axis])


def scatter_buffers(n_x, rows, cols, order):
    sizes = {"y": 2, "z": N_Z, "x": n_x}
    shapes = [(2, N_Z, n_x, rows, cols)]
    left = dict(sizes)
    for axis in order:
        left[axis] = 1
        shapes.append((sizes[axis] - 1, left["y"], left["z"], left["x"], rows, cols))
    return [pltpu.VMEM(shape, BF16) for shape in shapes]


def scatter_count(n_x):
    return 1 + (N_Z - 1) + (n_x - 1)


def backward_kernel(n_dp, lens, *rest):
    (
        tokens,
        seen_in,
        att_in,
        e_all,
        q_in,
        v_in,
        kt_in,
        h_in,
        n_in,
        wq_in,
        d_res_in,
        t_out,
        t_up,
        t_down,
        vec_all,
        sums,
        sum_up,
    ) = rest[:17]
    grad_tokens, g_qkv, s_out, s_up, s_down = rest[17:22]
    vec_outs = rest[22:30]
    (
        seen,
        att,
        q_ref,
        v_ref,
        kt_ref,
        h_ref,
        n_ref,
        wq_ref,
        d_res,
        do_ref,
        dqt_ref,
        e_ref,
        d_all,
        t_core,
        t_far,
        w_own,
        w_x,
        w_z,
        w_mine,
        w_sum,
        v_own,
        v_x,
        v_z,
        v_y,
        v_c,
    ) = rest[30:55]
    buffers = rest[55:75]
    e_sem, send, recv, local = rest[75:]
    p = Place(n_dp)
    n_dev, n_x = n_dp * N_IN, n_dp // N_Z
    sems = Sems(send, recv, local)
    rows = tokens.shape[0]
    total = N_IN * rows
    half_down = t_down.shape[3] // 2
    half_up = t_up.shape[4] // 2

    loads = {
        name: sems.copy(src, dst)
        for name, src, dst in (
            ("seen", seen_in, seen),
            ("att", att_in, att),
            ("v", v_in, v_ref),
            ("kt", kt_in, kt_ref),
            ("q", q_in, q_ref),
            ("wq", wq_in, wq_ref),
            ("res", d_res_in, d_res),
        )
    }
    for name in ("seen", "att"):
        loads[name].start()
    pieces = []
    for number, (ref, out, first, size, axis) in enumerate(
        (
            (t_down, s_down, 0, half_down, 0),
            (t_down, s_down, half_down, half_down, 0),
            (t_up, s_up, 0, half_up, 1),
            (t_up, s_up, half_up, half_up, 1),
            (t_out, s_out, 0, t_out.shape[3], 0),
        )
    ):
        pieces.append(
            Scatter(
                p,
                sems,
                part(ref, first, size, axis),
                SCATTER_ORDERS[number],
                buffers[4 * number : 4 * number + 4],
                part(out, first, size, axis),
            )
        )
    down0, down1, up0, up1, small = pieces
    for item in (down0, down1, small, up0, up1):
        item.step(0)
    for name in ("v", "kt", "q", "wq", "res"):
        loads[name].start()

    def room(i):
        return e_ref.at[i // 3, :, pl.ds(i % 3 * D, D)]

    dh_far, dh_own, dh_diag, dh_sib, tok = (room(i) for i in range(5))
    loads["tok"] = sems.copy(tokens, tok)

    def fetch(it, slot):
        h, kb = it % HP, it // HP
        return pltpu.make_async_copy(
            e_all.at[h, pl.ds(pl.multiple_of(kb * BK, BK), BK), :], e_ref.at[slot], e_sem.at[slot]
        )

    fetch(0, 0).start()
    slots = [slot_of(device, p.inn) for device in (p.diag, p.far, p.sib, p.inn)]
    feeds = []
    for i, s in enumerate(slots):
        at = pl.ds(pl.multiple_of(s * rows, rows), rows)
        feeds.append(
            [sems.copy(n_in.at[at], n_ref.at[i % 2]), sems.copy(h_in.at[at], h_ref.at[i % 2])]
        )
    for feed in feeds[0:2]:
        start(feed)
    here, there = (p.dp, p.sib), (p.dp, p.far)
    give_diag = sems.remote(dh_diag, t_core.at[1], here)
    give_sib = sems.remote(dh_sib, t_core.at[0], here)
    across = sems.remote(dh_far, t_far, there)
    w_to_x = [
        sems.remote(w_own.at[:, :, at], w_x.at[k - 1], device) for at, device, k in p.peers("x")
    ]
    w_to_z = [
        sems.remote(w_own.at[:, at, p.x], w_z.at[k - 1], device) for at, device, k in p.peers("z")
    ]
    v_to_x = [
        sems.remote(v_own.at[:, at], v_x.at[k - 1], device) for at, device, k in p.peers("x")
    ]
    v_to_z = [
        sems.remote(v_own.at[at, p.x], v_z.at[k - 1], device) for at, device, k in p.peers("z")
    ]
    v_to_y = sems.remote(v_own.at[p.z, p.x, pl.ds((1 - p.y) * 2, 2)], v_y, there)
    v_to_c = sems.remote(v_own.at[p.z, p.x, p.sib], v_c, here)
    unit_base = sems.n

    def unit(t):
        u = p.inn + N_IN * t
        owner, r = u // 3, u % 3
        away = pltpu.make_async_remote_copy(
            src_ref=w_mine.at[t],
            dst_ref=w_sum.at[r],
            send_sem=send.at[unit_base + t],
            recv_sem=recv.at[unit_base + r],
            device_id=(p.dp, owner),
            device_id_type=MESH,
        )
        return owner == p.inn, r, away

    def arrival(r):
        u = 3 * p.inn + r
        bring = pltpu.make_async_remote_copy(
            src_ref=w_mine.at[0],
            dst_ref=w_sum.at[r],
            send_sem=send.at[unit_base],
            recv_sem=recv.at[unit_base + r],
            device_id=(p.dp, p.far),
            device_id_type=MESH,
        )
        return u % N_IN == p.inn, bring

    greet(p, "zxyc", diagonal=True)
    for item in (down0, down1, small):
        item.step(1)
    dqt_ref[...] = jnp.zeros_like(dqt_ref)
    loads["seen"].wait()
    loads["att"].wait()
    for s in range(N_IN):
        at = pl.ds(s * rows, rows)
        for h in range(HP):
            grad = seen[s, :, h * HEAD_DIM : (h + 1) * HEAD_DIM].astype(F32)
            both = att[h, at, :]
            scale = SCALE / both[:, HEAD_DIM : HEAD_DIM + 1]
            delta = jnp.sum(grad * both[:, 0:HEAD_DIM], axis=-1, keepdims=True) * -scale
            high = delta.astype(BF16).astype(F32)
            lane = lax.broadcasted_iota(jnp.int32, (rows, HEAD_DIM), 1)
            tail = jnp.where(lane == 0, high, jnp.where(lane == 1, delta - high, 0.0))
            do_ref[h, at, :] = jnp.concatenate([grad * scale, tail], axis=1).astype(BF16)
    for name in ("v", "kt", "q"):
        loads[name].wait()

    actions = {
        2: [(down0, 2), (up0, 1), (down1, 2), (up1, 1), (small, 2)],
        5: [(down0, 3), (down1, 3), (small, 3)],
        6: [(small, 4)],
        7: [(up0, 2), (up1, 2)],
        9: [(down0, 4), (down1, 4), (up0, 3), (up1, 3)],
    }
    items = (total // BK) * HP

    def body(kb, _):
        at = pl.ds(pl.multiple_of(kb * BK, BK), BK)
        for h in range(HP):
            it = kb * HP + h
            slot = it % 2

            @pl.when(it + 1 < items)
            def _():
                fetch(it + 1, 1 - slot).start()

            fetch(it, slot).wait()
            va, kt = v_ref[h, at, :], kt_ref[h, :, at]
            dv = dk = None
            for c in range(total // CQ):
                cs = slice(c * CQ, (c + 1) * CQ)
                expo = e_ref[slot, :, cs]
                do = do_ref[h, cs, :]
                ds = (expo.astype(F32) * product_nt(va, do)).astype(BF16)
                dv_term, dk_term = product(expo, do), product(ds, q_ref[h, cs, :])
                dv = dv_term if dv is None else dv + dv_term
                dk = dk_term if dk is None else dk + dk_term
                dqt_ref[h, :, cs] += product(kt, ds)
            cols = slice(h * HEAD_DIM, (h + 1) * HEAD_DIM)
            root = HEAD_DIM**0.5
            d_all[1, at, cols] = (dk[:, 0:HEAD_DIM] * root).astype(BF16)
            d_all[2, at, cols] = (dv[:, 0:HEAD_DIM] * root).astype(BF16)
            for when, acts in actions.items():
                if when % HP != h:
                    continue

                @pl.when(kb == when // HP)
                def _():
                    for which, number in acts:
                        which.step(number)

        return 0

    lax.fori_loop(0, total // BK, body, 0)
    loads["tok"].start()
    for h in range(HP):
        d_all[0, :, h * HEAD_DIM : (h + 1) * HEAD_DIM] = dqt_ref[h].T.astype(BF16)
    loads["wq"].wait()

    def input_grad(i):
        at = pl.ds(pl.multiple_of(slots[i] * rows, rows), rows)
        feeds[i][0].wait()
        value = None
        for t in range(3):
            term = product_nt(d_all[t, at, :], wq_ref[:, t * CW : (t + 1) * CW])
            value = term if value is None else value + term
        gain_sum = jnp.sum(value * n_ref[i % 2].astype(F32), axis=0, keepdims=True)
        shift_sum = jnp.sum(value, axis=0, keepdims=True)
        return value.astype(BF16), gain_sum, shift_sum

    def weight_grad(i):
        at = pl.ds(pl.multiple_of(slots[i] * rows, rows), rows)
        feeds[i][1].wait()
        terms = [product_tn(h_ref[i % 2], d_all[t, at, :]) for t in range(3)]
        if i + 2 < len(feeds):
            start(feeds[i + 2])
        return terms

    value, gain_sum, shift_sum = input_grad(0)
    dh_diag[...] = value
    give_diag.start()
    value, g_sum, s_sum = input_grad(1)
    dh_far[...] = value
    gain_sum, shift_sum = gain_sum + g_sum, shift_sum + s_sum
    give_diag.wait_recv()
    add_rows(dh_far, [t_core.at[1]])
    across.start()
    g_w = weight_grad(0)
    g_w = [a + b for a, b in zip(g_w, weight_grad(1))]
    value, g_sum, s_sum = input_grad(2)
    dh_sib[...] = value
    give_sib.start()
    gain_sum, shift_sum = gain_sum + g_sum, shift_sum + s_sum
    g_w = [a + b for a, b in zip(g_w, weight_grad(2))]
    value, g_sum, s_sum = input_grad(3)
    dh_own[...] = value
    gain_sum, shift_sum = gain_sum + g_sum, shift_sum + s_sum
    g_w = [a + b for a, b in zip(g_w, weight_grad(3))]
    w_rows = D // n_dp
    for t in range(3):
        if w_rows % 16 == 0:
            w_own[t] = g_w[t].astype(BF16).reshape(N_Z, n_x, w_rows, CW)
        else:
            w_own[t] = g_w[t].reshape(N_Z, n_x, w_rows, CW).astype(BF16)
    start(w_to_x)

    row = lax.broadcasted_iota(jnp.int32, (8, D), 0)
    wide = sums[...]
    wide = wide + jnp.where(row == GAIN_ONE, gain_sum, 0.0)
    wide = wide + jnp.where(row == SHIFT_ONE, shift_sum, 0.0)
    packed = unspread(wide, n_dev, lens[GAIN_ONE])
    row = lax.broadcasted_iota(jnp.int32, (8, CW), 0)
    for t, first in ((0, 0), (2, D)):
        line = jnp.sum(d_all[t].astype(F32), axis=0, keepdims=True)
        line = jnp.where(row == BIAS_QV, line, 0.0)
        packed = packed + unspread(line, n_dev, lens[BIAS_QV], first + p.inn * CW)
    row = lax.broadcasted_iota(jnp.int32, (8, D), 0)
    for c in range(sum_up.shape[1] // D):
        line = jnp.where(row == BIAS_UP, sum_up[:, c * D : (c + 1) * D], 0.0)
        packed = packed + unspread(line, n_dev, lens[BIAS_UP], c * D)
    v_own[...] = packed.reshape(N_Z, n_x, N_IN, 8, LANES)
    start(v_to_x)

    up0.step(4)
    up1.step(4)
    wait_recv(v_to_x)
    for k in range(n_x - 1):
        v_own[:, p.x] = v_own[:, p.x] + v_x[k]
    start(v_to_z)
    wait_recv(w_to_x)

    def add_w(i, _):
        for t in range(3):
            value = w_own[t, i, p.x]
            for k in range(n_x - 1):
                value = value + w_x[k, t, i]
            w_own[t, i, p.x] = value
        return 0

    lax.fori_loop(0, N_Z, add_w, 0)
    start(w_to_z)
    wait_recv(v_to_z)
    for k in range(N_Z - 1):
        v_own[p.z, p.x] = v_own[p.z, p.x] + v_z[k]
    v_to_y.start()
    give_sib.wait_recv()
    add_rows(dh_own, [t_core.at[0]])
    v_to_y.wait_recv()
    mine = pl.ds(p.y * 2, 2)
    v_own[p.z, p.x, mine] = v_own[p.z, p.x, mine] + v_y[...]
    v_to_c.start()
    wait_recv(w_to_z)
    for t in range(3):
        value = w_own[t, p.z, p.x].astype(F32)
        for k in range(N_Z - 1):
            value = value + w_z[k, t].astype(F32)
        w_mine[t] = value
        stays, r, away = unit(t)

        @pl.when(jnp.logical_not(stays))
        def _():
            away.start()

        @pl.when(stays)
        def _():
            w_sum[r] = value

    blocks = vec_all[...].reshape(n_dev * 8, LANES)
    gain = spread(blocks, lens[GAIN_ONE], D)[GAIN_ONE : GAIN_ONE + 1]
    loads["tok"].wait()
    loads["res"].wait()
    normed, factor = norm_parts(tok[...].astype(F32))
    v_to_c.wait_recv()
    final = v_own[p.z, p.x, p.inn] + v_c[...]
    for r, length in enumerate(lens):
        vec_outs[r][...] = final[r : r + 1, 0:length]
    for r in range(3):
        stays, bring = arrival(r)

        @pl.when(jnp.logical_not(stays))
        def _():
            bring.wait_recv()

        g_qkv[:, r * CW : (r + 1) * CW] = w_sum[r]
    across.wait_recv()
    grad = dh_own[...].astype(F32) + t_far[...].astype(F32)
    grad_tokens[...] = (d_res[...] + norm_backward(grad, normed, factor, gain)).astype(BF16)
    for t in range(3):
        stays, _, away = unit(t)

        @pl.when(jnp.logical_not(stays))
        def _():
            away.wait_send()

    wait_send([give_diag, give_sib, across, v_to_y, v_to_c])
    wait_send(w_to_x + w_to_z + v_to_x + v_to_z)
    for item in pieces:
        item.finish()


def backward(n_dp, lens, tokens, seen, att, e_all, q, v, kt, h_one, n_one, wq, d_res, *grads):
    t_out, t_up, t_down, vec_all, sums, sum_up = grads
    n_x = n_dp // N_Z
    rows = tokens.shape[0]
    total = N_IN * rows
    w_rows = D // n_dp
    r_down, c_down = t_down.shape[3:]
    r_up, c_up = t_up.shape[3:]
    sizes = [(r_down // 2, c_down)] * 2 + [(r_up, c_up // 2)] * 2 + [t_out.shape[3:]]
    scratch = [
        pltpu.VMEM((N_IN, rows, CW), BF16),
        pltpu.VMEM((HP, total, LANES), F32),
        pltpu.VMEM((HP, total, LANES), BF16),
        pltpu.VMEM((HP, total, LANES), BF16),
        pltpu.VMEM((HP, HEAD_DIM, total), BF16),
        pltpu.VMEM((2, rows, D), BF16),
        pltpu.VMEM((2, rows, D), BF16),
        pltpu.VMEM((D, 3 * CW), BF16),
        pltpu.VMEM((rows, D), F32),
        pltpu.VMEM((HP, total, LANES), BF16),
        pltpu.VMEM((HP, HEAD_DIM, total), F32),
        pltpu.VMEM((2, BK, total), BF16),
        pltpu.VMEM((3, total, CW), BF16),
        pltpu.VMEM((2, rows, D), BF16),
        pltpu.VMEM((rows, D), BF16),
        pltpu.VMEM((3, N_Z, n_x, w_rows, CW), BF16),
        pltpu.VMEM((n_x - 1, 3, N_Z, w_rows, CW), BF16),
        pltpu.VMEM((N_Z - 1, 3, w_rows, CW), BF16),
        pltpu.VMEM((3, w_rows, CW), F32),
        pltpu.VMEM((3, w_rows, CW), F32),
        pltpu.VMEM((N_Z, n_x, N_IN, 8, LANES), F32),
        pltpu.VMEM((n_x - 1, N_Z, N_IN, 8, LANES), F32),
        pltpu.VMEM((N_Z - 1, N_IN, 8, LANES), F32),
        pltpu.VMEM((2, 8, LANES), F32),
        pltpu.VMEM((8, LANES), F32),
    ]
    for (r, c), order in zip(sizes, SCATTER_ORDERS):
        scratch += scatter_buffers(n_x, r, c, order)
    n_remote = 5 * scatter_count(n_x) + 3 + 2 * (n_x - 1) + 2 * (N_Z - 1) + 2 + 3
    return pl.pallas_call(
        functools.partial(backward_kernel, n_dp, lens),
        out_shape=(
            jax.ShapeDtypeStruct((rows, D), BF16),
            jax.ShapeDtypeStruct((w_rows, 3 * CW), F32),
            jax.ShapeDtypeStruct(t_out.shape[3:], F32),
            jax.ShapeDtypeStruct(t_up.shape[3:], F32),
            jax.ShapeDtypeStruct(t_down.shape[3:], F32),
        )
        + tuple(jax.ShapeDtypeStruct((1, length), F32) for length in lens),
        in_specs=[ANY] * 14 + [VMEM] * 3,
        out_specs=(VMEM,) * 13,
        scratch_shapes=scratch + [pltpu.SemaphoreType.DMA((2,))] + sem_shapes(n_remote, 21),
        compiler_params=params(2),
        name="backward",
    )(
        tokens,
        seen,
        att,
        e_all,
        q,
        v,
        kt,
        h_one,
        n_one,
        wq,
        d_res,
        t_out,
        t_up,
        t_down,
        vec_all,
        sums,
        sum_up,
    )


def on_device(
    tokens,
    lengths,
    w_qkv,
    bias_qv,
    w_out,
    bias_out,
    w_up,
    bias_up,
    w_down,
    bias_down,
    gain_one,
    shift_one,
    gain_two,
    shift_two,
    cotangent,
):
    n_dp = lax.axis_size("dp")
    n_x = n_dp // N_Z
    vectors = (
        bias_qv,
        bias_out,
        bias_up,
        bias_down,
        gain_one,
        shift_one,
        gain_two,
        shift_two,
    )
    lens = tuple(v.shape[0] for v in vectors)
    h_one, n_one, q, v, kt, att, e_all, mixed, a_out, a_up, a_down, vec_all, wq = forward(
        n_dp, tokens, lengths, w_qkv, vectors, w_out, w_up, w_down
    )
    output, d_res, seen, t_out, t_up, t_down, sums, sum_up = middle(
        n_dp,
        lens,
        tokens,
        mixed,
        a_out.reshape(N_IN, D, -1),
        a_up.reshape(N_IN, D, -1),
        a_down.reshape(N_IN, -1, CW),
        vec_all,
        cotangent,
    )

    def blocks(grads, like):
        return grads.reshape((2, N_Z, n_x) + like.shape)

    grad_tokens, g_qkv, g_out, g_up, g_down, *vecs = backward(
        n_dp,
        lens,
        tokens,
        seen,
        att,
        e_all,
        q,
        v,
        kt,
        h_one,
        n_one,
        wq,
        d_res,
        blocks(t_out, w_out),
        blocks(t_up, w_up),
        blocks(t_down, w_down),
        vec_all,
        sums,
        sum_up,
    )
    vecs = [vec.reshape(-1) for vec in vecs]
    return (
        output,
        grad_tokens,
        g_qkv,
        vecs[BIAS_QV],
        g_out,
        vecs[BIAS_OUT],
        g_up,
        vecs[BIAS_UP],
        g_down,
        vecs[BIAS_DOWN],
        vecs[GAIN_ONE],
        vecs[SHIFT_ONE],
        vecs[GAIN_TWO],
        vecs[SHIFT_TWO],
    )


def solution(mesh):
    rows = P(("dp", "inner"), None)
    mat = P("dp", "inner")
    vec = P(("dp", "inner"))
    return jax.shard_map(
        on_device,
        mesh=mesh,
        in_specs=(
            rows,
            P("dp", None),
            mat,
            vec,
            mat,
            vec,
            mat,
            vec,
            mat,
            vec,
            vec,
            vec,
            vec,
            vec,
            rows,
        ),
        out_specs=(rows, rows, mat, vec, mat, vec, mat, vec, mat, vec, vec, vec, vec, vec),
        check_vma=False,
    )
```

```python
import functools

import jax
import jax.numpy as jnp
from jax import lax
from jax.experimental import pallas as pl
from jax.experimental.pallas import tpu as pltpu
from jax.sharding import PartitionSpec as P

D = 768
HEADS = 12
HEAD_DIM = 64
EPS = 1e-06
NEG = -1e30
LANES = 128
HC = 256
N_Z = 4
N_IN = 4
HP = HEADS // N_IN
CW = HP * HEAD_DIM
SCALE = HEAD_DIM**-0.5
MESH = pl.DeviceIdType.MESH
NT = (((1,), (1,)), ((), ()))
TN = (((0,), (0,)), ((), ()))
F32, BF16 = jnp.float32, jnp.bfloat16
ANY = pl.BlockSpec(memory_space=pl.ANY)
VMEM = pl.BlockSpec(memory_space=pltpu.VMEM)
SMEM = pl.BlockSpec(memory_space=pltpu.SMEM)
VMEM_LIMIT = 62 << 20
BIAS_QV, BIAS_OUT, BIAS_UP, BIAS_DOWN, GAIN_ONE, SHIFT_ONE, GAIN_TWO, SHIFT_TWO = range(8)


def product(left, right):
    return jnp.dot(left, right, preferred_element_type=F32)


def product_tn(left, right):
    return lax.dot_general(left, right, TN, preferred_element_type=F32)


def product_nt(left, right):
    return lax.dot_general(left, right, NT, preferred_element_type=F32)


class Place:
    def __init__(self, n_dp):
        self.n_x = n_dp // N_Z
        self.dp = lax.axis_index("dp")
        self.inn = lax.axis_index("inner")
        self.x, self.z = self.dp % self.n_x, self.dp // self.n_x
        self.c, self.y = self.inn % 2, self.inn // 2
        self.sib = self.y * 2 + 1 - self.c
        self.far = (1 - self.y) * 2 + self.c
        self.diag = (1 - self.y) * 2 + 1 - self.c
        self.slots = (self.diag, self.far, self.sib, self.inn)

    def size(self, axis):
        return {"z": N_Z, "x": self.n_x, "y": 2, "c": 2}[axis]

    def peer(self, axis, k):
        if axis == "z":
            at = (self.z + k) % N_Z
            return at, (at * self.n_x + self.x, self.inn)
        if axis == "x":
            at = (self.x + k) % self.n_x
            return at, (self.z * self.n_x + at, self.inn)
        if axis == "y":
            return 1 - self.y, (self.dp, self.far)
        return 1 - self.c, (self.dp, self.sib)

    def peers(self, axis):
        return [self.peer(axis, k) + (k,) for k in range(1, self.size(axis))]


class Sems:
    def __init__(self, send, recv, local):
        self.send, self.recv, self.local = send, recv, local
        self.n = self.m = 0

    def remote(self, src, dst, device):
        i = self.n
        self.n += 1
        return pltpu.make_async_remote_copy(
            src_ref=src,
            dst_ref=dst,
            send_sem=self.send.at[i],
            recv_sem=self.recv.at[i],
            device_id=device,
            device_id_type=MESH,
        )

    def copy(self, src, dst):
        i = self.m
        self.m += 1
        return pltpu.make_async_copy(src, dst, self.local.at[i])


def sem_shapes(n_remote, n_local):
    return [
        pltpu.SemaphoreType.DMA((n_remote,)),
        pltpu.SemaphoreType.DMA((n_remote,)),
        pltpu.SemaphoreType.DMA((n_local,)),
    ]


def greet(place, axes, diagonal=False):
    devices = [device for axis in axes for _, device, _ in place.peers(axis)]
    if diagonal:
        devices.append((place.dp, place.diag))
    barrier = pltpu.get_barrier_semaphore()
    for device in devices:
        pl.semaphore_signal(barrier, inc=1, device_id=device, device_id_type=MESH)
    pl.semaphore_wait(barrier, len(devices))


def start(copies):
    for copy in copies:
        copy.start()


def wait_recv(copies):
    for copy in copies:
        copy.wait_recv()


def wait_send(copies):
    for copy in copies:
        copy.wait_send()


def wait(copies):
    for copy in copies:
        copy.wait()


def params(collective_id):
    return pltpu.CompilerParams(
        collective_id=collective_id, has_side_effects=True, vmem_limit_bytes=VMEM_LIMIT
    )


def part(ref, first, size, axis):
    cut = pl.ds(first, size)
    lead = (slice(None),) * (len(ref.shape) - 2)
    return ref.at[lead + ((cut, slice(None)) if axis == 0 else (slice(None), cut))]


def pack(value):
    half = value.shape[0] // 2
    return jnp.concatenate([value[:half], value[half:]], axis=1)


def packs(rows):
    return rows % 32 == 0


def packed_shape(rows, cols):
    return (rows // 2, 2 * cols) if packs(rows) else (rows, cols)


def first_rows(rows):
    return -(-rows // 32) * 16


DIAG, FAR, SIB, OWN = range(N_IN)


def place_mask(n_dev, length, size, first):
    column = lax.broadcasted_iota(jnp.int32, (n_dev * 8, size), 1) + first
    row = lax.broadcasted_iota(jnp.int32, (n_dev * 8, size), 0)
    begin = (row // 8) * length
    owned = jnp.logical_and(column >= begin, column < begin + length)
    column = lax.broadcasted_iota(jnp.int32, (LANES, size), 1) + first
    lane = lax.broadcasted_iota(jnp.int32, (LANES, size), 0)
    return owned, jnp.where(column % length == lane, 1.0, 0.0).astype(BF16)


def spread(blocks, length, size, first=0):
    n_dev = blocks.shape[0] // 8
    owned, lanes = place_mask(n_dev, length, size, first)
    wide = jnp.where(owned, product(blocks.astype(BF16), lanes), 0.0)
    return jnp.sum(wide.reshape(n_dev, 8, size), axis=0)


def unspread(rows, n_dev, length, first=0):
    size = rows.shape[1]
    if size > HC and n_dev * size > 32 * D:
        cut = size // 3
        parts = [
            unspread(rows[:, at : at + cut], n_dev, length, first + at)
            for at in range(0, size, cut)
        ]
        return parts[0] + parts[1] + parts[2]
    owned, lanes = place_mask(n_dev, length, size, first)
    total = None
    for _ in range(3):
        low = rows.astype(BF16)
        rows = rows - low.astype(F32)
        many = jnp.broadcast_to(low.astype(F32)[None], (n_dev,) + low.shape)
        many = jnp.where(owned, many.reshape(n_dev * 8, low.shape[1]), 0.0).astype(BF16)
        term = product_nt(many, lanes)
        total = term if total is None else total + term
    return total


def norm_parts(value):
    mean = jnp.mean(value, axis=-1, keepdims=True)
    centred = value - mean
    spread_of = jnp.mean(centred * centred, axis=-1, keepdims=True)
    factor = lax.rsqrt(spread_of + EPS)
    return centred * factor, factor


def norm_backward(grad, normed, factor, gain):
    scaled = grad * gain
    inner_mean = jnp.mean(scaled, axis=-1, keepdims=True)
    cross_mean = jnp.mean(scaled * normed, axis=-1, keepdims=True)
    return factor * (scaled - inner_mean - normed * cross_mean)


class Gather:
    def __init__(self, place, sems, source, out, view, order):
        p = place

        def at(inn, z, x):
            return view(out.at[inn, z, x])

        everything = slice(None)
        zs, xs = p.z, p.x
        self.own = sems.copy(source, at(p.inn, zs, xs))
        inns = [p.inn]
        self.stages = []
        for number, axis in enumerate(order):
            copies = []
            for _, device, _ in p.peers(axis):
                for inn in inns:
                    target = at(inn, zs, xs)
                    copies.append(sems.remote(source if number == 0 else target, target, device))
            self.stages.append(copies)
            if axis == "z":
                zs = everything
            elif axis == "x":
                xs = everything
            elif axis == "y":
                inns = [p.inn, p.far]

    def step(self, number):
        if number == 0:
            self.own.start()
        else:
            if number == 1:
                self.own.wait()
            wait_recv(self.stages[number - 1])
        if number < len(self.stages):
            start(self.stages[number])

    def finish(self):
        for copies in self.stages:
            wait_send(copies)


def gather_count(n_x, order):
    count, inns = 0, 1
    for axis in order:
        count += inns * {"z": N_Z - 1, "x": n_x - 1, "y": 1, "c": 1}[axis]
        inns = 2 if axis == "y" else inns
    return count


BQ = 640
CK = 256
GATHER_ORDERS = {"down0": "xyzc", "down1": "zyxc", "up0": "zyxc", "up1": "zxyc", "out": "zyxc"}


def forward_kernel(
    n_dp,
    lens,
    tokens,
    lengths,
    w_qkv,
    *rest,
):
    vec_in, rest = rest[:8], rest[8:]
    (
        w_out,
        w_up,
        w_down,
        h_out,
        n_out,
        q_out,
        v_out,
        kt_out,
        att_out,
        e_out,
        mixed,
        all_out,
        all_up,
        all_down,
        vec_all,
        wq_full,
        tok,
        h_ref,
        n_ref,
        q_ref,
        v_ref,
        kt_ref,
        att_ref,
        k_ref,
        vt_ref,
        s_ref,
        e_ref,
        low_ref,
        units,
        unit_in,
        wq_all,
        vec_own,
        out_pack,
        down_pack,
        e_sem,
        send,
        recv,
        local,
    ) = rest
    p = Place(n_dp)
    n_dev = n_dp * N_IN
    sems = Sems(send, recv, local)
    rows = tokens.shape[0]
    total = N_IN * rows
    n_down = down_pack.shape[0]
    half_down = first_rows(n_down)
    half_up = w_up.shape[1] // 2

    def piece(name, ref, out, first, size, axis):
        view = functools.partial(part, first=first, size=size, axis=axis)
        return Gather(p, sems, view(ref), out, view, GATHER_ORDERS[name])

    down0 = piece("down0", down_pack, all_down, 0, half_down, 0)
    down1 = piece("down1", down_pack, all_down, half_down, n_down - half_down, 0)
    up0 = piece("up0", w_up, all_up, 0, half_up, 1)
    up1 = piece("up1", w_up, all_up, half_up, half_up, 1)
    small = Gather(p, sems, out_pack, all_out, lambda ref: ref, GATHER_ORDERS["out"])
    pieces = [down0, down1, up0, up1, small]

    own_tok = sems.copy(tokens, tok.at[OWN])
    tok_far = sems.remote(tokens, tok.at[FAR], (p.dp, p.far))
    tok_sib = sems.remote(tokens, tok.at[SIB], (p.dp, p.sib))
    tok_on = sems.remote(tok.at[FAR], tok.at[DIAG], (p.dp, p.sib))
    block = vec_all.at[p.z, p.x, p.inn]
    vec_i = [
        sems.remote(vec_own, block, (p.dp, other)) for other in (p.sib, p.far, p.diag)
    ]
    mine = vec_all.at[p.z, p.x]
    vec_x = [sems.remote(mine, mine, device) for _, device, _ in p.peers("x")]
    column = vec_all.at[p.z]
    vec_z = [sems.remote(column, column, device) for _, device, _ in p.peers("z")]
    unit_base = sems.n
    sems.n += 3

    def unit(r):
        u = 3 * p.inn + r
        away = pltpu.make_async_remote_copy(
            src_ref=units.at[r],
            dst_ref=unit_in.at[u // N_IN],
            send_sem=send.at[unit_base + r],
            recv_sem=recv.at[unit_base + u // N_IN],
            device_id=(p.dp, u % N_IN),
            device_id_type=MESH,
        )
        return u % N_IN == p.inn, u // N_IN, away

    def arrival(t):
        u = p.inn + N_IN * t
        bring = pltpu.make_async_remote_copy(
            src_ref=units.at[0],
            dst_ref=unit_in.at[t],
            send_sem=send.at[unit_base],
            recv_sem=recv.at[unit_base + t],
            device_id=(p.dp, p.far),
            device_id_type=MESH,
        )
        return u // 3 == p.inn, bring

    wq_block = wq_all.at[p.z, p.x]
    wq_z = [sems.remote(wq_block, wq_block, device) for _, device, _ in p.peers("z")]
    wq_x = []
    for k in range(N_Z):
        spot = wq_all.at[(p.z + N_Z - k) % N_Z, p.x]
        wq_x.append([sems.remote(spot, spot, device) for _, device, _ in p.peers("x")])
    swap = [
        sems.remote(low_ref.at[s], mixed.at[p.inn], (p.dp, p.slots[s])) for s in (DIAG, FAR, SIB)
    ]
    swap_own = sems.copy(low_ref.at[OWN], mixed.at[p.inn])
    saves = [
        sems.copy(ref, out)
        for ref, out in (
            (h_ref, h_out),
            (n_ref, n_out),
            (q_ref, q_out),
            (v_ref, v_out),
            (kt_ref, kt_out),
        )
    ]
    att_save = sems.copy(att_ref, att_out)

    own_tok.start()
    vec_own[...] = jnp.zeros_like(vec_own)
    for r, length in enumerate(lens):
        vec_own[r : r + 1, 0:length] = vec_in[r][...].astype(F32)
    for r in range(3):
        units[r] = w_qkv[:, r * CW : (r + 1) * CW]
    out_pack[...] = pack(w_out[...]) if packs(w_out.shape[0]) else w_out[...]
    down_pack[...] = pack(w_down[...])

    greet(p, "zxyc", diagonal=True)
    start(vec_i)
    for r in range(3):
        stays, t, away = unit(r)

        @pl.when(jnp.logical_not(stays))
        def _():
            away.start()

        @pl.when(stays)
        def _():
            unit_in[t] = units[r]

    tok_far.start()
    tok_sib.start()
    vec_all[p.z, p.x, p.inn] = vec_own[...]
    down0.step(0)
    for t in range(3):
        stays, bring = arrival(t)

        @pl.when(jnp.logical_not(stays))
        def _():
            bring.wait_recv()

        wq_all[p.z, p.x, :, t * CW : (t + 1) * CW] = unit_in[t]
    start(wq_z)
    start(wq_x[0])
    wait_recv(vec_i)
    start(vec_x)
    wait_recv(vec_x)
    start(vec_z)
    for k in range(1, N_Z):
        wq_z[k - 1].wait_recv()
        start(wq_x[k])
    up0.step(0)
    up1.step(0)
    down1.step(0)
    small.step(0)
    wait_recv(vec_z)

    blocks = vec_all[...].reshape(n_dev * 8, LANES)
    shared = spread(blocks, lens[GAIN_ONE], D)
    gain, shift = shared[GAIN_ONE : GAIN_ONE + 1], shared[SHIFT_ONE : SHIFT_ONE + 1]
    bias_q = spread(blocks, lens[BIAS_QV], CW, p.inn * CW)[BIAS_QV : BIAS_QV + 1]
    bias_v = spread(blocks, lens[BIAS_QV], CW, D + p.inn * CW)[BIAS_QV : BIAS_QV + 1]

    def norm(s):
        here = pl.ds(s * rows, rows)
        normed, _ = norm_parts(tok[s].astype(F32))
        h_ref[here, :] = (normed * gain + shift).astype(BF16)
        n_ref[here, :] = normed.astype(BF16)

    def heads(s):
        here = pl.ds(s * rows, rows)
        first = p.slots[s] * rows
        end_one = lengths[0, 0]
        end_two = end_one + lengths[0, 1]
        index = lax.broadcasted_iota(jnp.int32, (rows, HEAD_DIM), 0) + first
        lane = lax.broadcasted_iota(jnp.int32, (rows, HEAD_DIM), 1)
        item = jnp.where(index >= end_one, 1, 0) + jnp.where(index >= end_two, 1, 0)
        same = jnp.where(lane == item, 1.0, 0.0).astype(BF16)
        other = jnp.where(jnp.logical_and(lane != item, lane < 3), NEG, 0.0).astype(BF16)
        ones = jnp.where(lane < 2, 1.0, 0.0).astype(BF16)
        qkv = product(h_ref[here, :], wq_full[...])
        q = (qkv[:, 0:CW] + bias_q).astype(BF16) * BF16(SCALE)
        k = qkv[:, CW : 2 * CW].astype(BF16)
        v = (qkv[:, 2 * CW :] + bias_v).astype(BF16)
        for h in range(HP):
            cols = slice(h * HEAD_DIM, (h + 1) * HEAD_DIM)
            q_ref[h, here, :] = jnp.concatenate([q[:, cols], same], axis=1)
            k_aug = jnp.concatenate([k[:, cols], other], axis=1)
            k_ref[h, here, :] = k_aug
            v_aug = jnp.concatenate([v[:, cols], ones], axis=1)
            v_ref[h, here, :] = v_aug
            vt_ref[h, :, here] = v_aug.T
            kt_ref[h, :, here] = k_aug.T[0:HEAD_DIM]

    own_tok.wait()
    norm(OWN)
    tok_sib.wait_recv()
    norm(SIB)
    for copies in wq_x:
        wait_recv(copies)
    if w_qkv.shape[0] % 16 == 0:
        wq_full[...] = wq_all[...].reshape(D, 3 * CW)
    else:
        rows_of = [wq_all[z, x].astype(F32) for z in range(N_Z) for x in range(p.n_x)]
        wq_full[...] = jnp.concatenate(rows_of, axis=0).astype(BF16)
    heads(OWN)
    heads(SIB)
    tok_far.wait_recv()
    tok_on.start()
    up0.step(1)
    down0.step(1)
    norm(FAR)
    heads(FAR)
    up1.step(1)
    tok_on.wait_recv()
    norm(DIAG)
    heads(DIAG)
    down1.step(1)
    start(saves)

    items = N_IN * HP

    def spill(it, slot):
        h, qb = it % HP, it // HP
        return pltpu.make_async_copy(
            e_ref.at[slot],
            e_out.at[h, :, pl.ds(pl.multiple_of(qb * BQ, BQ), BQ)],
            e_sem.at[slot],
        )

    actions = {
        0: [(up0, 2), (small, 1), (down0, 2)],
        1: [(up1, 2)],
        2: [(down1, 2)],
        4: [(small, 2)],
        5: [(up0, 3)],
        9: [(up1, 3), (up0, 4)],
        10: [(down1, 3)],
    }

    def body(it, _):
        slot = it % 2
        h, qb = it % HP, it // HP
        here = pl.ds(pl.multiple_of(qb * BQ, BQ), BQ)

        @pl.when(it >= 2)
        def _():
            spill(it - 2, slot).wait()

        q = q_ref[h, here, :]
        top = None
        for c in range(total // CK):
            cs = slice(c * CK, (c + 1) * CK)
            scores = product_nt(k_ref[h, cs, :], q)
            s_ref[cs, :] = scores
            peak = jnp.max(scores, axis=0, keepdims=True)
            top = peak if top is None else jnp.maximum(top, peak)
        acc = None
        for c in range(total // CK):
            cs = slice(c * CK, (c + 1) * CK)
            expo = jnp.exp(s_ref[cs, :] - top).astype(BF16)
            e_ref[slot, cs, :] = expo
            term = product(vt_ref[h, :, cs], expo)
            acc = term if acc is None else acc + term
        spill(it, slot).start()
        wide = acc.T
        sums = wide[:, HEAD_DIM : HEAD_DIM + 1]
        lane = lax.broadcasted_iota(jnp.int32, wide.shape, 1)
        att_ref[h, here, :] = jnp.where(lane < HEAD_DIM, wide / sums, wide)

        @pl.when(h == HP - 1)
        def _():
            low_ref[qb] = pack(
                jnp.concatenate([att_ref[i, here, 0:HEAD_DIM] for i in range(HP)], axis=1)
            ).astype(BF16)

        for when, acts in actions.items():

            @pl.when(it == when)
            def _():
                for which, number in acts:
                    which.step(number)

        for s in range(N_IN - 1):

            @pl.when(it == s * HP + HP - 1)
            def _():
                swap[s].start()

        return 0

    lax.fori_loop(0, items, body, 0)
    swap_own.start()
    att_save.start()
    down0.step(3)
    small.step(3)
    up1.step(4)
    down1.step(4)
    down0.step(4)
    small.step(4)
    wait(swap)
    swap_own.wait()
    wait(saves)
    att_save.wait()
    for it in (items - 2, items - 1):
        spill(it, it % 2).wait()
    for item in pieces:
        item.finish()
    for r in range(3):
        stays, _, away = unit(r)

        @pl.when(jnp.logical_not(stays))
        def _():
            away.wait_send()

    wait_send([tok_far, tok_sib, tok_on] + vec_i + vec_x + vec_z + wq_z)
    for copies in wq_x:
        wait_send(copies)


def forward(n_dp, tokens, lengths, w_qkv, vectors, w_out, w_up, w_down):
    n_x = n_dp // N_Z
    rows = tokens.shape[0]
    total = N_IN * rows
    lens = tuple(v.shape[0] for v in vectors)
    w_rows = w_qkv.shape[0]
    wide = (HP, total, LANES)

    def whole(shape):
        return jax.ShapeDtypeStruct((N_IN, N_Z, n_x) + shape, BF16)

    out_shape, down_shape = packed_shape(*w_out.shape), packed_shape(*w_down.shape)

    n_remote = 3 + 3 + 3 + (1 + N_Z) * (n_x - 1) + 2 * (N_Z - 1) + 3
    n_remote += sum(gather_count(n_x, order) for order in GATHER_ORDERS.values())
    return pl.pallas_call(
        functools.partial(forward_kernel, n_dp, lens),
        out_shape=(
            jax.ShapeDtypeStruct((total, D), BF16),
            jax.ShapeDtypeStruct((total, D), BF16),
            jax.ShapeDtypeStruct(wide, BF16),
            jax.ShapeDtypeStruct(wide, BF16),
            jax.ShapeDtypeStruct((HP, HEAD_DIM, total), BF16),
            jax.ShapeDtypeStruct(wide, F32),
            jax.ShapeDtypeStruct((HP, total, total), BF16),
            jax.ShapeDtypeStruct((N_IN,) + packed_shape(rows, CW), BF16),
            whole(out_shape),
            whole(w_up.shape),
            whole(down_shape),
            jax.ShapeDtypeStruct((N_Z, n_x, N_IN, 8, LANES), F32),
            jax.ShapeDtypeStruct((D, 3 * CW), BF16),
        ),
        in_specs=[ANY, SMEM, VMEM] + [VMEM] * 8 + [VMEM, ANY, VMEM],
        out_specs=(ANY,) * 11 + (VMEM,) * 2,
        scratch_shapes=[
            pltpu.VMEM((N_IN, rows, D), BF16),
            pltpu.VMEM((total, D), BF16),
            pltpu.VMEM((total, D), BF16),
            pltpu.VMEM(wide, BF16),
            pltpu.VMEM(wide, BF16),
            pltpu.VMEM((HP, HEAD_DIM, total), BF16),
            pltpu.VMEM(wide, F32),
            pltpu.VMEM(wide, BF16),
            pltpu.VMEM((HP, LANES, total), BF16),
            pltpu.VMEM((total, BQ), F32),
            pltpu.VMEM((2, total, BQ), BF16),
            pltpu.VMEM((N_IN,) + packed_shape(rows, CW), BF16),
            pltpu.VMEM((3, w_rows, CW), BF16),
            pltpu.VMEM((3, w_rows, CW), BF16),
            pltpu.VMEM((N_Z, n_x, w_rows, 3 * CW), BF16),
            pltpu.VMEM((8, LANES), F32),
            pltpu.VMEM(out_shape, BF16),
            pltpu.VMEM(down_shape, BF16),
            pltpu.SemaphoreType.DMA((2,)),
        ]
        + sem_shapes(n_remote, 13),
        compiler_params=params(0),
        name="forward",
    )(tokens, lengths, w_qkv, *[v.reshape(1, -1) for v in vectors], w_out, w_up, w_down)


GC = 384


def add_rows(total, terms, out=None):
    step = 128

    def one(i, _):
        at = pl.ds(pl.multiple_of(i * step, step), step)
        if out is None:
            value = total[at, :]
            for term in terms:
                value = value + term[at, :]
            total[at, :] = value
        else:
            value = total[at, :].astype(F32)
            for term in terms:
                value = value + term[at, :].astype(F32)
            out[at, :] = value
        return 0

    lax.fori_loop(0, total.shape[0] // step, one, 0)


def add_blocks(total, term):
    if len(total.shape) == 2:
        add_rows(total, [term])
        return

    def one(i, _):
        total[i] = total[i] + term[i]
        return 0

    lax.fori_loop(0, total.shape[0], one, 0)


def unpack_into(out, parts, rows):
    half = rows // 2
    packed = parts.shape[-1] == 2 * CW

    def one(d, _):
        for i in range(N_IN):
            cols = slice(i * CW, (i + 1) * CW)
            if packed:
                first = pl.ds(pl.multiple_of(d * rows, 16), half)
                second = pl.ds(pl.multiple_of(d * rows + half, 16), half)
                out[first, cols] = parts[i, d, :, 0:CW]
                out[second, cols] = parts[i, d, :, CW : 2 * CW]
            else:
                at = pl.ds(pl.multiple_of(d * LANES, LANES), LANES)
                out[at, cols] = parts[i, at, :]
        return 0

    lax.fori_loop(0, out.shape[0] // (rows if packed else LANES), one, 0)


def pack_into(parts, value, rows, first):
    for i in range(N_IN):
        cols = slice(i * CW, (i + 1) * CW)
        if parts.shape[-1] == 2 * CW:
            for b in range(value.shape[0] // rows):
                parts[i, first + b] = pack(value[b * rows : (b + 1) * rows, cols])
        else:
            parts[i] = value[:, cols]


def middle_kernel(
    n_dp,
    lens,
    tokens,
    mixed,
    a_out,
    a_up,
    a_down,
    vec_all,
    cotangent,
    output,
    d_res_out,
    seen,
    t_out,
    t_up,
    t_down,
    sums,
    sum_up,
    tok,
    mix,
    po,
    pu,
    pd,
    cot,
    fo,
    fd,
    att,
    res,
    n_two,
    h_two,
    act,
    d_up,
    b_up,
    d_mixed,
    d_res,
    out_ref,
    d_att,
    co,
    cu,
    cd,
    send,
    recv,
    local,
):
    p = Place(n_dp)
    n_dev = n_dp * N_IN
    sems = Sems(send, recv, local)
    rows = tokens.shape[0]
    ff = a_up.shape[0] * a_up.shape[2]
    r_out, r_down = D // n_dp, ff // n_dp
    loads = {
        name: sems.copy(src, dst)
        for name, src, dst in (
            ("out", a_out, po),
            ("mix", mixed, mix),
            ("tok", tokens, tok),
            ("up", a_up, pu),
            ("cot", cotangent, cot),
            ("down", a_down, pd),
        )
    }
    for load in loads.values():
        load.start()
    swap = [
        sems.remote(d_att.at[p.slots[s]], seen.at[s], (p.dp, p.slots[s])) for s in (DIAG, FAR, SIB)
    ]
    swap_own = sems.copy(d_att.at[p.inn], seen.at[OWN])

    def across(parts, buffer):
        return [
            sems.remote(parts.at[2 * yy + 1 - p.c], buffer.at[yy], (p.dp, p.sib))
            for yy in range(2)
        ]

    core_up, core_down, core_out = across(pu, cu), across(pd, cd), across(po, co)
    keeps = {
        name: [sems.copy(parts.at[2 * yy + p.c], out.at[yy]) for yy in range(2)]
        for name, parts, out in (("up", pu, t_up), ("down", pd, t_down), ("out", po, t_out))
    }
    out_save = sems.copy(out_ref, output)
    res_save = sems.copy(d_res, d_res_out)

    greet(p, "yc", diagonal=True)
    blocks = vec_all[...].reshape(n_dev * 8, LANES)
    shared = spread(blocks, lens[BIAS_OUT], D)
    for c in range(ff // D):
        b_up[:, c * D : (c + 1) * D] = spread(blocks, lens[BIAS_UP], D, c * D)[
            BIAS_UP : BIAS_UP + 1
        ]

    loads["out"].wait()
    loads["mix"].wait()
    unpack_into(fo, po, r_out)
    half = rows // 2
    for i in range(N_IN):
        cols = slice(i * CW, (i + 1) * CW)
        att[0:half, cols] = mix[i, :, 0:CW]
        att[half:rows, cols] = mix[i, :, CW : 2 * CW]
    loads["tok"].wait()
    residual = (
        tok[...].astype(F32) + product(att[...], fo[...]) + shared[BIAS_OUT : BIAS_OUT + 1]
    )
    res[...] = residual
    normed, factor = norm_parts(residual)
    n_two[...] = normed
    gain = shared[GAIN_TWO : GAIN_TWO + 1]
    h_two[...] = (normed * gain + shared[SHIFT_TWO : SHIFT_TWO + 1]).astype(BF16)
    loads["down"].wait()
    unpack_into(fd, pd, r_down)
    loads["up"].wait()
    loads["cot"].wait()

    def hidden(it, _):
        hid = pl.ds(pl.multiple_of(it * HC, HC), HC)
        inside = pl.ds(pl.multiple_of(it % (D // HC) * HC, HC), HC)
        up = product(h_two[...], pu[it // (D // HC), :, inside]) + b_up[:, hid]
        d_act = product_nt(cot[...], fd[hid, :])
        cdf = 0.5 * (1.0 + lax.erf(up * 0.7071067811865476))
        pdf = jnp.exp(-0.5 * up * up) * 0.3989422804014327
        act[:, hid] = (up * cdf).astype(BF16)
        grad = (d_act * (cdf + up * pdf)).astype(BF16)
        d_up[:, hid] = grad
        sum_up[:, hid] = jnp.sum(grad.astype(F32), axis=0, keepdims=True)
        return 0

    lax.fori_loop(0, ff // HC, hidden, 0)

    dh_two = None
    for i in range(N_IN):
        term = product_nt(d_up[:, i * D : (i + 1) * D], pu[i])
        dh_two = term if dh_two is None else dh_two + term
    normed = n_two[...]
    upstream = cot[...].astype(F32)
    value = upstream + norm_backward(dh_two, normed, factor, gain)
    d_res[...] = value
    res_save.start()
    low = value.astype(BF16)
    d_mixed[...] = low
    grad_att = product_nt(low, fo[...]).astype(BF16)
    for i in range(N_IN):
        d_att[i] = pack(grad_att[:, i * CW : (i + 1) * CW])
    start(swap)
    swap_own.start()

    def grad_up(i):
        cols = pl.ds(pl.multiple_of(i * D, D), D)
        pu[i] = product_tn(h_two[...], d_up[:, cols]).astype(BF16)

    for yy in range(2):
        grad_up(2 * yy + 1 - p.c)
    start(core_up)

    def grad_down(it, _):
        hid = pl.ds(pl.multiple_of(it * GC, GC), GC)
        value = product_tn(act[:, hid], cot[...])
        pack_into(pd, value.astype(BF16), r_down, it * (GC // r_down))
        return 0

    lax.fori_loop(0, ff // GC, grad_down, 0)
    start(core_down)
    pack_into(po, product_tn(att[...], d_mixed[...]).astype(BF16), r_out, 0)
    start(core_out)
    for yy in range(2):
        grad_up(2 * yy + p.c)

    def output_part(n, _):
        cols = pl.ds(pl.multiple_of(n * HC, HC), HC)
        value = product(act[...], fd[:, cols]) + res[:, cols]
        out_ref[:, cols] = value.astype(BF16)
        return 0

    res[...] = res[...] + shared[BIAS_DOWN : BIAS_DOWN + 1]
    lax.fori_loop(0, D // HC, output_part, 0)
    out_save.start()

    sums[...] = jnp.zeros_like(sums)
    sums[BIAS_OUT : BIAS_OUT + 1, :] = jnp.sum(low.astype(F32), axis=0, keepdims=True)
    sums[BIAS_DOWN : BIAS_DOWN + 1, :] = jnp.sum(upstream, axis=0, keepdims=True)
    sums[GAIN_TWO : GAIN_TWO + 1, :] = jnp.sum(dh_two * normed, axis=0, keepdims=True)
    sums[SHIFT_TWO : SHIFT_TWO + 1, :] = jnp.sum(dh_two, axis=0, keepdims=True)
    for copies, parts, buffer, name in (
        (core_up, pu, cu, "up"),
        (core_down, pd, cd, "down"),
        (core_out, po, co, "out"),
    ):
        wait_recv(copies)
        for yy in range(2):
            add_blocks(parts.at[2 * yy + p.c], buffer.at[yy])
        start(keeps[name])
    wait(swap)
    swap_own.wait()
    for copies in (core_up, core_down, core_out):
        wait_send(copies)
    for copies in keeps.values():
        wait(copies)
    out_save.wait()
    res_save.wait()


def middle(n_dp, lens, tokens, mixed, a_out, a_up, a_down, vec_all, cotangent):
    rows = tokens.shape[0]
    ff = a_up.shape[0] * a_up.shape[2]
    out_parts, up_parts, down_parts = a_out.shape[1:], a_up.shape[1:], a_down.shape[1:]
    return pl.pallas_call(
        functools.partial(middle_kernel, n_dp, lens),
        out_shape=(
            jax.ShapeDtypeStruct((rows, D), BF16),
            jax.ShapeDtypeStruct((rows, D), F32),
            jax.ShapeDtypeStruct((N_IN,) + packed_shape(rows, CW), BF16),
            jax.ShapeDtypeStruct((2,) + out_parts, BF16),
            jax.ShapeDtypeStruct((2,) + up_parts, BF16),
            jax.ShapeDtypeStruct((2,) + down_parts, BF16),
            jax.ShapeDtypeStruct((8, D), F32),
            jax.ShapeDtypeStruct((1, ff), F32),
        ),
        in_specs=[ANY] * 5 + [VMEM, ANY],
        out_specs=(ANY,) * 6 + (VMEM,) * 2,
        scratch_shapes=[
            pltpu.VMEM((rows, D), BF16),
            pltpu.VMEM((N_IN,) + packed_shape(rows, CW), BF16),
            pltpu.VMEM((N_IN,) + out_parts, BF16),
            pltpu.VMEM((N_IN,) + up_parts, BF16),
            pltpu.VMEM((N_IN,) + down_parts, BF16),
            pltpu.VMEM((rows, D), BF16),
            pltpu.VMEM((D, D), BF16),
            pltpu.VMEM((ff, D), BF16),
            pltpu.VMEM((rows, D), BF16),
            pltpu.VMEM((rows, D), F32),
            pltpu.VMEM((rows, D), F32),
            pltpu.VMEM((rows, D), BF16),
            pltpu.VMEM((rows, ff), BF16),
            pltpu.VMEM((rows, ff), BF16),
            pltpu.VMEM((1, ff), F32),
            pltpu.VMEM((rows, D), BF16),
            pltpu.VMEM((rows, D), F32),
            pltpu.VMEM((rows, D), BF16),
            pltpu.VMEM((N_IN,) + packed_shape(rows, CW), BF16),
            pltpu.VMEM((2,) + out_parts, BF16),
            pltpu.VMEM((2,) + up_parts, BF16),
            pltpu.VMEM((2,) + down_parts, BF16),
        ]
        + sem_shapes(9, 15),
        compiler_params=params(1),
        name="middle",
    )(tokens, mixed, a_out, a_up, a_down, vec_all, cotangent)


BK = 640
CQ = 1280
SCATTER_ORDERS = ("yxz", "xyz", "yxz", "xyz", "zyx")


class Scatter:
    def __init__(self, place, sems, blocks, order, buffers, out):
        self.order, self.out = order, out
        p = place
        self.total, self.buffers = buffers[0], dict(zip(order, buffers[1:]))
        self.load = sems.copy(blocks, self.total)
        _, _, n_x, _, _ = self.total.shape
        where = {"y": pl.ds(0, 2), "z": pl.ds(0, N_Z), "x": pl.ds(0, n_x)}
        own = {"y": p.y, "z": p.z, "x": p.x}
        self.copies, self.regions = {}, {}
        for axis in order:
            copies = []
            for at, device, k in p.peers(axis):
                there = dict(where)
                there[axis] = pl.ds(at, 1)
                src = self.total.at[there["y"], there["z"], there["x"]]
                copies.append(sems.remote(src, self.buffers[axis].at[k - 1], device))
            self.copies[axis] = copies
            where[axis] = pl.ds(own[axis], 1)
            self.regions[axis] = (where["y"], where["z"], where["x"])

    def step(self, number):
        if number == 0:
            self.load.start()
            return
        if number == 1:
            self.load.wait()
        else:
            axis = self.order[number - 2]
            wait_recv(self.copies[axis])
            region, buffer = self.total.at[self.regions[axis]], self.buffers[axis]
            if number - 1 == len(self.order):
                value = region[0, 0, 0].astype(F32)
                for k in range(buffer.shape[0]):
                    value = value + buffer[k, 0, 0, 0].astype(F32)
                self.out(value)
                return
            _, n_y, n_z, n_x, _, _ = buffer.shape

            def one(i, _):
                for y in range(n_y):
                    for x in range(n_x):
                        value = region[y, i, x]
                        for k in range(buffer.shape[0]):
                            value = value + buffer[k, y, i, x]
                        region[y, i, x] = value
                return 0

            lax.fori_loop(0, n_z, one, 0)
        start(self.copies[self.order[number - 1]])

    def finish(self):
        for axis in self.order:
            wait_send(self.copies[axis])


def scatter_buffers(n_x, rows, cols, order):
    sizes = {"y": 2, "z": N_Z, "x": n_x}
    shapes = [(2, N_Z, n_x, rows, cols)]
    left = dict(sizes)
    for axis in order:
        left[axis] = 1
        shapes.append((sizes[axis] - 1, left["y"], left["z"], left["x"], rows, cols))
    return [pltpu.VMEM(shape, BF16) for shape in shapes]


def scatter_count(n_x):
    return 1 + (N_Z - 1) + (n_x - 1)


def backward_kernel(n_dp, lens, *rest):
    (
        tokens,
        seen_in,
        att_in,
        e_all,
        q_in,
        v_in,
        kt_in,
        h_in,
        n_in,
        wq_in,
        d_res_in,
        t_out,
        t_up,
        t_down,
        vec_all,
        sums,
        sum_up,
    ) = rest[:17]
    grad_tokens, g_qkv, s_out, s_up, s_down = rest[17:22]
    vec_outs = rest[22:30]
    (
        seen,
        att,
        q_ref,
        v_ref,
        kt_ref,
        h_ref,
        n_ref,
        wq_ref,
        d_res,
        do_ref,
        dqt_ref,
        e_ref,
        d_all,
        t_core,
        t_far,
        g_w,
        norm_sums,
        w_own,
        w_x,
        w_z,
        w_mine,
        w_sum,
        v_own,
        v_x,
        v_z,
        v_y,
        v_c,
    ) = rest[30:57]
    buffers = rest[57:77]
    e_sem, send, recv, local = rest[77:]
    p = Place(n_dp)
    n_dev, n_x = n_dp * N_IN, n_dp // N_Z
    sems = Sems(send, recv, local)
    rows = tokens.shape[0]
    total = N_IN * rows
    n_down = t_down.shape[3]
    half_down = first_rows(n_down)
    half_up = t_up.shape[4] // 2

    def put(out, first):
        def write(value):
            size, cols = value.shape
            if cols == CW:
                out[...] = value
            elif cols == 2 * CW and out.shape[1] == CW:
                half = out.shape[0] // 2
                out[first : first + size, :] = value[:, 0:CW]
                out[half + first : half + first + size, :] = value[:, CW:]
            else:
                out[:, first : first + cols] = value

        return write

    loads = {
        name: sems.copy(src, dst)
        for name, src, dst in (
            ("seen", seen_in, seen),
            ("att", att_in, att),
            ("v", v_in, v_ref),
            ("kt", kt_in, kt_ref),
            ("q", q_in, q_ref),
            ("wq", wq_in, wq_ref),
            ("res", d_res_in, d_res),
        )
    }
    for name in ("seen", "att"):
        loads[name].start()
    pieces = []
    for number, (ref, out, first, size, axis) in enumerate(
        (
            (t_down, s_down, 0, half_down, 0),
            (t_down, s_down, half_down, n_down - half_down, 0),
            (t_up, s_up, 0, half_up, 1),
            (t_up, s_up, half_up, half_up, 1),
            (t_out, s_out, 0, t_out.shape[3], 0),
        )
    ):
        pieces.append(
            Scatter(
                p,
                sems,
                part(ref, first, size, axis),
                SCATTER_ORDERS[number],
                buffers[4 * number : 4 * number + 4],
                put(out, first),
            )
        )
    down0, down1, up0, up1, small = pieces
    for item in (down0, down1, small, up0, up1):
        item.step(0)
    for name in ("v", "kt", "q", "wq", "res"):
        loads[name].start()

    def room(i):
        return e_ref.at[i, :, pl.ds(0, D)]

    dh_far, dh_diag, dh_sib, dh_own = room(2), room(3), room(0), room(1)
    tok = n_ref.at[0]
    loads["tok"] = sems.copy(tokens, tok)

    def fetch(kb, h, half, slot):
        at = pl.ds(pl.multiple_of(kb * BK, BK), BK)
        src = e_all.at[h, at, pl.ds(half * CQ, CQ)]
        return pltpu.make_async_copy(src, e_ref.at[slot], e_sem.at[slot])

    fetch(0, 0, 0, 0).start()
    fetch(0, 0, 1, 1).start()
    feeds = []
    for s in range(N_IN):
        at = pl.ds(s * rows, rows)
        feeds.append(
            [sems.copy(n_in.at[at], n_ref.at[s % 2]), sems.copy(h_in.at[at], h_ref.at[s % 2])]
        )
    for feed in feeds[0:2]:
        start(feed)
    here, there = (p.dp, p.sib), (p.dp, p.far)
    give_diag = sems.remote(dh_diag, t_core.at[1], here)
    give_sib = sems.remote(dh_sib, t_core.at[0], here)
    across = sems.remote(dh_far, t_far, there)
    w_order = tuple(range(1, N_Z)) + (0,)
    w_to_x = {}
    for kz in w_order:
        w_to_x[kz] = [
            sems.remote(w_own.at[(p.z + kz) % N_Z, at], w_x.at[k - 1, kz], device)
            for at, device, k in p.peers("x")
        ]
    w_to_z = [
        sems.remote(w_own.at[at, p.x], w_z.at[k - 1], device) for at, device, k in p.peers("z")
    ]
    v_to_x = [
        sems.remote(v_own.at[:, at], v_x.at[k - 1], device) for at, device, k in p.peers("x")
    ]
    v_to_z = [
        sems.remote(v_own.at[at, p.x], v_z.at[k - 1], device) for at, device, k in p.peers("z")
    ]
    v_to_y = sems.remote(v_own.at[p.z, p.x, pl.ds((1 - p.y) * 2, 2)], v_y, there)
    v_to_c = sems.remote(v_own.at[p.z, p.x, p.sib], v_c, here)
    unit_base = sems.n

    def unit(t):
        u = p.inn + N_IN * t
        owner, r = u // 3, u % 3
        away = pltpu.make_async_remote_copy(
            src_ref=w_mine.at[t],
            dst_ref=w_sum.at[r],
            send_sem=send.at[unit_base + t],
            recv_sem=recv.at[unit_base + r],
            device_id=(p.dp, owner),
            device_id_type=MESH,
        )
        return owner == p.inn, r, away

    def arrival(r):
        u = 3 * p.inn + r
        bring = pltpu.make_async_remote_copy(
            src_ref=w_mine.at[0],
            dst_ref=w_sum.at[r],
            send_sem=send.at[unit_base],
            recv_sem=recv.at[unit_base + r],
            device_id=(p.dp, p.far),
            device_id_type=MESH,
        )
        return u % N_IN == p.inn, bring

    greet(p, "zxyc", diagonal=True)
    for item in (down0, down1, small, up0, up1):
        item.step(1)
    dqt_ref[...] = jnp.zeros_like(dqt_ref)
    loads["seen"].wait()
    loads["att"].wait()
    for s in range(N_IN):
        at = pl.ds(s * rows, rows)
        for h in range(HP):
            grad = jnp.concatenate(
                [
                    seen[s, :, side * CW + h * HEAD_DIM : side * CW + (h + 1) * HEAD_DIM]
                    for side in range(2)
                ],
                axis=0,
            ).astype(F32)
            both = att[h, at, :]
            scale = SCALE / both[:, HEAD_DIM : HEAD_DIM + 1]
            delta = jnp.sum(grad * both[:, 0:HEAD_DIM], axis=-1, keepdims=True) * -scale
            high = delta.astype(BF16).astype(F32)
            lane = lax.broadcasted_iota(jnp.int32, (rows, HEAD_DIM), 1)
            tail = jnp.where(lane == 0, high, jnp.where(lane == 1, delta - high, 0.0))
            do_ref[h, at, :] = jnp.concatenate([grad * scale, tail], axis=1).astype(BF16)
    for name in ("v", "kt", "q"):
        loads[name].wait()

    actions = {
        3: [(small, 2), (down0, 2), (down1, 2)],
        8: [(small, 3), (up0, 2), (up1, 2)],
        10: [(down0, 3), (down1, 3), (small, 4)],
        12: [(up0, 3), (up1, 3)],
        14: [(down0, 4), (down1, 4)],
    }
    last = N_IN - 1
    root = HEAD_DIM**0.5

    def act(kb, first, number):
        for when, acts in actions.items():
            if when in (number, number + HP):

                @pl.when(kb == first + (when - number) // HP)
                def _():
                    for which, stage in acts:
                        which.step(stage)

    def piece(kb, h, half, slot):
        at = pl.ds(pl.multiple_of(kb * BK, BK), BK)
        cs = slice(half * CQ, (half + 1) * CQ)
        expo, do = e_ref[slot], do_ref[h, cs, :]
        ds = (expo.astype(F32) * product_nt(v_ref[h, at, :], do)).astype(BF16)
        dv, dk = product(expo, do), product(ds, q_ref[h, cs, :])
        dqt_ref[h, :, cs] += product(kt_ref[h, :, at], ds)
        return dv, dk

    def finish_keys(kb, h, dv, dk):
        at = pl.ds(pl.multiple_of(kb * BK, BK), BK)
        cols = slice(h * HEAD_DIM, (h + 1) * HEAD_DIM)
        d_all[1, at, cols] = (dk * root).astype(BF16)
        d_all[2, at, cols] = (dv * root).astype(BF16)

    def both_halves(kb, _):
        for h in range(HP):
            slot = (kb * HP + h) % 2 * 2
            other = 2 - slot
            if h < HP - 1:
                for half in range(2):
                    fetch(kb, h + 1, half, other + half).start()
            else:

                @pl.when(kb == 0)
                def _():
                    for half in range(2):
                        fetch(1, 0, half, other + half).start()

                @pl.when(kb == 1)
                def _():
                    fetch(2, 0, 0, 0).start()

            for half in range(2):
                fetch(kb, h, half, slot + half).wait()
            dv0, dk0 = piece(kb, h, 0, slot)
            dv1, dk1 = piece(kb, h, 1, slot + 1)
            dv, dk = dv0 + dv1, dk0 + dk1
            finish_keys(kb, h, dv[:, 0:HEAD_DIM], dk[:, 0:HEAD_DIM])
            act(kb, 0, h)
        return 0

    lax.fori_loop(0, 2, both_halves, 0)

    def one_half(half, first):
        def run(kb, _):
            for h in range(HP):
                slot = ((kb - 2) * HP + h) % 2
                other = 1 - slot
                if h < HP - 1:
                    fetch(kb, h + 1, half, other).start()
                else:

                    @pl.when(kb == 2)
                    def _():
                        fetch(3, 0, half, other).start()

                    if half == 0:

                        @pl.when(kb == last)
                        def _():
                            fetch(2, 0, 1, other).start()

                fetch(kb, h, half, slot).wait()
                dv, dk = piece(kb, h, half, slot)
                at = pl.ds(pl.multiple_of(kb * BK, BK), BK)
                if half == 0:
                    att[h, at, :] = jnp.concatenate([dk[:, 0:HEAD_DIM], dv[:, 0:HEAD_DIM]], axis=1)
                else:
                    dk = dk[:, 0:HEAD_DIM] + att[h, at, 0:HEAD_DIM]
                    dv = dv[:, 0:HEAD_DIM] + att[h, at, HEAD_DIM:LANES]
                    finish_keys(kb, h, dv, dk)
                act(kb, 2, first + h)
            return 0

        lax.fori_loop(2, N_IN, run, 0)
        for h in range(HP):
            cs = slice(half * CQ, (half + 1) * CQ)
            d_all[0, cs, h * HEAD_DIM : (h + 1) * HEAD_DIM] = dqt_ref[h, :, cs].T.astype(BF16)

    def input_grad(i):
        at = pl.ds(i * rows, rows)
        feeds[i][0].wait()
        value = None
        for t in range(3):
            term = product_nt(d_all[t, at, :], wq_ref[:, t * CW : (t + 1) * CW])
            value = term if value is None else value + term
        gain_sum = jnp.sum(value * n_ref[i % 2].astype(F32), axis=0, keepdims=True)
        shift_sum = jnp.sum(value, axis=0, keepdims=True)
        return value.astype(BF16), gain_sum, shift_sum

    def weight_grad(i):
        at = pl.ds(i * rows, rows)
        feeds[i][1].wait()
        return [product_tn(h_ref[i % 2], d_all[t, at, :]) for t in range(3)]

    one_half(0, 2 * HP)
    loads["wq"].wait()
    value, gain_sum, shift_sum = input_grad(DIAG)
    dh_diag[...] = value
    give_diag.start()
    value, g_sum, s_sum = input_grad(FAR)
    dh_far[...] = value
    norm_sums[0:1, :] = gain_sum + g_sum
    norm_sums[1:2, :] = shift_sum + s_sum
    for t, (one, two) in enumerate(zip(weight_grad(DIAG), weight_grad(FAR))):
        g_w[t] = one + two
    for feed in feeds[2:4]:
        start(feed)
    give_diag.wait_recv()
    add_rows(dh_far, [t_core.at[1]])
    across.start()
    one_half(1, 4 * HP)
    wide = [one + two for one, two in zip(weight_grad(SIB), weight_grad(OWN))]
    wide = jnp.concatenate([value + g_w[t] for t, value in enumerate(wide)], axis=1)
    w_rows = D // n_dp
    if w_rows % 16 == 0:
        w_own[...] = wide.astype(BF16).reshape(N_Z, n_x, w_rows, 3 * CW)
    else:
        w_own[...] = wide.reshape(N_Z, n_x, w_rows, 3 * CW).astype(BF16)
    for kz in w_order:
        start(w_to_x[kz])
    value, gain_sum, shift_sum = input_grad(SIB)
    dh_sib[...] = value
    give_sib.start()
    loads["tok"].start()
    value, g_sum, s_sum = input_grad(OWN)
    dh_own[...] = value
    gain_sum = gain_sum + g_sum + norm_sums[0:1, :]
    shift_sum = shift_sum + s_sum + norm_sums[1:2, :]

    row = lax.broadcasted_iota(jnp.int32, (8, D), 0)
    wide = sums[...]
    wide = wide + jnp.where(row == GAIN_ONE, gain_sum, 0.0)
    wide = wide + jnp.where(row == SHIFT_ONE, shift_sum, 0.0)
    packed = unspread(wide, n_dev, lens[GAIN_ONE])
    row = lax.broadcasted_iota(jnp.int32, (8, CW), 0)
    for t, first in ((0, 0), (2, D)):
        line = jnp.sum(d_all[t].astype(F32), axis=0, keepdims=True)
        line = jnp.where(row == BIAS_QV, line, 0.0)
        packed = packed + unspread(line, n_dev, lens[BIAS_QV], first + p.inn * CW)
    row = lax.broadcasted_iota(jnp.int32, (8, D), 0)
    for c in range(sum_up.shape[1] // D):
        line = jnp.where(row == BIAS_UP, sum_up[:, c * D : (c + 1) * D], 0.0)
        packed = packed + unspread(line, n_dev, lens[BIAS_UP], c * D)
    v_own[...] = packed.reshape(N_Z, n_x, N_IN, 8, LANES)
    start(v_to_x)

    for kz in w_order:
        wait_recv(w_to_x[kz])
        at = (p.z + kz) % N_Z
        value = w_own[at, p.x]
        for k in range(n_x - 1):
            value = value + w_x[k, kz]
        w_own[at, p.x] = value
        if kz:
            w_to_z[kz - 1].start()
    wait_recv(v_to_x)
    for k in range(n_x - 1):
        v_own[:, p.x] = v_own[:, p.x] + v_x[k]
    start(v_to_z)
    up0.step(4)
    up1.step(4)
    give_sib.wait_recv()
    add_rows(dh_own, [t_core.at[0]])
    wait_recv(v_to_z)
    for k in range(N_Z - 1):
        v_own[p.z, p.x] = v_own[p.z, p.x] + v_z[k]
    v_to_y.start()
    wide = w_own[p.z, p.x].astype(F32)
    for k in range(N_Z - 1):
        w_to_z[k].wait_recv()
        wide = wide + w_z[k].astype(F32)
    for t in range(3):
        value = wide[:, t * CW : (t + 1) * CW]
        w_mine[t] = value
        stays, r, away = unit(t)

        @pl.when(jnp.logical_not(stays))
        def _():
            away.start()

        @pl.when(stays)
        def _():
            w_sum[r] = value

    v_to_y.wait_recv()
    mine = pl.ds(p.y * 2, 2)
    v_own[p.z, p.x, mine] = v_own[p.z, p.x, mine] + v_y[...]
    v_to_c.start()
    blocks = vec_all[...].reshape(n_dev * 8, LANES)
    gain = spread(blocks, lens[GAIN_ONE], D)[GAIN_ONE : GAIN_ONE + 1]
    loads["tok"].wait()
    loads["res"].wait()
    normed, factor = norm_parts(tok[...].astype(F32))
    v_to_c.wait_recv()
    final = v_own[p.z, p.x, p.inn] + v_c[...]
    for r, length in enumerate(lens):
        vec_outs[r][...] = final[r : r + 1, 0:length]
    for r in range(3):
        stays, bring = arrival(r)

        @pl.when(jnp.logical_not(stays))
        def _():
            bring.wait_recv()

        g_qkv[:, r * CW : (r + 1) * CW] = w_sum[r]
    across.wait_recv()
    grad = dh_own[...].astype(F32) + t_far[...].astype(F32)
    grad_tokens[...] = (d_res[...] + norm_backward(grad, normed, factor, gain)).astype(BF16)
    for t in range(3):
        stays, _, away = unit(t)

        @pl.when(jnp.logical_not(stays))
        def _():
            away.wait_send()

    wait_send([give_diag, give_sib, across, v_to_y, v_to_c])
    wait_send(w_to_z + v_to_x + v_to_z)
    for kz in w_order:
        wait_send(w_to_x[kz])
    for item in pieces:
        item.finish()


def backward(n_dp, lens, like_out, like_down, tokens, seen, att, e_all, q, v, kt, h_one, n_one, wq, d_res, *grads):
    t_out, t_up, t_down, vec_all, sums, sum_up = grads
    n_x = n_dp // N_Z
    rows = tokens.shape[0]
    total = N_IN * rows
    w_rows = D // n_dp
    r_down, c_down = t_down.shape[3:]
    r_up, c_up = t_up.shape[3:]
    r_first = first_rows(r_down)
    sizes = [(r_first, c_down), (r_down - r_first, c_down)]
    sizes += [(r_up, c_up // 2)] * 2 + [t_out.shape[3:]]
    scratch = [
        pltpu.VMEM((N_IN,) + packed_shape(rows, CW), BF16),
        pltpu.VMEM((HP, total, LANES), F32),
        pltpu.VMEM((HP, total, LANES), BF16),
        pltpu.VMEM((HP, total, LANES), BF16),
        pltpu.VMEM((HP, HEAD_DIM, total), BF16),
        pltpu.VMEM((2, rows, D), BF16),
        pltpu.VMEM((2, rows, D), BF16),
        pltpu.VMEM((D, 3 * CW), BF16),
        pltpu.VMEM((rows, D), F32),
        pltpu.VMEM((HP, total, LANES), BF16),
        pltpu.VMEM((HP, HEAD_DIM, total), F32),
        pltpu.VMEM((4, BK, CQ), BF16),
        pltpu.VMEM((3, total, CW), BF16),
        pltpu.VMEM((2, rows, D), BF16),
        pltpu.VMEM((rows, D), BF16),
        pltpu.VMEM((3, D, CW), F32),
        pltpu.VMEM((2, D), F32),
        pltpu.VMEM((N_Z, n_x, w_rows, 3 * CW), BF16),
        pltpu.VMEM((n_x - 1, N_Z, w_rows, 3 * CW), BF16),
        pltpu.VMEM((N_Z - 1, w_rows, 3 * CW), BF16),
        pltpu.VMEM((3, w_rows, CW), F32),
        pltpu.VMEM((3, w_rows, CW), F32),
        pltpu.VMEM((N_Z, n_x, N_IN, 8, LANES), F32),
        pltpu.VMEM((n_x - 1, N_Z, N_IN, 8, LANES), F32),
        pltpu.VMEM((N_Z - 1, N_IN, 8, LANES), F32),
        pltpu.VMEM((2, 8, LANES), F32),
        pltpu.VMEM((8, LANES), F32),
    ]
    for (r, c), order in zip(sizes, SCATTER_ORDERS):
        scratch += scatter_buffers(n_x, r, c, order)
    n_remote = 5 * scatter_count(n_x) + 3 + (N_Z + 1) * (n_x - 1) + 2 * (N_Z - 1) + 2 + 3
    return pl.pallas_call(
        functools.partial(backward_kernel, n_dp, lens),
        out_shape=(
            jax.ShapeDtypeStruct((rows, D), BF16),
            jax.ShapeDtypeStruct((w_rows, 3 * CW), F32),
            jax.ShapeDtypeStruct(like_out.shape, F32),
            jax.ShapeDtypeStruct(t_up.shape[3:], F32),
            jax.ShapeDtypeStruct(like_down.shape, F32),
        )
        + tuple(jax.ShapeDtypeStruct((1, length), F32) for length in lens),
        in_specs=[ANY] * 14 + [VMEM] * 3,
        out_specs=(VMEM,) * 13,
        scratch_shapes=scratch + [pltpu.SemaphoreType.DMA((4,))] + sem_shapes(n_remote, 21),
        compiler_params=params(2),
        name="backward",
    )(
        tokens,
        seen,
        att,
        e_all,
        q,
        v,
        kt,
        h_one,
        n_one,
        wq,
        d_res,
        t_out,
        t_up,
        t_down,
        vec_all,
        sums,
        sum_up,
    )


def on_device(
    tokens,
    lengths,
    w_qkv,
    bias_qv,
    w_out,
    bias_out,
    w_up,
    bias_up,
    w_down,
    bias_down,
    gain_one,
    shift_one,
    gain_two,
    shift_two,
    cotangent,
):
    n_dp = lax.axis_size("dp")
    n_x = n_dp // N_Z
    vectors = (
        bias_qv,
        bias_out,
        bias_up,
        bias_down,
        gain_one,
        shift_one,
        gain_two,
        shift_two,
    )
    lens = tuple(v.shape[0] for v in vectors)
    h_one, n_one, q, v, kt, att, e_all, mixed, a_out, a_up, a_down, vec_all, wq = forward(
        n_dp, tokens, lengths, w_qkv, vectors, w_out, w_up, w_down
    )

    def by_dp(blocks):
        return blocks.reshape((N_IN, n_dp) + blocks.shape[3:])

    output, d_res, seen, t_out, t_up, t_down, sums, sum_up = middle(
        n_dp,
        lens,
        tokens,
        mixed,
        by_dp(a_out) if packs(w_out.shape[0]) else a_out.reshape(N_IN, D, CW),
        a_up.reshape(N_IN, D, -1),
        by_dp(a_down),
        vec_all,
        cotangent,
    )

    def blocks(grads, like):
        return grads.reshape((2, N_Z, n_x) + like.shape[3:])

    grad_tokens, g_qkv, g_out, g_up, g_down, *vecs = backward(
        n_dp,
        lens,
        w_out,
        w_down,
        tokens,
        seen,
        att,
        e_all,
        q,
        v,
        kt,
        h_one,
        n_one,
        wq,
        d_res,
        blocks(t_out, a_out),
        blocks(t_up, a_up),
        blocks(t_down, a_down),
        vec_all,
        sums,
        sum_up,
    )
    vecs = [vec.reshape(-1) for vec in vecs]
    return (
        output,
        grad_tokens,
        g_qkv,
        vecs[BIAS_QV],
        g_out,
        vecs[BIAS_OUT],
        g_up,
        vecs[BIAS_UP],
        g_down,
        vecs[BIAS_DOWN],
        vecs[GAIN_ONE],
        vecs[SHIFT_ONE],
        vecs[GAIN_TWO],
        vecs[SHIFT_TWO],
    )


def solution(mesh):
    rows = P(("dp", "inner"), None)
    mat = P("dp", "inner")
    vec = P(("dp", "inner"))
    return jax.shard_map(
        on_device,
        mesh=mesh,
        in_specs=(
            rows,
            P("dp", None),
            mat,
            vec,
            mat,
            vec,
            mat,
            vec,
            mat,
            vec,
            vec,
            vec,
            vec,
            vec,
            rows,
        ),
        out_specs=(rows, rows, mat, vec, mat, vec, mat, vec, mat, vec, vec, vec, vec, vec),
        check_vma=False,
    )
```

```python
import functools

import jax
import jax.numpy as jnp
from jax import lax
from jax.experimental import pallas as pl
from jax.experimental.pallas import tpu as pltpu
from jax.sharding import PartitionSpec as P

D = 768
HEADS = 12
HEAD_DIM = 64
EPS = 1e-06
NEG = -1e30
LANES = 128
HC = 256
N_Z = 4
N_IN = 4
HP = HEADS // N_IN
CW = HP * HEAD_DIM
SCALE = HEAD_DIM**-0.5
MESH = pl.DeviceIdType.MESH
NT = (((1,), (1,)), ((), ()))
TN = (((0,), (0,)), ((), ()))
F32, BF16 = jnp.float32, jnp.bfloat16
ANY = pl.BlockSpec(memory_space=pl.ANY)
VMEM = pl.BlockSpec(memory_space=pltpu.VMEM)
SMEM = pl.BlockSpec(memory_space=pltpu.SMEM)
VMEM_LIMIT = 62 << 20
BIAS_QV, BIAS_OUT, BIAS_UP, BIAS_DOWN, GAIN_ONE, SHIFT_ONE, GAIN_TWO, SHIFT_TWO = range(8)


def product(left, right):
    return jnp.dot(left, right, preferred_element_type=F32)


def product_tn(left, right):
    return lax.dot_general(left, right, TN, preferred_element_type=F32)


def product_nt(left, right):
    return lax.dot_general(left, right, NT, preferred_element_type=F32)


class Place:
    def __init__(self, n_dp):
        self.n_x = n_dp // N_Z
        self.dp = lax.axis_index("dp")
        self.inn = lax.axis_index("inner")
        self.x, self.z = self.dp % self.n_x, self.dp // self.n_x
        self.c, self.y = self.inn % 2, self.inn // 2
        self.sib = self.y * 2 + 1 - self.c
        self.far = (1 - self.y) * 2 + self.c
        self.diag = (1 - self.y) * 2 + 1 - self.c
        self.slots = (self.diag, self.far, self.sib, self.inn)

    def size(self, axis):
        return {"z": N_Z, "x": self.n_x, "y": 2, "c": 2}[axis]

    def peer(self, axis, k):
        if axis == "z":
            at = (self.z + k) % N_Z
            return at, (at * self.n_x + self.x, self.inn)
        if axis == "x":
            at = (self.x + k) % self.n_x
            return at, (self.z * self.n_x + at, self.inn)
        if axis == "y":
            return 1 - self.y, (self.dp, self.far)
        return 1 - self.c, (self.dp, self.sib)

    def peers(self, axis):
        return [self.peer(axis, k) + (k,) for k in range(1, self.size(axis))]


class Sems:
    def __init__(self, send, recv, local):
        self.send, self.recv, self.local = send, recv, local
        self.n = self.m = 0

    def remote(self, src, dst, device):
        i = self.n
        self.n += 1
        return pltpu.make_async_remote_copy(
            src_ref=src,
            dst_ref=dst,
            send_sem=self.send.at[i],
            recv_sem=self.recv.at[i],
            device_id=device,
            device_id_type=MESH,
        )

    def copy(self, src, dst):
        i = self.m
        self.m += 1
        return pltpu.make_async_copy(src, dst, self.local.at[i])


def sem_shapes(n_remote, n_local):
    return [
        pltpu.SemaphoreType.DMA((n_remote,)),
        pltpu.SemaphoreType.DMA((n_remote,)),
        pltpu.SemaphoreType.DMA((n_local,)),
    ]


def partners(place, axes, diagonal=False):
    devices = [device for axis in axes for _, device, _ in place.peers(axis)]
    if diagonal:
        devices.append((place.dp, place.diag))
    return devices


def arrive(devices):
    barrier = pltpu.get_barrier_semaphore()
    for device in devices:
        pl.semaphore_signal(barrier, inc=1, device_id=device, device_id_type=MESH)


def all_in(devices):
    pl.semaphore_wait(pltpu.get_barrier_semaphore(), len(devices))


def start(copies):
    for copy in copies:
        copy.start()


def wait_recv(copies):
    for copy in copies:
        copy.wait_recv()


def wait_send(copies):
    for copy in copies:
        copy.wait_send()


def wait(copies):
    for copy in copies:
        copy.wait()


def params(collective_id):
    return pltpu.CompilerParams(
        collective_id=collective_id, has_side_effects=True, vmem_limit_bytes=VMEM_LIMIT
    )


def part(ref, first, size, axis):
    cut = pl.ds(first, size)
    lead = (slice(None),) * (len(ref.shape) - 2)
    return ref.at[lead + ((cut, slice(None)) if axis == 0 else (slice(None), cut))]


def pack(value):
    half = value.shape[0] // 2
    return jnp.concatenate([value[:half], value[half:]], axis=1)


def packs(rows):
    return rows % 32 == 0


def packed_shape(rows, cols):
    return (rows // 2, 2 * cols) if packs(rows) else (rows, cols)


def first_rows(rows):
    return -(-rows // 32) * 16


DIAG, FAR, SIB, OWN = range(N_IN)


def place_mask(n_dev, length, size, first):
    column = lax.broadcasted_iota(jnp.int32, (n_dev * 8, size), 1) + first
    row = lax.broadcasted_iota(jnp.int32, (n_dev * 8, size), 0)
    begin = (row // 8) * length
    owned = jnp.logical_and(column >= begin, column < begin + length)
    column = lax.broadcasted_iota(jnp.int32, (LANES, size), 1) + first
    lane = lax.broadcasted_iota(jnp.int32, (LANES, size), 0)
    return owned, jnp.where(column % length == lane, 1.0, 0.0).astype(BF16)


def spread(blocks, length, size, first=0):
    n_dev = blocks.shape[0] // 8
    owned, lanes = place_mask(n_dev, length, size, first)
    wide = jnp.where(owned, product(blocks.astype(BF16), lanes), 0.0)
    return jnp.sum(wide.reshape(n_dev, 8, size), axis=0)


def unspread(rows, n_dev, length, first=0):
    size = rows.shape[1]
    if size > HC and n_dev * size > 32 * D:
        cut = size // 3
        parts = [
            unspread(rows[:, at : at + cut], n_dev, length, first + at)
            for at in range(0, size, cut)
        ]
        return parts[0] + parts[1] + parts[2]
    owned, lanes = place_mask(n_dev, length, size, first)
    total = None
    for _ in range(3):
        low = rows.astype(BF16)
        rows = rows - low.astype(F32)
        many = jnp.broadcast_to(low.astype(F32)[None], (n_dev,) + low.shape)
        many = jnp.where(owned, many.reshape(n_dev * 8, low.shape[1]), 0.0).astype(BF16)
        term = product_nt(many, lanes)
        total = term if total is None else total + term
    return total


def norm_parts(value):
    mean = jnp.mean(value, axis=-1, keepdims=True)
    centred = value - mean
    spread_of = jnp.mean(centred * centred, axis=-1, keepdims=True)
    factor = lax.rsqrt(spread_of + EPS)
    return centred * factor, factor


def norm_backward(grad, normed, factor, gain):
    scaled = grad * gain
    inner_mean = jnp.mean(scaled, axis=-1, keepdims=True)
    cross_mean = jnp.mean(scaled * normed, axis=-1, keepdims=True)
    return factor * (scaled - inner_mean - normed * cross_mean)


class Gather:
    def __init__(self, place, sems, source, out, view, order):
        p = place

        def at(inn, z, x):
            return view(out.at[inn, z, x])

        everything = slice(None)
        zs, xs = p.z, p.x
        self.own = sems.copy(source, at(p.inn, zs, xs))
        inns = [p.inn]
        self.stages = []
        for number, axis in enumerate(order):
            copies = []
            for _, device, _ in p.peers(axis):
                for inn in inns:
                    target = at(inn, zs, xs)
                    copies.append(sems.remote(source if number == 0 else target, target, device))
            self.stages.append(copies)
            if axis == "z":
                zs = everything
            elif axis == "x":
                xs = everything
            elif axis == "y":
                inns = [p.inn, p.far]

    def step(self, number):
        if number == 0:
            self.own.start()
        else:
            if number == 1:
                self.own.wait()
            wait_recv(self.stages[number - 1])
        if number < len(self.stages):
            start(self.stages[number])

    def finish(self):
        for copies in self.stages:
            wait_send(copies)


def gather_count(n_x, order):
    count, inns = 0, 1
    for axis in order:
        count += inns * {"z": N_Z - 1, "x": n_x - 1, "y": 1, "c": 1}[axis]
        inns = 2 if axis == "y" else inns
    return count


BQ = 640
CK = 256
GATHER_ORDERS = {"down0": "xyzc", "down1": "zyxc", "up0": "zyxc", "up1": "zxyc", "out": "zxyc"}


def forward_kernel(
    n_dp,
    lens,
    tokens,
    lengths,
    w_qkv,
    *rest,
):
    vec_in, rest = rest[:8], rest[8:]
    (
        w_out,
        w_up,
        w_down,
        h_out,
        n_out,
        q_out,
        v_out,
        kt_out,
        att_out,
        e_out,
        mixed,
        all_out,
        all_up,
        all_down,
        vec_all,
        wq_full,
        tok,
        h_ref,
        n_ref,
        q_ref,
        v_ref,
        kt_ref,
        att_ref,
        k_ref,
        vt_ref,
        s_ref,
        e_ref,
        low_ref,
        units,
        unit_in,
        w_wide,
        wq_all,
        vec_own,
        out_pack,
        e_sem,
        send,
        recv,
        local,
    ) = rest
    p = Place(n_dp)
    n_dev = n_dp * N_IN
    sems = Sems(send, recv, local)
    rows = tokens.shape[0]
    total = N_IN * rows
    n_down = w_down.shape[0]
    half_down = first_rows(n_down)
    half_up = w_up.shape[1] // 2

    def piece(name, ref, out, first, size, axis):
        view = functools.partial(part, first=first, size=size, axis=axis)
        return Gather(p, sems, view(ref), out, view, GATHER_ORDERS[name])

    down0 = piece("down0", w_down, all_down, 0, half_down, 0)
    down1 = piece("down1", w_down, all_down, half_down, n_down - half_down, 0)
    up0 = piece("up0", w_up, all_up, 0, half_up, 1)
    up1 = piece("up1", w_up, all_up, half_up, half_up, 1)
    small = Gather(p, sems, out_pack, all_out, lambda ref: ref, GATHER_ORDERS["out"])
    pieces = [down0, down1, up0, up1, small]

    own_tok = sems.copy(tokens, tok.at[OWN])
    tok_sib = sems.remote(tokens, tok.at[SIB], (p.dp, p.sib))
    half_rows = rows // 2
    halves = [pl.ds(i * half_rows, half_rows) for i in range(2)]
    tok_far = [sems.remote(tokens.at[at], tok.at[FAR, at], (p.dp, p.far)) for at in halves]
    tok_on = [sems.remote(tok.at[FAR, at], tok.at[DIAG, at], (p.dp, p.sib)) for at in halves]
    block = vec_all.at[p.z, p.x, p.inn]
    vec_i = [
        sems.remote(vec_own, block, (p.dp, other)) for other in (p.sib, p.far, p.diag)
    ]
    mine = vec_all.at[p.z, p.x]
    vec_x = [sems.remote(mine, mine, device) for _, device, _ in p.peers("x")]
    column = vec_all.at[p.z]
    vec_z = [sems.remote(column, column, device) for _, device, _ in p.peers("z")]
    unit_base = sems.n
    sems.n += 3

    def unit(r):
        u = 3 * p.inn + r
        away = pltpu.make_async_remote_copy(
            src_ref=units.at[r],
            dst_ref=unit_in.at[u // N_IN],
            send_sem=send.at[unit_base + r],
            recv_sem=recv.at[unit_base + u // N_IN],
            device_id=(p.dp, u % N_IN),
            device_id_type=MESH,
        )
        return u % N_IN == p.inn, u // N_IN, away

    def arrival(t):
        u = p.inn + N_IN * t
        bring = pltpu.make_async_remote_copy(
            src_ref=units.at[0],
            dst_ref=unit_in.at[t],
            send_sem=send.at[unit_base],
            recv_sem=recv.at[unit_base + t],
            device_id=(p.dp, p.far),
            device_id_type=MESH,
        )
        return u // 3 == p.inn, bring

    wq_block = wq_all.at[p.z, p.x]
    wq_z = [sems.remote(wq_block, wq_block, device) for _, device, _ in p.peers("z")]
    wq_x = []
    for k in range(N_Z):
        spot = wq_all.at[(p.z + N_Z - k) % N_Z, p.x]
        wq_x.append([sems.remote(spot, spot, device) for _, device, _ in p.peers("x")])
    swap = [
        sems.remote(low_ref.at[s], mixed.at[p.inn], (p.dp, p.slots[s])) for s in (DIAG, FAR, SIB)
    ]
    swap_own = sems.copy(low_ref.at[OWN], mixed.at[p.inn])
    saves = [
        sems.copy(ref, out)
        for ref, out in (
            (h_ref, h_out),
            (n_ref, n_out),
            (q_ref, q_out),
            (v_ref, v_out),
        )
    ]
    late_saves = [sems.copy(att_ref, att_out), sems.copy(kt_ref, kt_out)]

    near = partners(p, "zxyc", diagonal=True)
    arrive(near)
    own_tok.start()
    vec_own[...] = jnp.zeros_like(vec_own)
    for r, length in enumerate(lens):
        vec_own[r : r + 1, 0:length] = vec_in[r][...].astype(F32)
    for r in range(3):
        units[r] = w_qkv[:, r * CW : (r + 1) * CW]

    all_in(near)
    start(vec_i)
    for r in range(3):
        stays, t, away = unit(r)

        @pl.when(jnp.logical_not(stays))
        def _():
            away.start()

        @pl.when(stays)
        def _():
            unit_in[t] = units[r]

    start(tok_far)
    tok_sib.start()
    vec_all[p.z, p.x, p.inn] = vec_own[...]
    down0.step(0)
    out_pack[...] = pack(w_out[...]) if packs(w_out.shape[0]) else w_out[...]
    for t in range(3):
        stays, bring = arrival(t)

        @pl.when(jnp.logical_not(stays))
        def _():
            bring.wait_recv()

        wq_all[p.z, p.x, :, t * CW : (t + 1) * CW] = unit_in[t]
    start(wq_z)
    start(wq_x[0])
    wait_recv(vec_i)
    start(vec_x)
    wait_recv(vec_x)
    start(vec_z)
    for k in range(1, N_Z):
        wq_z[k - 1].wait_recv()
        start(wq_x[k])
    up1.step(0)
    up0.step(0)
    down1.step(0)
    small.step(0)
    wait_recv(vec_z)

    blocks = vec_all[...].reshape(n_dev * 8, LANES)
    shared = spread(blocks, lens[GAIN_ONE], D)
    gain, shift = shared[GAIN_ONE : GAIN_ONE + 1], shared[SHIFT_ONE : SHIFT_ONE + 1]
    bias_q = spread(blocks, lens[BIAS_QV], CW, p.inn * CW)[BIAS_QV : BIAS_QV + 1] * SCALE
    bias_v = spread(blocks, lens[BIAS_QV], CW, D + p.inn * CW)[BIAS_QV : BIAS_QV + 1]
    blank = jnp.zeros((1, HEAD_DIM), F32)

    def beside(row, h):
        return jnp.concatenate([row[:, h * HEAD_DIM : (h + 1) * HEAD_DIM], blank], axis=1)

    def norm(s, first=0, size=rows):
        here = pl.ds(s * rows + first, size)
        normed, _ = norm_parts(tok[s, first : first + size, :].astype(F32))
        h_ref[here, :] = (normed * gain + shift).astype(BF16)
        n_ref[here, :] = normed.astype(BF16)

    def heads(s, first=0, size=rows):
        here = pl.ds(s * rows + first, size)
        place_of = p.slots[s] * rows + first
        end_one = lengths[0, 0]
        end_two = end_one + lengths[0, 1]
        index = lax.broadcasted_iota(jnp.int32, (size, LANES), 0) + place_of
        lane = lax.broadcasted_iota(jnp.int32, (size, LANES), 1) - HEAD_DIM
        item = jnp.where(index >= end_one, 1, 0) + jnp.where(index >= end_two, 1, 0)
        same = jnp.where(lane == item, 1.0, 0.0)
        inside = jnp.logical_and(lane >= 0, lane < 3)
        other = jnp.where(jnp.logical_and(lane != item, inside), NEG, 0.0)
        ones = jnp.where(jnp.logical_and(lane >= 0, lane < 2), 1.0, 0.0)
        qkv = product(h_ref[here, :], w_wide[...])
        for h in range(HP):
            q, k, v = (qkv[:, (t * HP + h) * LANES : (t * HP + h + 1) * LANES] for t in range(3))
            q_ref[h, here, :] = (q + (same + beside(bias_q, h))).astype(BF16)
            k_ref[h, here, :] = (k + other).astype(BF16)
            v_aug = (v + (ones + beside(bias_v, h))).astype(BF16)
            v_ref[h, here, :] = v_aug
            vt_ref[h, :, here] = v_aug.T

    own_tok.wait()
    norm(OWN)
    tok_sib.wait_recv()
    norm(SIB)
    tok_far[0].wait_recv()
    tok_on[0].start()
    norm(FAR, 0, half_rows)
    for copies in wq_x:
        wait_recv(copies)
    down0.step(1)
    if w_qkv.shape[0] % 16 == 0:
        wq_full[...] = wq_all[...].reshape(D, 3 * CW)
    else:
        rows_of = [wq_all[z, x].astype(F32) for z in range(N_Z) for x in range(p.n_x)]
        wq_full[...] = jnp.concatenate(rows_of, axis=0).astype(BF16)
    for i in range(3 * HP):
        value = wq_full[:, i * HEAD_DIM : (i + 1) * HEAD_DIM]
        if i < HP:
            value = value * BF16(SCALE)
        w_wide[:, i * LANES : (i + 1) * LANES] = jnp.concatenate(
            [value, jnp.zeros_like(value)], axis=1
        )
    heads(OWN)
    up1.step(1)
    heads(SIB)
    tok_far[1].wait_recv()
    tok_on[1].start()
    norm(FAR, half_rows, half_rows)
    heads(FAR)
    up0.step(1)
    for i in range(2):
        tok_on[i].wait_recv()
        norm(DIAG, i * half_rows, half_rows)
    heads(DIAG)
    down0.step(2)
    start(saves)

    items = N_IN * HP

    def spill(it, slot):
        h, qb = it % HP, it // HP
        return pltpu.make_async_copy(
            e_ref.at[slot],
            e_out.at[h, :, pl.ds(pl.multiple_of(qb * BQ, BQ), BQ)],
            e_sem.at[slot],
        )

    actions = {
        0: [(down1, 1)],
        1: [(small, 1), (up0, 2), (up1, 2)],
        3: [(down1, 2)],
        4: [(small, 2)],
        7: [(up0, 3)],
        9: [(up1, 3), (up0, 4)],
    }

    def body(it, _):
        slot = it % 2
        h, qb = it % HP, it // HP
        here = pl.ds(pl.multiple_of(qb * BQ, BQ), BQ)

        @pl.when(it >= 2)
        def _():
            spill(it - 2, slot).wait()

        kt_ref[h, :, here] = k_ref[h, here, :].T[0:HEAD_DIM]
        q = q_ref[h, here, :]
        top = None
        for c in range(total // CK):
            cs = slice(c * CK, (c + 1) * CK)
            scores = product_nt(k_ref[h, cs, :], q)
            s_ref[cs, :] = scores
            peak = jnp.max(scores, axis=0, keepdims=True)
            top = peak if top is None else jnp.maximum(top, peak)
        acc = None
        for c in range(total // CK):
            cs = slice(c * CK, (c + 1) * CK)
            expo = jnp.exp(s_ref[cs, :] - top).astype(BF16)
            e_ref[slot, cs, :] = expo
            term = product(vt_ref[h, :, cs], expo)
            acc = term if acc is None else acc + term
        spill(it, slot).start()
        wide = acc.T
        sums = wide[:, HEAD_DIM : HEAD_DIM + 1]
        lane = lax.broadcasted_iota(jnp.int32, wide.shape, 1)
        att_ref[h, here, :] = jnp.where(lane < HEAD_DIM, wide / sums, wide)

        @pl.when(h == HP - 1)
        def _():
            low_ref[qb] = pack(
                jnp.concatenate([att_ref[i, here, 0:HEAD_DIM] for i in range(HP)], axis=1)
            ).astype(BF16)

        for when, acts in actions.items():

            @pl.when(it == when)
            def _():
                for which, number in acts:
                    which.step(number)

        for s in range(N_IN - 1):

            @pl.when(it == s * HP + HP - 1)
            def _():
                swap[s].start()

        return 0

    lax.fori_loop(0, items, body, 0)
    swap_own.start()
    start(late_saves)
    down0.step(3)
    down1.step(3)
    small.step(3)
    up1.step(4)
    down1.step(4)
    down0.step(4)
    small.step(4)
    wait(swap)
    swap_own.wait()
    wait(saves)
    wait(late_saves)
    for it in (items - 2, items - 1):
        spill(it, it % 2).wait()
    for item in pieces:
        item.finish()
    for r in range(3):
        stays, _, away = unit(r)

        @pl.when(jnp.logical_not(stays))
        def _():
            away.wait_send()

    wait_send(tok_far + tok_on + [tok_sib] + vec_i + vec_x + vec_z + wq_z)
    for copies in wq_x:
        wait_send(copies)


def forward(n_dp, tokens, lengths, w_qkv, vectors, w_out, w_up, w_down):
    n_x = n_dp // N_Z
    rows = tokens.shape[0]
    total = N_IN * rows
    lens = tuple(v.shape[0] for v in vectors)
    w_rows = w_qkv.shape[0]
    wide = (HP, total, LANES)

    def whole(shape):
        return jax.ShapeDtypeStruct((N_IN, N_Z, n_x) + shape, BF16)

    out_shape = packed_shape(*w_out.shape)

    n_remote = 5 + 3 + 3 + (1 + N_Z) * (n_x - 1) + 2 * (N_Z - 1) + 3
    n_remote += sum(gather_count(n_x, order) for order in GATHER_ORDERS.values())
    return pl.pallas_call(
        functools.partial(forward_kernel, n_dp, lens),
        out_shape=(
            jax.ShapeDtypeStruct((total, D), BF16),
            jax.ShapeDtypeStruct((total, D), BF16),
            jax.ShapeDtypeStruct(wide, BF16),
            jax.ShapeDtypeStruct(wide, BF16),
            jax.ShapeDtypeStruct((HP, HEAD_DIM, total), BF16),
            jax.ShapeDtypeStruct(wide, F32),
            jax.ShapeDtypeStruct((HP, total, total), BF16),
            jax.ShapeDtypeStruct((N_IN,) + packed_shape(rows, CW), BF16),
            whole(out_shape),
            whole(w_up.shape),
            whole(w_down.shape),
            jax.ShapeDtypeStruct((N_Z, n_x, N_IN, 8, LANES), F32),
            jax.ShapeDtypeStruct((D, 3 * CW), BF16),
        ),
        in_specs=[ANY, SMEM, VMEM] + [VMEM] * 8 + [VMEM, ANY, VMEM],
        out_specs=(ANY,) * 11 + (VMEM,) * 2,
        scratch_shapes=[
            pltpu.VMEM((N_IN, rows, D), BF16),
            pltpu.VMEM((total, D), BF16),
            pltpu.VMEM((total, D), BF16),
            pltpu.VMEM(wide, BF16),
            pltpu.VMEM(wide, BF16),
            pltpu.VMEM((HP, HEAD_DIM, total), BF16),
            pltpu.VMEM(wide, F32),
            pltpu.VMEM(wide, BF16),
            pltpu.VMEM((HP, LANES, total), BF16),
            pltpu.VMEM((total, BQ), F32),
            pltpu.VMEM((2, total, BQ), BF16),
            pltpu.VMEM((N_IN,) + packed_shape(rows, CW), BF16),
            pltpu.VMEM((3, w_rows, CW), BF16),
            pltpu.VMEM((3, w_rows, CW), BF16),
            pltpu.VMEM((D, 3 * HP * LANES), BF16),
            pltpu.VMEM((N_Z, n_x, w_rows, 3 * CW), BF16),
            pltpu.VMEM((8, LANES), F32),
            pltpu.VMEM(out_shape, BF16),
            pltpu.SemaphoreType.DMA((2,)),
        ]
        + sem_shapes(n_remote, 13),
        compiler_params=params(0),
        name="forward",
    )(tokens, lengths, w_qkv, *[v.reshape(1, -1) for v in vectors], w_out, w_up, w_down)


GC = 384


def add_rows(total, terms, out=None):
    step = 128

    def one(i, _):
        at = pl.ds(pl.multiple_of(i * step, step), step)
        if out is None:
            value = total[at, :]
            for term in terms:
                value = value + term[at, :]
            total[at, :] = value
        else:
            value = total[at, :].astype(F32)
            for term in terms:
                value = value + term[at, :].astype(F32)
            out[at, :] = value
        return 0

    lax.fori_loop(0, total.shape[0] // step, one, 0)


def add_blocks(total, term):
    if len(total.shape) == 2:
        add_rows(total, [term])
        return

    def one(i, _):
        total[i] = total[i] + term[i]
        return 0

    lax.fori_loop(0, total.shape[0], one, 0)


def unpack_into(out, parts, rows):
    half = rows // 2
    packed = parts.shape[-1] == 2 * CW

    def one(d, _):
        for i in range(N_IN):
            cols = slice(i * CW, (i + 1) * CW)
            if packed:
                first = pl.ds(pl.multiple_of(d * rows, 16), half)
                second = pl.ds(pl.multiple_of(d * rows + half, 16), half)
                out[first, cols] = parts[i, d, :, 0:CW]
                out[second, cols] = parts[i, d, :, CW : 2 * CW]
            else:
                at = pl.ds(pl.multiple_of(d * LANES, LANES), LANES)
                out[at, cols] = parts[i, at, :]
        return 0

    lax.fori_loop(0, out.shape[0] // (rows if packed else LANES), one, 0)


def pack_into(parts, value, rows, first):
    for i in range(N_IN):
        cols = slice(i * CW, (i + 1) * CW)
        if parts.shape[-1] == 2 * CW:
            for b in range(value.shape[0] // rows):
                parts[i, first + b] = pack(value[b * rows : (b + 1) * rows, cols])
        else:
            parts[i] = value[:, cols]


def middle_kernel(
    n_dp,
    lens,
    tokens,
    mixed,
    a_out,
    a_up,
    a_down,
    vec_all,
    cotangent,
    output,
    d_res_out,
    seen,
    t_out,
    t_up,
    t_down,
    sums,
    sum_up,
    tok,
    mix,
    po,
    pu,
    pd,
    cot,
    fo,
    fd,
    att,
    res,
    n_two,
    h_two,
    act,
    d_up,
    b_up,
    d_mixed,
    d_res,
    out_ref,
    d_att,
    co,
    cu,
    cd,
    h_turned,
    cot_turned,
    send,
    recv,
    local,
):
    p = Place(n_dp)
    n_dev = n_dp * N_IN
    sems = Sems(send, recv, local)
    rows = tokens.shape[0]
    ff = a_up.shape[0] * a_up.shape[2]
    r_out, r_down = D // n_dp, a_down.shape[3]
    loads = {
        name: sems.copy(src, dst)
        for name, src, dst in (
            ("out", a_out, po),
            ("mix", mixed, mix),
            ("tok", tokens, tok),
            ("up", a_up, pu),
            ("cot", cotangent, cot),
            ("down", a_down, pd),
        )
    }
    for load in loads.values():
        load.start()
    swap = [
        sems.remote(d_att.at[p.slots[s]], seen.at[s], (p.dp, p.slots[s])) for s in (DIAG, FAR, SIB)
    ]
    swap_own = sems.copy(d_att.at[p.inn], seen.at[OWN])

    def across(parts, buffer):
        return [
            sems.remote(parts.at[2 * yy + 1 - p.c], buffer.at[yy], (p.dp, p.sib))
            for yy in range(2)
        ]

    core_up, core_down, core_out = across(pu, cu), across(pd, cd), across(po, co)
    keeps = {
        name: [sems.copy(parts.at[2 * yy + p.c], out.at[yy]) for yy in range(2)]
        for name, parts, out in (("up", pu, t_up), ("down", pd, t_down), ("out", po, t_out))
    }
    out_save = sems.copy(out_ref, output)
    res_save = sems.copy(d_res, d_res_out)

    near = partners(p, "yc", diagonal=True)
    arrive(near)
    blocks = vec_all[...].reshape(n_dev * 8, LANES)
    shared = spread(blocks, lens[BIAS_OUT], D)
    for c in range(ff // D):
        b_up[:, c * D : (c + 1) * D] = spread(blocks, lens[BIAS_UP], D, c * D)[
            BIAS_UP : BIAS_UP + 1
        ]

    loads["out"].wait()
    loads["mix"].wait()
    unpack_into(fo, po, r_out)
    half = rows // 2
    for i in range(N_IN):
        cols = slice(i * CW, (i + 1) * CW)
        att[0:half, cols] = mix[i, :, 0:CW]
        att[half:rows, cols] = mix[i, :, CW : 2 * CW]
    loads["tok"].wait()
    residual = (
        tok[...].astype(F32) + product(att[...], fo[...]) + shared[BIAS_OUT : BIAS_OUT + 1]
    )
    res[...] = residual
    normed, factor = norm_parts(residual)
    n_two[...] = normed
    gain = shared[GAIN_TWO : GAIN_TWO + 1]
    h_two[...] = (normed * gain + shared[SHIFT_TWO : SHIFT_TWO + 1]).astype(BF16)
    loads["down"].wait()
    for i in range(N_IN):
        for d in range(n_dp):
            fd[i * CW : (i + 1) * CW, d * r_down : (d + 1) * r_down] = pd[i, d]
    loads["up"].wait()
    loads["cot"].wait()

    def hidden(it, _):
        hid = pl.ds(pl.multiple_of(it * HC, HC), HC)
        inside = pl.ds(pl.multiple_of(it % (D // HC) * HC, HC), HC)
        up = product(h_two[...], pu[it // (D // HC), :, inside]) + b_up[:, hid]
        d_act = product(cot[...], fd[:, hid])
        cdf = 0.5 * (1.0 + lax.erf(up * 0.7071067811865476))
        pdf = jnp.exp(-0.5 * up * up) * 0.3989422804014327
        act[:, hid] = (up * cdf).astype(BF16)
        grad = (d_act * (cdf + up * pdf)).astype(BF16)
        d_up[:, hid] = grad
        sum_up[:, hid] = jnp.sum(grad.astype(F32), axis=0, keepdims=True)
        return 0

    lax.fori_loop(0, ff // HC, hidden, 0)

    dh_two = None
    for i in range(N_IN):
        term = product_nt(d_up[:, i * D : (i + 1) * D], pu[i])
        dh_two = term if dh_two is None else dh_two + term
    normed = n_two[...]
    upstream = cot[...].astype(F32)
    value = upstream + norm_backward(dh_two, normed, factor, gain)
    d_res[...] = value
    res_save.start()
    low = value.astype(BF16)
    d_mixed[...] = low
    grad_att = product_nt(low, fo[...]).astype(BF16)
    for i in range(N_IN):
        d_att[i] = pack(grad_att[:, i * CW : (i + 1) * CW])
    all_in(near)
    start(swap)
    swap_own.start()

    def grad_up(i):
        cols = pl.ds(pl.multiple_of(i * D, D), D)
        pu[i] = product(h_turned[...], d_up[:, cols]).astype(BF16)

    h_turned[...] = h_two[...].T
    cot_turned[...] = cot[...].T
    for yy in range(2):
        grad_up(2 * yy + 1 - p.c)
    start(core_up)

    def grad_down(it, _):
        hid = pl.ds(pl.multiple_of(it * GC, GC), GC)
        value = product(cot_turned[...], act[:, hid]).astype(BF16)
        for i in range(N_IN):
            for b in range(GC // r_down):
                cols = slice(b * r_down, (b + 1) * r_down)
                pd[i, it * (GC // r_down) + b] = value[i * CW : (i + 1) * CW, cols]
        return 0

    lax.fori_loop(0, ff // GC, grad_down, 0)
    start(core_down)
    pack_into(po, product_tn(att[...], d_mixed[...]).astype(BF16), r_out, 0)
    start(core_out)
    for yy in range(2):
        grad_up(2 * yy + p.c)

    def output_part(n, _):
        cols = pl.ds(pl.multiple_of(n * HC, HC), HC)
        value = product_nt(act[...], fd[cols, :]) + res[:, cols]
        out_ref[:, cols] = value.astype(BF16)
        return 0

    res[...] = res[...] + shared[BIAS_DOWN : BIAS_DOWN + 1]
    lax.fori_loop(0, D // HC, output_part, 0)
    out_save.start()

    sums[...] = jnp.zeros_like(sums)
    sums[BIAS_OUT : BIAS_OUT + 1, :] = jnp.sum(low.astype(F32), axis=0, keepdims=True)
    sums[BIAS_DOWN : BIAS_DOWN + 1, :] = jnp.sum(upstream, axis=0, keepdims=True)
    sums[GAIN_TWO : GAIN_TWO + 1, :] = jnp.sum(dh_two * normed, axis=0, keepdims=True)
    sums[SHIFT_TWO : SHIFT_TWO + 1, :] = jnp.sum(dh_two, axis=0, keepdims=True)
    for copies, parts, buffer, name in (
        (core_up, pu, cu, "up"),
        (core_down, pd, cd, "down"),
        (core_out, po, co, "out"),
    ):
        wait_recv(copies)
        for yy in range(2):
            add_blocks(parts.at[2 * yy + p.c], buffer.at[yy])
        start(keeps[name])
    wait(swap)
    swap_own.wait()
    for copies in (core_up, core_down, core_out):
        wait_send(copies)
    for copies in keeps.values():
        wait(copies)
    out_save.wait()
    res_save.wait()


def middle(n_dp, lens, tokens, mixed, a_out, a_up, a_down, vec_all, cotangent):
    rows = tokens.shape[0]
    ff = a_up.shape[0] * a_up.shape[2]
    out_parts, up_parts, down_parts = a_out.shape[1:], a_up.shape[1:], a_down.shape[1:]
    return pl.pallas_call(
        functools.partial(middle_kernel, n_dp, lens),
        out_shape=(
            jax.ShapeDtypeStruct((rows, D), BF16),
            jax.ShapeDtypeStruct((rows, D), F32),
            jax.ShapeDtypeStruct((N_IN,) + packed_shape(rows, CW), BF16),
            jax.ShapeDtypeStruct((2,) + out_parts, BF16),
            jax.ShapeDtypeStruct((2,) + up_parts, BF16),
            jax.ShapeDtypeStruct((2,) + down_parts, BF16),
            jax.ShapeDtypeStruct((8, D), F32),
            jax.ShapeDtypeStruct((1, ff), F32),
        ),
        in_specs=[ANY] * 5 + [VMEM, ANY],
        out_specs=(ANY,) * 6 + (VMEM,) * 2,
        scratch_shapes=[
            pltpu.VMEM((rows, D), BF16),
            pltpu.VMEM((N_IN,) + packed_shape(rows, CW), BF16),
            pltpu.VMEM((N_IN,) + out_parts, BF16),
            pltpu.VMEM((N_IN,) + up_parts, BF16),
            pltpu.VMEM((N_IN,) + down_parts, BF16),
            pltpu.VMEM((rows, D), BF16),
            pltpu.VMEM((D, D), BF16),
            pltpu.VMEM((D, ff), BF16),
            pltpu.VMEM((rows, D), BF16),
            pltpu.VMEM((rows, D), F32),
            pltpu.VMEM((rows, D), F32),
            pltpu.VMEM((rows, D), BF16),
            pltpu.VMEM((rows, ff), BF16),
            pltpu.VMEM((rows, ff), BF16),
            pltpu.VMEM((1, ff), F32),
            pltpu.VMEM((rows, D), BF16),
            pltpu.VMEM((rows, D), F32),
            pltpu.VMEM((rows, D), BF16),
            pltpu.VMEM((N_IN,) + packed_shape(rows, CW), BF16),
            pltpu.VMEM((2,) + out_parts, BF16),
            pltpu.VMEM((2,) + up_parts, BF16),
            pltpu.VMEM((2,) + down_parts, BF16),
            pltpu.VMEM((D, rows), BF16),
            pltpu.VMEM((D, rows), BF16),
        ]
        + sem_shapes(9, 15),
        compiler_params=params(1),
        name="middle",
    )(tokens, mixed, a_out, a_up, a_down, vec_all, cotangent)


BK = 640
CQ = 1280
SCATTER_ORDERS = ("yxz", "xyz", "yxz", "xyz", "zyx")


class Scatter:
    def __init__(self, place, sems, blocks, order, buffers, out):
        self.order, self.out = order, out
        p = place
        self.total, self.buffers = buffers[0], dict(zip(order, buffers[1:]))
        self.load = sems.copy(blocks, self.total)
        _, _, n_x, _, _ = self.total.shape
        where = {"y": pl.ds(0, 2), "z": pl.ds(0, N_Z), "x": pl.ds(0, n_x)}
        own = {"y": p.y, "z": p.z, "x": p.x}
        self.copies, self.regions = {}, {}
        for axis in order:
            copies = []
            for at, device, k in p.peers(axis):
                there = dict(where)
                there[axis] = pl.ds(at, 1)
                src = self.total.at[there["y"], there["z"], there["x"]]
                copies.append(sems.remote(src, self.buffers[axis].at[k - 1], device))
            self.copies[axis] = copies
            where[axis] = pl.ds(own[axis], 1)
            self.regions[axis] = (where["y"], where["z"], where["x"])

    def step(self, number):
        if number == 0:
            self.load.start()
            return
        if number == 1:
            self.load.wait()
        else:
            axis = self.order[number - 2]
            wait_recv(self.copies[axis])
            region, buffer = self.total.at[self.regions[axis]], self.buffers[axis]
            if number - 1 == len(self.order):
                value = region[0, 0, 0].astype(F32)
                for k in range(buffer.shape[0]):
                    value = value + buffer[k, 0, 0, 0].astype(F32)
                self.out(value)
                return
            _, n_y, n_z, n_x, _, _ = buffer.shape

            def one(i, _):
                for y in range(n_y):
                    for x in range(n_x):
                        value = region[y, i, x]
                        for k in range(buffer.shape[0]):
                            value = value + buffer[k, y, i, x]
                        region[y, i, x] = value
                return 0

            lax.fori_loop(0, n_z, one, 0)
        start(self.copies[self.order[number - 1]])

    def finish(self):
        for axis in self.order:
            wait_send(self.copies[axis])


def scatter_buffers(n_x, rows, cols, order):
    sizes = {"y": 2, "z": N_Z, "x": n_x}
    shapes = [(2, N_Z, n_x, rows, cols)]
    left = dict(sizes)
    for axis in order:
        left[axis] = 1
        shapes.append((sizes[axis] - 1, left["y"], left["z"], left["x"], rows, cols))
    return [pltpu.VMEM(shape, BF16) for shape in shapes]


def scatter_count(n_x):
    return 1 + (N_Z - 1) + (n_x - 1)


def backward_kernel(n_dp, lens, *rest):
    (
        tokens,
        seen_in,
        att_in,
        e_all,
        q_in,
        v_in,
        kt_in,
        h_in,
        n_in,
        wq_in,
        d_res_in,
        t_out,
        t_up,
        t_down,
        vec_all,
        sums,
        sum_up,
    ) = rest[:17]
    grad_tokens, g_qkv, s_out, s_up, s_down = rest[17:22]
    vec_outs = rest[22:30]
    (
        seen,
        att,
        q_ref,
        v_ref,
        kt_ref,
        h_ref,
        n_ref,
        wq_ref,
        d_res,
        do_ref,
        dqt_ref,
        e_ref,
        d_all,
        t_core,
        t_far,
        g_w,
        norm_sums,
        w_own,
        w_x,
        w_z,
        w_mine,
        w_sum,
        v_own,
        v_x,
        v_z,
        v_y,
        v_c,
    ) = rest[30:57]
    buffers = rest[57:77]
    e_sem, send, recv, local = rest[77:]
    p = Place(n_dp)
    n_dev, n_x = n_dp * N_IN, n_dp // N_Z
    sems = Sems(send, recv, local)
    rows = tokens.shape[0]
    total = N_IN * rows
    n_down = t_down.shape[3]
    half_down = first_rows(n_down)
    half_up = t_up.shape[4] // 2

    def put(out, first):
        def write(value):
            size, cols = value.shape
            if cols == 2 * CW and out.shape[1] == CW:
                out[0:size, :] = value[:, 0:CW]
                out[size:, :] = value[:, CW:]
            elif cols == out.shape[1]:
                out[first : first + size, :] = value
            else:
                out[:, first : first + cols] = value

        return write

    near = partners(p, "zxyc", diagonal=True)
    arrive(near)
    loads = {
        name: sems.copy(src, dst)
        for name, src, dst in (
            ("seen", seen_in, seen),
            ("att", att_in, att),
            ("v", v_in, v_ref),
            ("kt", kt_in, kt_ref),
            ("q", q_in, q_ref),
            ("wq", wq_in, wq_ref),
            ("res", d_res_in, d_res),
        )
    }
    for name in ("seen", "att"):
        loads[name].start()
    pieces = []
    for number, (ref, out, first, size, axis) in enumerate(
        (
            (t_down, s_down, 0, half_down, 0),
            (t_down, s_down, half_down, n_down - half_down, 0),
            (t_up, s_up, 0, half_up, 1),
            (t_up, s_up, half_up, half_up, 1),
            (t_out, s_out, 0, t_out.shape[3], 0),
        )
    ):
        pieces.append(
            Scatter(
                p,
                sems,
                part(ref, first, size, axis),
                SCATTER_ORDERS[number],
                buffers[4 * number : 4 * number + 4],
                put(out, first),
            )
        )
    down0, down1, up0, up1, small = pieces
    for item in (down0, down1, small, up0, up1):
        item.step(0)
    for name in ("v", "kt", "q", "wq", "res"):
        loads[name].start()

    def room(i):
        return e_ref.at[i, :, pl.ds(0, D)]

    dh_far, dh_diag, dh_sib, dh_own = room(2), room(3), room(0), room(1)
    tok = n_ref.at[0]
    loads["tok"] = sems.copy(tokens, tok)

    def fetch(kb, h, half, slot):
        at = pl.ds(pl.multiple_of(kb * BK, BK), BK)
        src = e_all.at[h, at, pl.ds(half * CQ, CQ)]
        return pltpu.make_async_copy(src, e_ref.at[slot], e_sem.at[slot])

    fetch(0, 0, 0, 0).start()
    fetch(0, 0, 1, 1).start()
    feeds = []
    for s in range(N_IN):
        at = pl.ds(s * rows, rows)
        feeds.append(
            [sems.copy(n_in.at[at], n_ref.at[s % 2]), sems.copy(h_in.at[at], h_ref.at[s % 2])]
        )
    for feed in feeds[0:2]:
        start(feed)
    here, there = (p.dp, p.sib), (p.dp, p.far)
    give_diag = sems.remote(dh_diag, t_core.at[1], here)
    give_sib = sems.remote(dh_sib, t_core.at[0], here)
    across = sems.remote(dh_far, t_far, there)
    w_order = tuple(range(1, N_Z)) + (0,)
    w_to_x = {}
    for kz in w_order:
        w_to_x[kz] = [
            sems.remote(w_own.at[(p.z + kz) % N_Z, at], w_x.at[k - 1, kz], device)
            for at, device, k in p.peers("x")
        ]
    w_to_z = [
        sems.remote(w_own.at[at, p.x], w_z.at[k - 1], device) for at, device, k in p.peers("z")
    ]
    v_to_x = [
        sems.remote(v_own.at[:, at], v_x.at[k - 1], device) for at, device, k in p.peers("x")
    ]
    v_to_z = [
        sems.remote(v_own.at[at, p.x], v_z.at[k - 1], device) for at, device, k in p.peers("z")
    ]
    v_to_y = sems.remote(v_own.at[p.z, p.x, pl.ds((1 - p.y) * 2, 2)], v_y, there)
    v_to_c = sems.remote(v_own.at[p.z, p.x, p.sib], v_c, here)
    unit_base = sems.n

    def unit(t):
        u = p.inn + N_IN * t
        owner, r = u // 3, u % 3
        away = pltpu.make_async_remote_copy(
            src_ref=w_mine.at[t],
            dst_ref=w_sum.at[r],
            send_sem=send.at[unit_base + t],
            recv_sem=recv.at[unit_base + r],
            device_id=(p.dp, owner),
            device_id_type=MESH,
        )
        return owner == p.inn, r, away

    def arrival(r):
        u = 3 * p.inn + r
        bring = pltpu.make_async_remote_copy(
            src_ref=w_mine.at[0],
            dst_ref=w_sum.at[r],
            send_sem=send.at[unit_base],
            recv_sem=recv.at[unit_base + r],
            device_id=(p.dp, p.far),
            device_id_type=MESH,
        )
        return u % N_IN == p.inn, bring

    all_in(near)
    for item in (down0, down1, small, up0, up1):
        item.step(1)
    dqt_ref[...] = jnp.zeros_like(dqt_ref)
    loads["seen"].wait()
    loads["att"].wait()
    for s in range(N_IN):
        at = pl.ds(s * rows, rows)
        for h in range(HP):
            grad = jnp.concatenate(
                [
                    seen[s, :, side * CW + h * HEAD_DIM : side * CW + (h + 1) * HEAD_DIM]
                    for side in range(2)
                ],
                axis=0,
            ).astype(F32)
            both = att[h, at, :]
            scale = SCALE / both[:, HEAD_DIM : HEAD_DIM + 1]
            delta = jnp.sum(grad * both[:, 0:HEAD_DIM], axis=-1, keepdims=True) * -scale
            high = delta.astype(BF16).astype(F32)
            lane = lax.broadcasted_iota(jnp.int32, (rows, HEAD_DIM), 1)
            tail = jnp.where(lane == 0, high, jnp.where(lane == 1, delta - high, 0.0))
            do_ref[h, at, :] = jnp.concatenate([grad * scale, tail], axis=1).astype(BF16)
    for name in ("v", "kt", "q"):
        loads[name].wait()

    actions = {
        3: [(small, 2), (down0, 2), (down1, 2)],
        8: [(small, 3), (up0, 2), (up1, 2)],
        10: [(down0, 3), (down1, 3), (small, 4)],
        12: [(up0, 3), (up1, 3)],
        14: [(down0, 4), (down1, 4)],
    }
    last = N_IN - 1
    root = HEAD_DIM**0.5

    def act(kb, first, number):
        for when, acts in actions.items():
            if when in (number, number + HP):

                @pl.when(kb == first + (when - number) // HP)
                def _():
                    for which, stage in acts:
                        which.step(stage)

    def piece(kb, h, half, slot):
        at = pl.ds(pl.multiple_of(kb * BK, BK), BK)
        cs = slice(half * CQ, (half + 1) * CQ)
        expo, do = e_ref[slot], do_ref[h, cs, :]
        ds = (expo.astype(F32) * product_nt(v_ref[h, at, :], do)).astype(BF16)
        dv, dk = product(expo, do), product(ds, q_ref[h, cs, :])
        dqt_ref[h, :, cs] += product(kt_ref[h, :, at], ds)
        return dv, dk

    def finish_keys(kb, h, dv, dk):
        at = pl.ds(pl.multiple_of(kb * BK, BK), BK)
        cols = slice(h * HEAD_DIM, (h + 1) * HEAD_DIM)
        d_all[1, at, cols] = (dk * root).astype(BF16)
        d_all[2, at, cols] = (dv * root).astype(BF16)

    def both_halves(kb, _):
        for h in range(HP):
            slot = (kb * HP + h) % 2 * 2
            other = 2 - slot
            if h < HP - 1:
                for half in range(2):
                    fetch(kb, h + 1, half, other + half).start()
            else:

                @pl.when(kb == 0)
                def _():
                    for half in range(2):
                        fetch(1, 0, half, other + half).start()

                @pl.when(kb == 1)
                def _():
                    fetch(2, 0, 0, 0).start()

            for half in range(2):
                fetch(kb, h, half, slot + half).wait()
            dv0, dk0 = piece(kb, h, 0, slot)
            dv1, dk1 = piece(kb, h, 1, slot + 1)
            dv, dk = dv0 + dv1, dk0 + dk1
            finish_keys(kb, h, dv[:, 0:HEAD_DIM], dk[:, 0:HEAD_DIM])
            act(kb, 0, h)
        return 0

    lax.fori_loop(0, 2, both_halves, 0)

    def one_half(half, first):
        def run(kb, _):
            for h in range(HP):
                slot = ((kb - 2) * HP + h) % 2
                other = 1 - slot
                if h < HP - 1:
                    fetch(kb, h + 1, half, other).start()
                else:

                    @pl.when(kb == 2)
                    def _():
                        fetch(3, 0, half, other).start()

                    if half == 0:

                        @pl.when(kb == last)
                        def _():
                            fetch(2, 0, 1, other).start()

                fetch(kb, h, half, slot).wait()
                dv, dk = piece(kb, h, half, slot)
                at = pl.ds(pl.multiple_of(kb * BK, BK), BK)
                if half == 0:
                    att[h, at, :] = jnp.concatenate([dk[:, 0:HEAD_DIM], dv[:, 0:HEAD_DIM]], axis=1)
                else:
                    dk = dk[:, 0:HEAD_DIM] + att[h, at, 0:HEAD_DIM]
                    dv = dv[:, 0:HEAD_DIM] + att[h, at, HEAD_DIM:LANES]
                    finish_keys(kb, h, dv, dk)
                act(kb, 2, first + h)
            return 0

        lax.fori_loop(2, N_IN, run, 0)
        for h in range(HP):
            cs = slice(half * CQ, (half + 1) * CQ)
            d_all[0, cs, h * HEAD_DIM : (h + 1) * HEAD_DIM] = dqt_ref[h, :, cs].T.astype(BF16)

    def input_grad(i):
        at = pl.ds(i * rows, rows)
        feeds[i][0].wait()
        value = None
        for t in range(3):
            term = product_nt(d_all[t, at, :], wq_ref[:, t * CW : (t + 1) * CW])
            value = term if value is None else value + term
        gain_sum = jnp.sum(value * n_ref[i % 2].astype(F32), axis=0, keepdims=True)
        shift_sum = jnp.sum(value, axis=0, keepdims=True)
        return value.astype(BF16), gain_sum, shift_sum

    def weight_grad(i):
        at = pl.ds(i * rows, rows)
        feeds[i][1].wait()
        return [product_tn(h_ref[i % 2], d_all[t, at, :]) for t in range(3)]

    one_half(0, 2 * HP)
    loads["wq"].wait()
    value, gain_sum, shift_sum = input_grad(DIAG)
    dh_diag[...] = value
    give_diag.start()
    value, g_sum, s_sum = input_grad(FAR)
    dh_far[...] = value
    norm_sums[0:1, :] = gain_sum + g_sum
    norm_sums[1:2, :] = shift_sum + s_sum
    for t, (one, two) in enumerate(zip(weight_grad(DIAG), weight_grad(FAR))):
        g_w[t] = one + two
    for feed in feeds[2:4]:
        start(feed)
    give_diag.wait_recv()
    add_rows(dh_far, [t_core.at[1]])
    across.start()
    one_half(1, 4 * HP)
    wide = [one + two for one, two in zip(weight_grad(SIB), weight_grad(OWN))]
    wide = jnp.concatenate([value + g_w[t] for t, value in enumerate(wide)], axis=1)
    w_rows = D // n_dp
    if w_rows % 16 == 0:
        w_own[...] = wide.astype(BF16).reshape(N_Z, n_x, w_rows, 3 * CW)
    else:
        w_own[...] = wide.reshape(N_Z, n_x, w_rows, 3 * CW).astype(BF16)
    for kz in w_order:
        start(w_to_x[kz])
    value, gain_sum, shift_sum = input_grad(SIB)
    dh_sib[...] = value
    give_sib.start()
    loads["tok"].start()
    value, g_sum, s_sum = input_grad(OWN)
    dh_own[...] = value
    gain_sum = gain_sum + g_sum + norm_sums[0:1, :]
    shift_sum = shift_sum + s_sum + norm_sums[1:2, :]

    row = lax.broadcasted_iota(jnp.int32, (8, D), 0)
    wide = sums[...]
    wide = wide + jnp.where(row == GAIN_ONE, gain_sum, 0.0)
    wide = wide + jnp.where(row == SHIFT_ONE, shift_sum, 0.0)
    packed = unspread(wide, n_dev, lens[GAIN_ONE])
    row = lax.broadcasted_iota(jnp.int32, (8, CW), 0)
    for t, first in ((0, 0), (2, D)):
        line = jnp.sum(d_all[t].astype(F32), axis=0, keepdims=True)
        line = jnp.where(row == BIAS_QV, line, 0.0)
        packed = packed + unspread(line, n_dev, lens[BIAS_QV], first + p.inn * CW)
    row = lax.broadcasted_iota(jnp.int32, (8, D), 0)
    for c in range(sum_up.shape[1] // D):
        line = jnp.where(row == BIAS_UP, sum_up[:, c * D : (c + 1) * D], 0.0)
        packed = packed + unspread(line, n_dev, lens[BIAS_UP], c * D)
    v_own[...] = packed.reshape(N_Z, n_x, N_IN, 8, LANES)
    start(v_to_x)

    for kz in w_order:
        wait_recv(w_to_x[kz])
        at = (p.z + kz) % N_Z
        value = w_own[at, p.x]
        for k in range(n_x - 1):
            value = value + w_x[k, kz]
        w_own[at, p.x] = value
        if kz:
            w_to_z[kz - 1].start()
    wait_recv(v_to_x)
    for k in range(n_x - 1):
        v_own[:, p.x] = v_own[:, p.x] + v_x[k]
    start(v_to_z)
    up0.step(4)
    up1.step(4)
    give_sib.wait_recv()
    add_rows(dh_own, [t_core.at[0]])
    wait_recv(v_to_z)
    for k in range(N_Z - 1):
        v_own[p.z, p.x] = v_own[p.z, p.x] + v_z[k]
    v_to_y.start()
    wide = w_own[p.z, p.x].astype(F32)
    for k in range(N_Z - 1):
        w_to_z[k].wait_recv()
        wide = wide + w_z[k].astype(F32)
    for t in range(3):
        value = wide[:, t * CW : (t + 1) * CW]
        w_mine[t] = value
        stays, r, away = unit(t)

        @pl.when(jnp.logical_not(stays))
        def _():
            away.start()

        @pl.when(stays)
        def _():
            w_sum[r] = value

    v_to_y.wait_recv()
    mine = pl.ds(p.y * 2, 2)
    v_own[p.z, p.x, mine] = v_own[p.z, p.x, mine] + v_y[...]
    v_to_c.start()
    blocks = vec_all[...].reshape(n_dev * 8, LANES)
    gain = spread(blocks, lens[GAIN_ONE], D)[GAIN_ONE : GAIN_ONE + 1]
    loads["tok"].wait()
    loads["res"].wait()
    normed, factor = norm_parts(tok[...].astype(F32))
    v_to_c.wait_recv()
    final = v_own[p.z, p.x, p.inn] + v_c[...]
    for r, length in enumerate(lens):
        vec_outs[r][...] = final[r : r + 1, 0:length]
    for r in range(3):
        stays, bring = arrival(r)

        @pl.when(jnp.logical_not(stays))
        def _():
            bring.wait_recv()

        g_qkv[:, r * CW : (r + 1) * CW] = w_sum[r]
    across.wait_recv()
    grad = dh_own[...].astype(F32) + t_far[...].astype(F32)
    grad_tokens[...] = (d_res[...] + norm_backward(grad, normed, factor, gain)).astype(BF16)
    for t in range(3):
        stays, _, away = unit(t)

        @pl.when(jnp.logical_not(stays))
        def _():
            away.wait_send()

    wait_send([give_diag, give_sib, across, v_to_y, v_to_c])
    wait_send(w_to_z + v_to_x + v_to_z)
    for kz in w_order:
        wait_send(w_to_x[kz])
    for item in pieces:
        item.finish()


def backward(n_dp, lens, like_out, like_down, tokens, seen, att, e_all, q, v, kt, h_one, n_one, wq, d_res, *grads):
    t_out, t_up, t_down, vec_all, sums, sum_up = grads
    n_x = n_dp // N_Z
    rows = tokens.shape[0]
    total = N_IN * rows
    w_rows = D // n_dp
    r_down, c_down = t_down.shape[3:]
    r_up, c_up = t_up.shape[3:]
    r_first = first_rows(r_down)
    sizes = [(r_first, c_down), (r_down - r_first, c_down)]
    sizes += [(r_up, c_up // 2)] * 2 + [t_out.shape[3:]]
    scratch = [
        pltpu.VMEM((N_IN,) + packed_shape(rows, CW), BF16),
        pltpu.VMEM((HP, total, LANES), F32),
        pltpu.VMEM((HP, total, LANES), BF16),
        pltpu.VMEM((HP, total, LANES), BF16),
        pltpu.VMEM((HP, HEAD_DIM, total), BF16),
        pltpu.VMEM((2, rows, D), BF16),
        pltpu.VMEM((2, rows, D), BF16),
        pltpu.VMEM((D, 3 * CW), BF16),
        pltpu.VMEM((rows, D), F32),
        pltpu.VMEM((HP, total, LANES), BF16),
        pltpu.VMEM((HP, HEAD_DIM, total), F32),
        pltpu.VMEM((4, BK, CQ), BF16),
        pltpu.VMEM((3, total, CW), BF16),
        pltpu.VMEM((2, rows, D), BF16),
        pltpu.VMEM((rows, D), BF16),
        pltpu.VMEM((3, D, CW), F32),
        pltpu.VMEM((2, D), F32),
        pltpu.VMEM((N_Z, n_x, w_rows, 3 * CW), BF16),
        pltpu.VMEM((n_x - 1, N_Z, w_rows, 3 * CW), BF16),
        pltpu.VMEM((N_Z - 1, w_rows, 3 * CW), BF16),
        pltpu.VMEM((3, w_rows, CW), F32),
        pltpu.VMEM((3, w_rows, CW), F32),
        pltpu.VMEM((N_Z, n_x, N_IN, 8, LANES), F32),
        pltpu.VMEM((n_x - 1, N_Z, N_IN, 8, LANES), F32),
        pltpu.VMEM((N_Z - 1, N_IN, 8, LANES), F32),
        pltpu.VMEM((2, 8, LANES), F32),
        pltpu.VMEM((8, LANES), F32),
    ]
    for (r, c), order in zip(sizes, SCATTER_ORDERS):
        scratch += scatter_buffers(n_x, r, c, order)
    n_remote = 5 * scatter_count(n_x) + 3 + (N_Z + 1) * (n_x - 1) + 2 * (N_Z - 1) + 2 + 3
    return pl.pallas_call(
        functools.partial(backward_kernel, n_dp, lens),
        out_shape=(
            jax.ShapeDtypeStruct((rows, D), BF16),
            jax.ShapeDtypeStruct((w_rows, 3 * CW), F32),
            jax.ShapeDtypeStruct(like_out.shape, F32),
            jax.ShapeDtypeStruct(t_up.shape[3:], F32),
            jax.ShapeDtypeStruct(like_down.shape, F32),
        )
        + tuple(jax.ShapeDtypeStruct((1, length), F32) for length in lens),
        in_specs=[ANY] * 14 + [VMEM] * 3,
        out_specs=(VMEM,) * 13,
        scratch_shapes=scratch + [pltpu.SemaphoreType.DMA((4,))] + sem_shapes(n_remote, 21),
        compiler_params=params(2),
        name="backward",
    )(
        tokens,
        seen,
        att,
        e_all,
        q,
        v,
        kt,
        h_one,
        n_one,
        wq,
        d_res,
        t_out,
        t_up,
        t_down,
        vec_all,
        sums,
        sum_up,
    )


def finish_kernel(n, *rest):
    for source, result in zip(rest[:n], rest[n:]):
        result[...] = source[...]


def finish(*arrays):
    n = len(arrays)
    return pl.pallas_call(
        functools.partial(finish_kernel, n),
        out_shape=tuple(jax.ShapeDtypeStruct(array.shape, array.dtype) for array in arrays),
        in_specs=[VMEM] * n,
        out_specs=(VMEM,) * n,
        compiler_params=pltpu.CompilerParams(vmem_limit_bytes=VMEM_LIMIT),
        name="finish",
    )(*arrays)


def on_device(
    tokens,
    lengths,
    w_qkv,
    bias_qv,
    w_out,
    bias_out,
    w_up,
    bias_up,
    w_down,
    bias_down,
    gain_one,
    shift_one,
    gain_two,
    shift_two,
    cotangent,
):
    n_dp = lax.axis_size("dp")
    n_x = n_dp // N_Z
    vectors = (
        bias_qv,
        bias_out,
        bias_up,
        bias_down,
        gain_one,
        shift_one,
        gain_two,
        shift_two,
    )
    lens = tuple(v.shape[0] for v in vectors)
    h_one, n_one, q, v, kt, att, e_all, mixed, a_out, a_up, a_down, vec_all, wq = forward(
        n_dp, tokens, lengths, w_qkv, vectors, w_out, w_up, w_down.T
    )

    def by_dp(blocks):
        return blocks.reshape((N_IN, n_dp) + blocks.shape[3:])

    output, d_res, seen, t_out, t_up, t_down, sums, sum_up = middle(
        n_dp,
        lens,
        tokens,
        mixed,
        by_dp(a_out) if packs(w_out.shape[0]) else a_out.reshape(N_IN, D, CW),
        a_up.reshape(N_IN, D, -1),
        by_dp(a_down),
        vec_all,
        cotangent,
    )

    def blocks(grads, like):
        return grads.reshape((2, N_Z, n_x) + like.shape[3:])

    grad_tokens, g_qkv, g_out, g_up, g_down, *vecs = backward(
        n_dp,
        lens,
        w_out,
        w_down.T,
        tokens,
        seen,
        att,
        e_all,
        q,
        v,
        kt,
        h_one,
        n_one,
        wq,
        d_res,
        blocks(t_out, a_out),
        blocks(t_up, a_up),
        blocks(t_down, a_down),
        vec_all,
        sums,
        sum_up,
    )
    output, grad_tokens, g_qkv, g_out, g_up, g_down, *vecs = finish(
        output, grad_tokens, g_qkv, g_out, g_up, g_down, *vecs
    )
    vecs = [vec.reshape(-1) for vec in vecs]
    return (
        output,
        grad_tokens,
        g_qkv,
        vecs[BIAS_QV],
        g_out,
        vecs[BIAS_OUT],
        g_up,
        vecs[BIAS_UP],
        g_down.T,
        vecs[BIAS_DOWN],
        vecs[GAIN_ONE],
        vecs[SHIFT_ONE],
        vecs[GAIN_TWO],
        vecs[SHIFT_TWO],
    )


def solution(mesh):
    rows = P(("dp", "inner"), None)
    mat = P("dp", "inner")
    vec = P(("dp", "inner"))
    return jax.shard_map(
        on_device,
        mesh=mesh,
        in_specs=(
            rows,
            P("dp", None),
            mat,
            vec,
            mat,
            vec,
            mat,
            vec,
            mat,
            vec,
            vec,
            vec,
            vec,
            vec,
            rows,
        ),
        out_specs=(rows, rows, mat, vec, mat, vec, mat, vec, mat, vec, vec, vec, vec, vec),
        check_vma=False,
    )
```

```python
import functools

import jax
import jax.numpy as jnp
from jax import lax
from jax.experimental import pallas as pl
from jax.experimental.pallas import tpu as pltpu
from jax.sharding import PartitionSpec as P

D = 768
HEADS = 12
HEAD_DIM = 64
EPS = 1e-06
NEG = -1e30
LANES = 128
HC = 256
N_Z = 4
N_IN = 4
HP = HEADS // N_IN
CW = HP * HEAD_DIM
SCALE = HEAD_DIM**-0.5
MESH = pl.DeviceIdType.MESH
NT = (((1,), (1,)), ((), ()))
TN = (((0,), (0,)), ((), ()))
F32, BF16 = jnp.float32, jnp.bfloat16
ANY = pl.BlockSpec(memory_space=pl.ANY)
VMEM = pl.BlockSpec(memory_space=pltpu.VMEM)
SMEM = pl.BlockSpec(memory_space=pltpu.SMEM)
VMEM_LIMIT = 62 << 20
BIAS_QV, BIAS_OUT, BIAS_UP, BIAS_DOWN, GAIN_ONE, SHIFT_ONE, GAIN_TWO, SHIFT_TWO = range(8)


def product(left, right):
    return jnp.dot(left, right, preferred_element_type=F32)


def product_tn(left, right):
    return lax.dot_general(left, right, TN, preferred_element_type=F32)


def product_nt(left, right):
    return lax.dot_general(left, right, NT, preferred_element_type=F32)


class Place:
    def __init__(self, n_dp):
        self.n_x = n_dp // N_Z
        self.dp = lax.axis_index("dp")
        self.inn = lax.axis_index("inner")
        self.x, self.z = self.dp % self.n_x, self.dp // self.n_x
        self.c, self.y = self.inn % 2, self.inn // 2
        self.sib = self.y * 2 + 1 - self.c
        self.far = (1 - self.y) * 2 + self.c
        self.diag = (1 - self.y) * 2 + 1 - self.c
        self.slots = (self.diag, self.far, self.sib, self.inn)

    def size(self, axis):
        return {"z": N_Z, "x": self.n_x, "y": 2, "c": 2}[axis]

    def peer(self, axis, k):
        if axis == "z":
            at = (self.z + k) % N_Z
            return at, (at * self.n_x + self.x, self.inn)
        if axis == "x":
            at = (self.x + k) % self.n_x
            return at, (self.z * self.n_x + at, self.inn)
        if axis == "y":
            return 1 - self.y, (self.dp, self.far)
        return 1 - self.c, (self.dp, self.sib)

    def peers(self, axis):
        return [self.peer(axis, k) + (k,) for k in range(1, self.size(axis))]


class Sems:
    def __init__(self, send, recv, local):
        self.send, self.recv, self.local = send, recv, local
        self.n = self.m = 0

    def remote(self, src, dst, device):
        i = self.n
        self.n += 1
        return pltpu.make_async_remote_copy(
            src_ref=src,
            dst_ref=dst,
            send_sem=self.send.at[i],
            recv_sem=self.recv.at[i],
            device_id=device,
            device_id_type=MESH,
        )

    def copy(self, src, dst):
        i = self.m
        self.m += 1
        return pltpu.make_async_copy(src, dst, self.local.at[i])


def sem_shapes(n_remote, n_local):
    return [
        pltpu.SemaphoreType.DMA((n_remote,)),
        pltpu.SemaphoreType.DMA((n_remote,)),
        pltpu.SemaphoreType.DMA((n_local,)),
    ]


def partners(place, axes, diagonal=False):
    devices = [device for axis in axes for _, device, _ in place.peers(axis)]
    if diagonal:
        devices.append((place.dp, place.diag))
    return devices


def arrive(devices):
    barrier = pltpu.get_barrier_semaphore()
    for device in devices:
        pl.semaphore_signal(barrier, inc=1, device_id=device, device_id_type=MESH)


def all_in(devices):
    pl.semaphore_wait(pltpu.get_barrier_semaphore(), len(devices))


def start(copies):
    for copy in copies:
        copy.start()


def wait_recv(copies):
    for copy in copies:
        copy.wait_recv()


def wait_send(copies):
    for copy in copies:
        copy.wait_send()


def wait(copies):
    for copy in copies:
        copy.wait()


def params(collective_id, limit=VMEM_LIMIT):
    return pltpu.CompilerParams(
        collective_id=collective_id, has_side_effects=True, vmem_limit_bytes=limit
    )


def part(ref, first, size, axis):
    cut = pl.ds(first, size)
    lead = (slice(None),) * (len(ref.shape) - 2)
    return ref.at[lead + ((cut, slice(None)) if axis == 0 else (slice(None), cut))]


def pack(value):
    half = value.shape[0] // 2
    return jnp.concatenate([value[:half], value[half:]], axis=1)


def packs(rows):
    return rows % 32 == 0


def packed_shape(rows, cols):
    return (rows // 2, 2 * cols) if packs(rows) else (rows, cols)


def first_rows(rows):
    return -(-rows // 32) * 16


DIAG, FAR, SIB, OWN = range(N_IN)


def place_mask(n_dev, length, size, first):
    column = lax.broadcasted_iota(jnp.int32, (n_dev * 8, size), 1) + first
    row = lax.broadcasted_iota(jnp.int32, (n_dev * 8, size), 0)
    begin = (row // 8) * length
    owned = jnp.logical_and(column >= begin, column < begin + length)
    column = lax.broadcasted_iota(jnp.int32, (LANES, size), 1) + first
    lane = lax.broadcasted_iota(jnp.int32, (LANES, size), 0)
    return owned, jnp.where(column % length == lane, 1.0, 0.0).astype(BF16)


def spread(blocks, length, size, first=0):
    n_dev = blocks.shape[0] // 8
    owned, lanes = place_mask(n_dev, length, size, first)
    wide = jnp.where(owned, product(blocks.astype(BF16), lanes), 0.0)
    return jnp.sum(wide.reshape(n_dev, 8, size), axis=0)


def unspread(rows, n_dev, length, first=0):
    size = rows.shape[1]
    if size > HC and n_dev * size > 32 * D:
        cut = size // 3
        parts = [
            unspread(rows[:, at : at + cut], n_dev, length, first + at)
            for at in range(0, size, cut)
        ]
        return parts[0] + parts[1] + parts[2]
    owned, lanes = place_mask(n_dev, length, size, first)
    total = None
    for _ in range(2):
        low = rows.astype(BF16)
        rows = rows - low.astype(F32)
        many = jnp.broadcast_to(low.astype(F32)[None], (n_dev,) + low.shape)
        many = jnp.where(owned, many.reshape(n_dev * 8, low.shape[1]), 0.0).astype(BF16)
        term = product_nt(many, lanes)
        total = term if total is None else total + term
    return total


def norm_parts(value):
    mean = jnp.mean(value, axis=-1, keepdims=True)
    centred = value - mean
    spread_of = jnp.mean(centred * centred, axis=-1, keepdims=True)
    factor = lax.rsqrt(spread_of + EPS)
    return centred * factor, factor


def norm_backward(grad, normed, factor, gain):
    scaled = grad * gain
    inner_mean = jnp.mean(scaled, axis=-1, keepdims=True)
    cross_mean = jnp.mean(scaled * normed, axis=-1, keepdims=True)
    return factor * (scaled - inner_mean - normed * cross_mean)


class Gather:
    def __init__(self, place, sems, source, out, view, order):
        p = place

        def at(inn, z, x):
            return view(out.at[inn, z, x])

        everything = slice(None)
        zs, xs = p.z, p.x
        self.own = sems.copy(source, at(p.inn, zs, xs))
        inns = [p.inn]
        self.stages = []
        for number, axis in enumerate(order):
            copies = []
            for _, device, _ in p.peers(axis):
                for inn in inns:
                    target = at(inn, zs, xs)
                    copies.append(sems.remote(source if number == 0 else target, target, device))
            self.stages.append(copies)
            if axis == "z":
                zs = everything
            elif axis == "x":
                xs = everything
            elif axis == "y":
                inns = [p.inn, p.far]

    def step(self, number):
        if number == 0:
            self.own.start()
        else:
            if number == 1:
                self.own.wait()
            wait_recv(self.stages[number - 1])
        if number < len(self.stages):
            start(self.stages[number])

    def finish(self):
        for copies in self.stages:
            wait_send(copies)


def gather_count(n_x, order):
    count, inns = 0, 1
    for axis in order:
        count += inns * {"z": N_Z - 1, "x": n_x - 1, "y": 1, "c": 1}[axis]
        inns = 2 if axis == "y" else inns
    return count


BQ = 640
CK = 256
GATHER_ORDERS = {"down0": "xyzc", "down1": "zyxc", "up0": "zyxc", "up1": "zxyc", "out": "xyzc"}


def forward_kernel(
    n_dp,
    lens,
    tokens,
    lengths,
    w_qkv,
    *rest,
):
    vec_in, rest = rest[:8], rest[8:]
    (
        w_out,
        w_up,
        w_down,
        h_out,
        n_out,
        q_out,
        v_out,
        kt_out,
        att_out,
        e_out,
        mixed,
        all_out,
        all_up,
        all_down,
        vec_all,
        wq_full,
        tok,
        h_ref,
        n_ref,
        q_ref,
        v_ref,
        kt_ref,
        att_ref,
        k_ref,
        vt_ref,
        s_ref,
        e_ref,
        low_ref,
        units,
        unit_in,
        w_wide,
        wq_all,
        vec_own,
        out_pack,
        e_sem,
        send,
        recv,
        local,
    ) = rest
    p = Place(n_dp)
    n_dev = n_dp * N_IN
    sems = Sems(send, recv, local)
    rows = tokens.shape[0]
    total = N_IN * rows
    n_down = w_down.shape[0]
    half_down = first_rows(n_down)
    half_up = w_up.shape[1] // 2

    def piece(name, ref, out, first, size, axis):
        view = functools.partial(part, first=first, size=size, axis=axis)
        return Gather(p, sems, view(ref), out, view, GATHER_ORDERS[name])

    down0 = piece("down0", w_down, all_down, 0, half_down, 0)
    down1 = piece("down1", w_down, all_down, half_down, n_down - half_down, 0)
    up0 = piece("up0", w_up, all_up, 0, half_up, 1)
    up1 = piece("up1", w_up, all_up, half_up, half_up, 1)
    small = Gather(p, sems, out_pack, all_out, lambda ref: ref, GATHER_ORDERS["out"])
    pieces = [down0, down1, up0, up1, small]

    own_tok = sems.copy(tokens, tok.at[OWN])
    tok_sib = sems.remote(tokens, tok.at[SIB], (p.dp, p.sib))
    half_rows = rows // 2
    halves = [pl.ds(i * half_rows, half_rows) for i in range(2)]
    tok_far = [sems.remote(tokens.at[at], tok.at[FAR, at], (p.dp, p.far)) for at in halves]
    tok_on = [sems.remote(tok.at[FAR, at], tok.at[DIAG, at], (p.dp, p.sib)) for at in halves]
    block = vec_all.at[p.z, p.x, p.inn]
    vec_i = [
        sems.remote(vec_own, block, (p.dp, other)) for other in (p.sib, p.far, p.diag)
    ]
    mine = vec_all.at[p.z, p.x]
    vec_x = [sems.remote(mine, mine, device) for _, device, _ in p.peers("x")]
    column = vec_all.at[p.z]
    vec_z = [sems.remote(column, column, device) for _, device, _ in p.peers("z")]
    unit_base = sems.n
    sems.n += 3

    def unit(r):
        u = 3 * p.inn + r
        away = pltpu.make_async_remote_copy(
            src_ref=units.at[r],
            dst_ref=unit_in.at[u // N_IN],
            send_sem=send.at[unit_base + r],
            recv_sem=recv.at[unit_base + u // N_IN],
            device_id=(p.dp, u % N_IN),
            device_id_type=MESH,
        )
        return u % N_IN == p.inn, u // N_IN, away

    def arrival(t):
        u = p.inn + N_IN * t
        bring = pltpu.make_async_remote_copy(
            src_ref=units.at[0],
            dst_ref=unit_in.at[t],
            send_sem=send.at[unit_base],
            recv_sem=recv.at[unit_base + t],
            device_id=(p.dp, p.far),
            device_id_type=MESH,
        )
        return u // 3 == p.inn, bring

    wq_block = wq_all.at[p.z, p.x]
    wq_z = [sems.remote(wq_block, wq_block, device) for _, device, _ in p.peers("z")]
    wq_x = []
    for k in range(N_Z):
        spot = wq_all.at[(p.z + N_Z - k) % N_Z, p.x]
        wq_x.append([sems.remote(spot, spot, device) for _, device, _ in p.peers("x")])
    swap = [
        sems.remote(low_ref.at[s], mixed.at[p.inn], (p.dp, p.slots[s])) for s in (DIAG, FAR, SIB)
    ]
    swap_own = sems.copy(low_ref.at[OWN], mixed.at[p.inn])
    saves = [
        sems.copy(ref, out)
        for ref, out in (
            (h_ref, h_out),
            (n_ref, n_out),
            (q_ref, q_out),
            (v_ref, v_out),
        )
    ]
    late_saves = [sems.copy(att_ref, att_out), sems.copy(kt_ref, kt_out)]

    near = partners(p, "zxyc", diagonal=True)
    arrive(near)
    own_tok.start()
    vec_own[...] = jnp.zeros_like(vec_own)
    for r, length in enumerate(lens):
        vec_own[r : r + 1, 0:length] = vec_in[r][...].astype(F32)
    for r in range(3):
        units[r] = w_qkv[:, r * CW : (r + 1) * CW]

    all_in(near)
    start(vec_i)
    for r in range(3):
        stays, t, away = unit(r)

        @pl.when(jnp.logical_not(stays))
        def _():
            away.start()

        @pl.when(stays)
        def _():
            unit_in[t] = units[r]

    start(tok_far)
    tok_sib.start()
    vec_all[p.z, p.x, p.inn] = vec_own[...]
    down0.step(0)
    out_pack[...] = pack(w_out[...]) if packs(w_out.shape[0]) else w_out[...]
    small.step(0)
    for t in range(3):
        stays, bring = arrival(t)

        @pl.when(jnp.logical_not(stays))
        def _():
            bring.wait_recv()

        wq_all[p.z, p.x, :, t * CW : (t + 1) * CW] = unit_in[t]
    start(wq_z)
    start(wq_x[0])
    wait_recv(vec_i)
    start(vec_x)
    wait_recv(vec_x)
    start(vec_z)
    for k in range(1, N_Z):
        wq_z[k - 1].wait_recv()
        start(wq_x[k])
    up1.step(0)
    up0.step(0)
    down1.step(0)
    wait_recv(vec_z)

    blocks = vec_all[...].reshape(n_dev * 8, LANES)
    shared = spread(blocks, lens[GAIN_ONE], D)
    gain, shift = shared[GAIN_ONE : GAIN_ONE + 1], shared[SHIFT_ONE : SHIFT_ONE + 1]
    bias_q = spread(blocks, lens[BIAS_QV], CW, p.inn * CW)[BIAS_QV : BIAS_QV + 1] * SCALE
    bias_v = spread(blocks, lens[BIAS_QV], CW, D + p.inn * CW)[BIAS_QV : BIAS_QV + 1]
    blank = jnp.zeros((1, HEAD_DIM), F32)

    def beside(row, h):
        return jnp.concatenate([row[:, h * HEAD_DIM : (h + 1) * HEAD_DIM], blank], axis=1)

    def norm(s, first=0, size=rows):
        here = pl.ds(s * rows + first, size)
        normed, _ = norm_parts(tok[s, first : first + size, :].astype(F32))
        h_ref[here, :] = (normed * gain + shift).astype(BF16)
        n_ref[here, :] = normed.astype(BF16)

    def heads(s, first=0, size=rows):
        here = pl.ds(s * rows + first, size)
        place_of = p.slots[s] * rows + first
        end_one = lengths[0, 0]
        end_two = end_one + lengths[0, 1]
        index = lax.broadcasted_iota(jnp.int32, (size, LANES), 0) + place_of
        lane = lax.broadcasted_iota(jnp.int32, (size, LANES), 1) - HEAD_DIM
        item = jnp.where(index >= end_one, 1, 0) + jnp.where(index >= end_two, 1, 0)
        same = jnp.where(lane == item, 1.0, 0.0)
        inside = jnp.logical_and(lane >= 0, lane < 3)
        other = jnp.where(jnp.logical_and(lane != item, inside), NEG, 0.0)
        ones = jnp.where(jnp.logical_and(lane >= 0, lane < 2), 1.0, 0.0)
        qkv = product(h_ref[here, :], w_wide[...])
        for h in range(HP):
            q, k, v = (qkv[:, (t * HP + h) * LANES : (t * HP + h + 1) * LANES] for t in range(3))
            q_ref[h, here, :] = (q + (same + beside(bias_q, h))).astype(BF16)
            k_ref[h, here, :] = (k + other).astype(BF16)
            v_aug = (v + (ones + beside(bias_v, h))).astype(BF16)
            v_ref[h, here, :] = v_aug
            vt_ref[h, :, here] = v_aug.T

    own_tok.wait()
    norm(OWN)
    tok_sib.wait_recv()
    norm(SIB)
    tok_far[0].wait_recv()
    tok_on[0].start()
    norm(FAR, 0, half_rows)
    for copies in wq_x:
        wait_recv(copies)
    down0.step(1)
    small.step(1)
    if w_qkv.shape[0] % 16 == 0:
        wq_full[...] = wq_all[...].reshape(D, 3 * CW)
    else:
        rows_of = [wq_all[z, x].astype(F32) for z in range(N_Z) for x in range(p.n_x)]
        wq_full[...] = jnp.concatenate(rows_of, axis=0).astype(BF16)
    for i in range(3 * HP):
        value = wq_full[:, i * HEAD_DIM : (i + 1) * HEAD_DIM]
        if i < HP:
            value = value * BF16(SCALE)
        w_wide[:, i * LANES : (i + 1) * LANES] = jnp.concatenate(
            [value, jnp.zeros_like(value)], axis=1
        )
    heads(OWN)
    up1.step(1)
    heads(SIB)
    tok_far[1].wait_recv()
    tok_on[1].start()
    norm(FAR, half_rows, half_rows)
    heads(FAR)
    up0.step(1)
    for i in range(2):
        tok_on[i].wait_recv()
        norm(DIAG, i * half_rows, half_rows)
    heads(DIAG)
    down0.step(2)
    start(saves)

    items = N_IN * HP

    def spill(it, slot):
        h, qb = it % HP, it // HP
        return pltpu.make_async_copy(
            e_ref.at[slot],
            e_out.at[h, :, pl.ds(pl.multiple_of(qb * BQ, BQ), BQ)],
            e_sem.at[slot],
        )

    actions = {
        0: [(down1, 1), (small, 2)],
        1: [(up0, 2), (up1, 2)],
        3: [(down1, 2)],
        7: [(up0, 3)],
        9: [(up1, 3), (up0, 4)],
    }

    def body(it, _):
        slot = it % 2
        h, qb = it % HP, it // HP
        here = pl.ds(pl.multiple_of(qb * BQ, BQ), BQ)

        @pl.when(it >= 2)
        def _():
            spill(it - 2, slot).wait()

        kt_ref[h, :, here] = k_ref[h, here, :].T[0:HEAD_DIM]
        q = q_ref[h, here, :]
        top = None
        for c in range(total // CK):
            cs = slice(c * CK, (c + 1) * CK)
            scores = product_nt(k_ref[h, cs, :], q)
            s_ref[cs, :] = scores
            peak = jnp.max(scores, axis=0, keepdims=True)
            top = peak if top is None else jnp.maximum(top, peak)
        acc = None
        for c in range(total // CK):
            cs = slice(c * CK, (c + 1) * CK)
            expo = jnp.exp(s_ref[cs, :] - top).astype(BF16)
            e_ref[slot, cs, :] = expo
            term = product(vt_ref[h, :, cs], expo)
            acc = term if acc is None else acc + term
        spill(it, slot).start()
        wide = acc.T
        sums = wide[:, HEAD_DIM : HEAD_DIM + 1]
        lane = lax.broadcasted_iota(jnp.int32, wide.shape, 1)
        att_ref[h, here, :] = jnp.where(lane < HEAD_DIM, wide / sums, wide)

        @pl.when(h == HP - 1)
        def _():
            low_ref[qb] = pack(
                jnp.concatenate([att_ref[i, here, 0:HEAD_DIM] for i in range(HP)], axis=1)
            ).astype(BF16)

        for when, acts in actions.items():

            @pl.when(it == when)
            def _():
                for which, number in acts:
                    which.step(number)

        for s in range(N_IN - 1):

            @pl.when(it == s * HP + HP - 1)
            def _():
                swap[s].start()

        return 0

    lax.fori_loop(0, items, body, 0)
    swap_own.start()
    start(late_saves)
    down0.step(3)
    down1.step(3)
    small.step(3)
    up1.step(4)
    down1.step(4)
    down0.step(4)
    small.step(4)
    wait(swap)
    swap_own.wait()
    wait(saves)
    wait(late_saves)
    for it in (items - 2, items - 1):
        spill(it, it % 2).wait()
    for item in pieces:
        item.finish()
    for r in range(3):
        stays, _, away = unit(r)

        @pl.when(jnp.logical_not(stays))
        def _():
            away.wait_send()

    wait_send(tok_far + tok_on + [tok_sib] + vec_i + vec_x + vec_z + wq_z)
    for copies in wq_x:
        wait_send(copies)


def forward(n_dp, tokens, lengths, w_qkv, vectors, w_out, w_up, w_down):
    n_x = n_dp // N_Z
    rows = tokens.shape[0]
    total = N_IN * rows
    lens = tuple(v.shape[0] for v in vectors)
    w_rows = w_qkv.shape[0]
    wide = (HP, total, LANES)

    def whole(shape):
        return jax.ShapeDtypeStruct((N_IN, N_Z, n_x) + shape, BF16)

    out_shape = packed_shape(*w_out.shape)

    n_remote = 5 + 3 + 3 + (1 + N_Z) * (n_x - 1) + 2 * (N_Z - 1) + 3
    n_remote += sum(gather_count(n_x, order) for order in GATHER_ORDERS.values())
    return pl.pallas_call(
        functools.partial(forward_kernel, n_dp, lens),
        out_shape=(
            jax.ShapeDtypeStruct((total, D), BF16),
            jax.ShapeDtypeStruct((total, D), BF16),
            jax.ShapeDtypeStruct(wide, BF16),
            jax.ShapeDtypeStruct(wide, BF16),
            jax.ShapeDtypeStruct((HP, HEAD_DIM, total), BF16),
            jax.ShapeDtypeStruct(wide, F32),
            jax.ShapeDtypeStruct((HP, total, total), BF16),
            jax.ShapeDtypeStruct((N_IN,) + packed_shape(rows, CW), BF16),
            whole(out_shape),
            whole(w_up.shape),
            whole(w_down.shape),
            jax.ShapeDtypeStruct((N_Z, n_x, N_IN, 8, LANES), F32),
            jax.ShapeDtypeStruct((D, 3 * CW), BF16),
        ),
        in_specs=[ANY, SMEM, VMEM] + [VMEM] * 8 + [VMEM, ANY, VMEM],
        out_specs=(ANY,) * 11 + (VMEM,) * 2,
        scratch_shapes=[
            pltpu.VMEM((N_IN, rows, D), BF16),
            pltpu.VMEM((total, D), BF16),
            pltpu.VMEM((total, D), BF16),
            pltpu.VMEM(wide, BF16),
            pltpu.VMEM(wide, BF16),
            pltpu.VMEM((HP, HEAD_DIM, total), BF16),
            pltpu.VMEM(wide, F32),
            pltpu.VMEM(wide, BF16),
            pltpu.VMEM((HP, LANES, total), BF16),
            pltpu.VMEM((total, BQ), F32),
            pltpu.VMEM((2, total, BQ), BF16),
            pltpu.VMEM((N_IN,) + packed_shape(rows, CW), BF16),
            pltpu.VMEM((3, w_rows, CW), BF16),
            pltpu.VMEM((3, w_rows, CW), BF16),
            pltpu.VMEM((D, 3 * HP * LANES), BF16),
            pltpu.VMEM((N_Z, n_x, w_rows, 3 * CW), BF16),
            pltpu.VMEM((8, LANES), F32),
            pltpu.VMEM(out_shape, BF16),
            pltpu.SemaphoreType.DMA((2,)),
        ]
        + sem_shapes(n_remote, 13),
        compiler_params=params(0),
        name="forward",
    )(tokens, lengths, w_qkv, *[v.reshape(1, -1) for v in vectors], w_out, w_up, w_down)


GC = 384


def add_rows(total, terms, out=None):
    step = 128

    def one(i, _):
        at = pl.ds(pl.multiple_of(i * step, step), step)
        if out is None:
            value = total[at, :]
            for term in terms:
                value = value + term[at, :]
            total[at, :] = value
        else:
            value = total[at, :].astype(F32)
            for term in terms:
                value = value + term[at, :].astype(F32)
            out[at, :] = value
        return 0

    lax.fori_loop(0, total.shape[0] // step, one, 0)


def add_blocks(total, term):
    if len(total.shape) == 2:
        add_rows(total, [term])
        return

    def one(i, _):
        total[i] = total[i] + term[i]
        return 0

    lax.fori_loop(0, total.shape[0], one, 0)


def unpack_into(out, parts, rows):
    half = rows // 2
    packed = parts.shape[-1] == 2 * CW

    def one(d, _):
        for i in range(N_IN):
            cols = slice(i * CW, (i + 1) * CW)
            if packed:
                first = pl.ds(pl.multiple_of(d * rows, 16), half)
                second = pl.ds(pl.multiple_of(d * rows + half, 16), half)
                out[first, cols] = parts[i, d, :, 0:CW]
                out[second, cols] = parts[i, d, :, CW : 2 * CW]
            else:
                at = pl.ds(pl.multiple_of(d * LANES, LANES), LANES)
                out[at, cols] = parts[i, at, :]
        return 0

    lax.fori_loop(0, out.shape[0] // (rows if packed else LANES), one, 0)


def pack_into(parts, value, rows, first):
    for i in range(N_IN):
        cols = slice(i * CW, (i + 1) * CW)
        if parts.shape[-1] == 2 * CW:
            for b in range(value.shape[0] // rows):
                parts[i, first + b] = pack(value[b * rows : (b + 1) * rows, cols])
        else:
            parts[i] = value[:, cols]


def middle_kernel(
    n_dp,
    lens,
    tokens,
    mixed,
    a_out,
    a_up,
    a_down,
    vec_all,
    cotangent,
    output,
    d_res_out,
    seen,
    t_out,
    t_up,
    t_down,
    sums,
    sum_up,
    tok,
    mix,
    po,
    pu,
    pd,
    cot,
    fo,
    fd,
    att,
    res,
    n_two,
    h_two,
    act,
    d_up,
    b_up,
    d_mixed,
    d_res,
    out_ref,
    d_att,
    co,
    cu,
    cd,
    h_turned,
    cot_turned,
    send,
    recv,
    local,
):
    p = Place(n_dp)
    n_dev = n_dp * N_IN
    sems = Sems(send, recv, local)
    rows = tokens.shape[0]
    ff = a_up.shape[0] * a_up.shape[2]
    r_out, r_down = D // n_dp, a_down.shape[3]
    loads = {
        name: sems.copy(src, dst)
        for name, src, dst in (
            ("out", a_out, po),
            ("mix", mixed, mix),
            ("tok", tokens, tok),
            ("up", a_up, pu),
            ("cot", cotangent, cot),
            ("down", a_down, pd),
        )
    }
    for load in loads.values():
        load.start()
    swap = [
        sems.remote(d_att.at[p.slots[s]], seen.at[s], (p.dp, p.slots[s])) for s in (DIAG, FAR, SIB)
    ]
    swap_own = sems.copy(d_att.at[p.inn], seen.at[OWN])

    def across(parts, buffer):
        return [
            sems.remote(parts.at[2 * yy + 1 - p.c], buffer.at[yy], (p.dp, p.sib))
            for yy in range(2)
        ]

    core_up, core_down, core_out = across(pu, cu), across(pd, cd), across(po, co)
    keeps = {
        name: [sems.copy(parts.at[2 * yy + p.c], out.at[yy]) for yy in range(2)]
        for name, parts, out in (("up", pu, t_up), ("down", pd, t_down), ("out", po, t_out))
    }
    out_save = sems.copy(out_ref, output)
    res_save = sems.copy(d_res, d_res_out)

    near = partners(p, "yc", diagonal=True)
    arrive(near)
    blocks = vec_all[...].reshape(n_dev * 8, LANES)
    shared = spread(blocks, lens[BIAS_OUT], D)
    for c in range(ff // D):
        b_up[:, c * D : (c + 1) * D] = spread(blocks, lens[BIAS_UP], D, c * D)[
            BIAS_UP : BIAS_UP + 1
        ]

    loads["out"].wait()
    loads["mix"].wait()
    unpack_into(fo, po, r_out)
    half = rows // 2
    for i in range(N_IN):
        cols = slice(i * CW, (i + 1) * CW)
        att[0:half, cols] = mix[i, :, 0:CW]
        att[half:rows, cols] = mix[i, :, CW : 2 * CW]
    loads["tok"].wait()
    residual = (
        tok[...].astype(F32) + product(att[...], fo[...]) + shared[BIAS_OUT : BIAS_OUT + 1]
    )
    res[...] = residual
    normed, factor = norm_parts(residual)
    n_two[...] = normed
    gain = shared[GAIN_TWO : GAIN_TWO + 1]
    h_two[...] = (normed * gain + shared[SHIFT_TWO : SHIFT_TWO + 1]).astype(BF16)
    loads["down"].wait()
    for i in range(N_IN):
        for d in range(n_dp):
            fd[i * CW : (i + 1) * CW, d * r_down : (d + 1) * r_down] = pd[i, d]
    loads["up"].wait()
    loads["cot"].wait()

    def hidden(it, _):
        hid = pl.ds(pl.multiple_of(it * HC, HC), HC)
        inside = pl.ds(pl.multiple_of(it % (D // HC) * HC, HC), HC)
        up = product(h_two[...], pu[it // (D // HC), :, inside]) + b_up[:, hid]
        d_act = product(cot[...], fd[:, hid])
        cdf = 0.5 * (1.0 + lax.erf(up * 0.7071067811865476))
        pdf = jnp.exp(-0.5 * up * up) * 0.3989422804014327
        act[:, hid] = (up * cdf).astype(BF16)
        grad = (d_act * (cdf + up * pdf)).astype(BF16)
        d_up[:, hid] = grad
        sum_up[:, hid] = jnp.sum(grad.astype(F32), axis=0, keepdims=True)
        return 0

    lax.fori_loop(0, ff // HC, hidden, 0)

    dh_two = None
    for i in range(N_IN):
        term = product_nt(d_up[:, i * D : (i + 1) * D], pu[i])
        dh_two = term if dh_two is None else dh_two + term
    normed = n_two[...]
    upstream = cot[...].astype(F32)
    value = upstream + norm_backward(dh_two, normed, factor, gain)
    d_res[...] = value
    res_save.start()
    low = value.astype(BF16)
    d_mixed[...] = low
    grad_att = product_nt(low, fo[...]).astype(BF16)
    for i in range(N_IN):
        d_att[i] = pack(grad_att[:, i * CW : (i + 1) * CW])
    all_in(near)
    start(swap)
    swap_own.start()

    def grad_up(i):
        cols = pl.ds(pl.multiple_of(i * D, D), D)
        pu[i] = product(h_turned[...], d_up[:, cols]).astype(BF16)

    h_turned[...] = h_two[...].T
    cot_turned[...] = cot[...].T
    for yy in range(2):
        grad_up(2 * yy + 1 - p.c)
    start(core_up)

    def grad_down(it, _):
        hid = pl.ds(pl.multiple_of(it * GC, GC), GC)
        value = product(cot_turned[...], act[:, hid]).astype(BF16)
        for i in range(N_IN):
            for b in range(GC // r_down):
                cols = slice(b * r_down, (b + 1) * r_down)
                pd[i, it * (GC // r_down) + b] = value[i * CW : (i + 1) * CW, cols]
        return 0

    lax.fori_loop(0, ff // GC, grad_down, 0)
    start(core_down)
    pack_into(po, product_tn(att[...], d_mixed[...]).astype(BF16), r_out, 0)
    start(core_out)
    for yy in range(2):
        grad_up(2 * yy + p.c)

    def output_part(n, _):
        cols = pl.ds(pl.multiple_of(n * HC, HC), HC)
        value = product_nt(act[...], fd[cols, :]) + res[:, cols]
        out_ref[:, cols] = value.astype(BF16)
        return 0

    res[...] = res[...] + shared[BIAS_DOWN : BIAS_DOWN + 1]
    lax.fori_loop(0, D // HC, output_part, 0)
    out_save.start()

    sums[...] = jnp.zeros_like(sums)
    sums[BIAS_OUT : BIAS_OUT + 1, :] = jnp.sum(low.astype(F32), axis=0, keepdims=True)
    sums[BIAS_DOWN : BIAS_DOWN + 1, :] = jnp.sum(upstream, axis=0, keepdims=True)
    sums[GAIN_TWO : GAIN_TWO + 1, :] = jnp.sum(dh_two * normed, axis=0, keepdims=True)
    sums[SHIFT_TWO : SHIFT_TWO + 1, :] = jnp.sum(dh_two, axis=0, keepdims=True)
    for copies, parts, buffer, name in (
        (core_up, pu, cu, "up"),
        (core_down, pd, cd, "down"),
        (core_out, po, co, "out"),
    ):
        wait_recv(copies)
        for yy in range(2):
            add_blocks(parts.at[2 * yy + p.c], buffer.at[yy])
        start(keeps[name])
    wait(swap)
    swap_own.wait()
    for copies in (core_up, core_down, core_out):
        wait_send(copies)
    for copies in keeps.values():
        wait(copies)
    out_save.wait()
    res_save.wait()


def middle(n_dp, lens, tokens, mixed, a_out, a_up, a_down, vec_all, cotangent):
    rows = tokens.shape[0]
    ff = a_up.shape[0] * a_up.shape[2]
    out_parts, up_parts, down_parts = a_out.shape[1:], a_up.shape[1:], a_down.shape[1:]
    return pl.pallas_call(
        functools.partial(middle_kernel, n_dp, lens),
        out_shape=(
            jax.ShapeDtypeStruct((rows, D), BF16),
            jax.ShapeDtypeStruct((rows, D), F32),
            jax.ShapeDtypeStruct((N_IN,) + packed_shape(rows, CW), BF16),
            jax.ShapeDtypeStruct((2,) + out_parts, BF16),
            jax.ShapeDtypeStruct((2,) + up_parts, BF16),
            jax.ShapeDtypeStruct((2,) + down_parts, BF16),
            jax.ShapeDtypeStruct((8, D), F32),
            jax.ShapeDtypeStruct((1, ff), F32),
        ),
        in_specs=[ANY] * 5 + [VMEM, ANY],
        out_specs=(ANY,) * 6 + (VMEM,) * 2,
        scratch_shapes=[
            pltpu.VMEM((rows, D), BF16),
            pltpu.VMEM((N_IN,) + packed_shape(rows, CW), BF16),
            pltpu.VMEM((N_IN,) + out_parts, BF16),
            pltpu.VMEM((N_IN,) + up_parts, BF16),
            pltpu.VMEM((N_IN,) + down_parts, BF16),
            pltpu.VMEM((rows, D), BF16),
            pltpu.VMEM((D, D), BF16),
            pltpu.VMEM((D, ff), BF16),
            pltpu.VMEM((rows, D), BF16),
            pltpu.VMEM((rows, D), F32),
            pltpu.VMEM((rows, D), F32),
            pltpu.VMEM((rows, D), BF16),
            pltpu.VMEM((rows, ff), BF16),
            pltpu.VMEM((rows, ff), BF16),
            pltpu.VMEM((1, ff), F32),
            pltpu.VMEM((rows, D), BF16),
            pltpu.VMEM((rows, D), F32),
            pltpu.VMEM((rows, D), BF16),
            pltpu.VMEM((N_IN,) + packed_shape(rows, CW), BF16),
            pltpu.VMEM((2,) + out_parts, BF16),
            pltpu.VMEM((2,) + up_parts, BF16),
            pltpu.VMEM((2,) + down_parts, BF16),
            pltpu.VMEM((D, rows), BF16),
            pltpu.VMEM((D, rows), BF16),
        ]
        + sem_shapes(9, 15),
        compiler_params=params(1),
        name="middle",
    )(tokens, mixed, a_out, a_up, a_down, vec_all, cotangent)


BK = 640
CQ = 1280
SCATTER_ORDERS = ("yxz", "xyz", "yxz", "xyz", "zyx")


class Scatter:
    def __init__(self, place, sems, blocks, order, buffers, out):
        self.order, self.out = order, out
        p = place
        self.total, self.buffers = buffers[0], dict(zip(order, buffers[1:]))
        self.load = sems.copy(blocks, self.total)
        _, _, n_x, _, _ = self.total.shape
        where = {"y": pl.ds(0, 2), "z": pl.ds(0, N_Z), "x": pl.ds(0, n_x)}
        own = {"y": p.y, "z": p.z, "x": p.x}
        self.copies, self.regions = {}, {}
        for axis in order:
            copies = []
            for at, device, k in p.peers(axis):
                there = dict(where)
                there[axis] = pl.ds(at, 1)
                src = self.total.at[there["y"], there["z"], there["x"]]
                copies.append(sems.remote(src, self.buffers[axis].at[k - 1], device))
            self.copies[axis] = copies
            where[axis] = pl.ds(own[axis], 1)
            self.regions[axis] = (where["y"], where["z"], where["x"])

    def step(self, number):
        if number == 0:
            self.load.start()
            return
        if number == 1:
            self.load.wait()
        else:
            axis = self.order[number - 2]
            wait_recv(self.copies[axis])
            region, buffer = self.total.at[self.regions[axis]], self.buffers[axis]
            if number - 1 == len(self.order):
                value = region[0, 0, 0].astype(F32)
                for k in range(buffer.shape[0]):
                    value = value + buffer[k, 0, 0, 0].astype(F32)
                self.out(value)
                return
            _, n_y, n_z, n_x, _, _ = buffer.shape

            def one(i, _):
                for y in range(n_y):
                    for x in range(n_x):
                        value = region[y, i, x]
                        for k in range(buffer.shape[0]):
                            value = value + buffer[k, y, i, x]
                        region[y, i, x] = value
                return 0

            lax.fori_loop(0, n_z, one, 0)
        start(self.copies[self.order[number - 1]])

    def finish(self):
        for axis in self.order:
            wait_send(self.copies[axis])


def scatter_buffers(n_x, rows, cols, order):
    sizes = {"y": 2, "z": N_Z, "x": n_x}
    shapes = [(2, N_Z, n_x, rows, cols)]
    left = dict(sizes)
    for axis in order:
        left[axis] = 1
        shapes.append((sizes[axis] - 1, left["y"], left["z"], left["x"], rows, cols))
    return [pltpu.VMEM(shape, BF16) for shape in shapes]


def scatter_count(n_x):
    return 1 + (N_Z - 1) + (n_x - 1)


def backward_kernel(n_dp, lens, *rest):
    (
        tokens,
        seen_in,
        att_in,
        e_all,
        q_in,
        v_in,
        kt_in,
        h_in,
        n_in,
        wq_in,
        d_res_in,
        t_out,
        t_up,
        t_down,
        vec_all,
        sums,
        sum_up,
    ) = rest[:17]
    grad_tokens, g_qkv, s_out, s_up, s_down = rest[17:22]
    vec_outs = rest[22:30]
    (
        seen,
        att,
        q_ref,
        v_ref,
        kt_ref,
        h_ref,
        n_ref,
        wq_ref,
        d_res,
        do_ref,
        dqt_ref,
        e_ref,
        d_all,
        t_core,
        t_far,
        g_w,
        norm_sums,
        w_own,
        w_x,
        w_in,
        v_own,
        v_all,
        v_y,
        v_c,
    ) = rest[30:54]
    buffers = rest[54:74]
    e_sem, send, recv, local = rest[74:]
    p = Place(n_dp)
    n_dev, n_x = n_dp * N_IN, n_dp // N_Z
    sems = Sems(send, recv, local)
    rows = tokens.shape[0]
    total = N_IN * rows
    n_down = t_down.shape[3]
    half_down = first_rows(n_down)
    half_up = t_up.shape[4] // 2

    def put(out, first):
        def write(value):
            size, cols = value.shape
            if cols == 2 * CW and out.shape[1] == CW:
                out[0:size, :] = value[:, 0:CW]
                out[size:, :] = value[:, CW:]
            elif cols == out.shape[1]:
                out[first : first + size, :] = value
            else:
                out[:, first : first + cols] = value

        return write

    near = partners(p, "yc", diagonal=True)
    others = [(p.dp + k) % n_dp for k in range(1, n_dp)]
    for k, dp in enumerate(others, 1):
        near += [(dp, inn) for inn in range(N_IN)] if k % n_x == 0 else [(dp, p.inn)]
    arrive(near)
    loads = {
        name: sems.copy(src, dst)
        for name, src, dst in (
            ("seen", seen_in, seen),
            ("att", att_in, att),
            ("v", v_in, v_ref),
            ("kt", kt_in, kt_ref),
            ("q", q_in, q_ref),
            ("wq", wq_in, wq_ref),
            ("res", d_res_in, d_res),
        )
    }
    for name in ("seen", "att"):
        loads[name].start()
    pieces = []
    for number, (ref, out, first, size, axis) in enumerate(
        (
            (t_down, s_down, 0, half_down, 0),
            (t_down, s_down, half_down, n_down - half_down, 0),
            (t_up, s_up, 0, half_up, 1),
            (t_up, s_up, half_up, half_up, 1),
            (t_out, s_out, 0, t_out.shape[3], 0),
        )
    ):
        pieces.append(
            Scatter(
                p,
                sems,
                part(ref, first, size, axis),
                SCATTER_ORDERS[number],
                buffers[4 * number : 4 * number + 4],
                put(out, first),
            )
        )
    down0, down1, up0, up1, small = pieces

    def room(i):
        return e_ref.at[i, :, pl.ds(0, D)]

    dh_far, dh_diag, dh_sib, dh_own = room(2), room(3), room(0), room(1)
    tok = n_ref.at[0]
    loads["tok"] = sems.copy(tokens, tok)

    def fetch(kb, h, half, slot):
        at = pl.ds(pl.multiple_of(kb * BK, BK), BK)
        src = e_all.at[h, at, pl.ds(half * CQ, CQ)]
        return pltpu.make_async_copy(src, e_ref.at[slot], e_sem.at[slot])

    fetch(0, 0, 0, 0).start()
    fetch(0, 0, 1, 1).start()
    feeds = []
    for s in range(N_IN):
        at = pl.ds(s * rows, rows)
        feeds.append(
            [sems.copy(n_in.at[at], n_ref.at[s % 2]), sems.copy(h_in.at[at], h_ref.at[s % 2])]
        )
    for name in ("v", "kt", "q"):
        loads[name].start()
    for item in (down0, down1, small, up0, up1):
        item.step(0)
    for feed in feeds[0:2]:
        start(feed)
    for name in ("wq", "res"):
        loads[name].start()
    here, there = (p.dp, p.sib), (p.dp, p.far)
    give_diag = sems.remote(dh_diag, t_core.at[1], here)
    give_sib = sems.remote(dh_sib, t_core.at[0], here)
    across = sems.remote(dh_far, t_far, there)
    w_order = tuple(range(1, N_Z)) + (0,)
    w_to_x = {}
    for kz in w_order:
        w_to_x[kz] = [
            sems.remote(w_own.at[(p.z + kz) % N_Z, at], w_x.at[k - 1, kz], device)
            for at, device, k in p.peers("x")
        ]
    v_to_c = [
        sems.remote(v_own.at[:, :, 2 * yy + 1 - p.c], v_c.at[yy], here) for yy in range(2)
    ]
    v_to_y = sems.remote(v_own.at[:, :, p.far], v_y, there)
    v_to_all = [
        sems.remote(v_own.at[dp // n_x, dp % n_x, p.inn], v_all.at[k], (dp, p.inn))
        for k, dp in enumerate(others)
    ]
    unit_base = sems.n

    def unit(t, kz):
        u = p.inn + N_IN * t
        owner, r = u // 3, u % 3
        at = (p.z + kz) % N_Z
        away = pltpu.make_async_remote_copy(
            src_ref=w_own.at[at, p.x, t],
            dst_ref=w_in.at[r, kz],
            send_sem=send.at[unit_base + t * N_Z + kz],
            recv_sem=recv.at[unit_base + r * N_Z + kz],
            device_id=(at * n_x + p.x, owner),
            device_id_type=MESH,
        )
        return owner == p.inn, r, away

    def arrival(r, kz):
        bring = pltpu.make_async_remote_copy(
            src_ref=w_own.at[p.z, p.x, 0],
            dst_ref=w_in.at[r, kz],
            send_sem=send.at[unit_base],
            recv_sem=recv.at[unit_base + r * N_Z + kz],
            device_id=(p.dp, p.far),
            device_id_type=MESH,
        )
        return (3 * p.inn + r) % N_IN == p.inn, bring

    dqt_ref[...] = jnp.zeros_like(dqt_ref)
    loads["seen"].wait()
    loads["att"].wait()
    for s in range(N_IN):
        if s == 1:
            all_in(near)
            for item in (down0, down1, small, up0, up1):
                item.step(1)
        at = pl.ds(s * rows, rows)
        for h in range(HP):
            grad = jnp.concatenate(
                [
                    seen[s, :, side * CW + h * HEAD_DIM : side * CW + (h + 1) * HEAD_DIM]
                    for side in range(2)
                ],
                axis=0,
            ).astype(F32)
            both = att[h, at, :]
            scale = SCALE / both[:, HEAD_DIM : HEAD_DIM + 1]
            delta = jnp.sum(grad * both[:, 0:HEAD_DIM], axis=-1, keepdims=True) * -scale
            high = delta.astype(BF16).astype(F32)
            lane = lax.broadcasted_iota(jnp.int32, (rows, HEAD_DIM), 1)
            tail = jnp.where(lane == 0, high, jnp.where(lane == 1, delta - high, 0.0))
            do_ref[h, at, :] = jnp.concatenate([grad * scale, tail], axis=1).astype(BF16)
    for name in ("v", "kt", "q"):
        loads[name].wait()

    actions = {
        3: [(small, 2), (down0, 2), (down1, 2)],
        7: [(small, 3), (up0, 2), (up1, 2)],
        9: [(down0, 3), (down1, 3), (small, 4)],
        14: [(down0, 4), (down1, 4)],
    }
    last = N_IN - 1
    root = HEAD_DIM**0.5

    def act(kb, first, number):
        for when, acts in actions.items():
            if when in (number, number + HP):

                @pl.when(kb == first + (when - number) // HP)
                def _():
                    for which, stage in acts:
                        which.step(stage)

    def piece(kb, h, half, slot):
        at = pl.ds(pl.multiple_of(kb * BK, BK), BK)
        cs = slice(half * CQ, (half + 1) * CQ)
        expo, do = e_ref[slot], do_ref[h, cs, :]
        ds = (expo.astype(F32) * product_nt(v_ref[h, at, :], do)).astype(BF16)
        dv, dk = product(expo, do), product(ds, q_ref[h, cs, :])
        dqt_ref[h, :, cs] += product(kt_ref[h, :, at], ds)
        return dv, dk

    def head_cols(t, h):
        return slice(t * CW + h * HEAD_DIM, t * CW + (h + 1) * HEAD_DIM)

    def finish_keys(kb, h, dv, dk):
        at = pl.ds(pl.multiple_of(kb * BK, BK), BK)
        d_all[at, head_cols(1, h)] = (dk * root).astype(BF16)
        d_all[at, head_cols(2, h)] = (dv * root).astype(BF16)

    def both_halves(kb, _):
        for h in range(HP):
            slot = (kb * HP + h) % 2 * 2
            other = 2 - slot
            if h < HP - 1:
                for half in range(2):
                    fetch(kb, h + 1, half, other + half).start()
            else:

                @pl.when(kb == 0)
                def _():
                    for half in range(2):
                        fetch(1, 0, half, other + half).start()

                @pl.when(kb == 1)
                def _():
                    fetch(2, 0, 0, 0).start()

            for half in range(2):
                fetch(kb, h, half, slot + half).wait()
            dv0, dk0 = piece(kb, h, 0, slot)
            dv1, dk1 = piece(kb, h, 1, slot + 1)
            dv, dk = dv0 + dv1, dk0 + dk1
            finish_keys(kb, h, dv[:, 0:HEAD_DIM], dk[:, 0:HEAD_DIM])
            act(kb, 0, h)
        return 0

    lax.fori_loop(0, 2, both_halves, 0)

    def one_half(half, first):
        def run(kb, _):
            for h in range(HP):
                slot = ((kb - 2) * HP + h) % 2
                other = 1 - slot
                if h < HP - 1:
                    fetch(kb, h + 1, half, other).start()
                else:

                    @pl.when(kb == 2)
                    def _():
                        fetch(3, 0, half, other).start()

                    if half == 0:

                        @pl.when(kb == last)
                        def _():
                            fetch(2, 0, 1, other).start()

                fetch(kb, h, half, slot).wait()
                dv, dk = piece(kb, h, half, slot)
                at = pl.ds(pl.multiple_of(kb * BK, BK), BK)
                if half == 0:
                    att[h, at, :] = jnp.concatenate([dk[:, 0:HEAD_DIM], dv[:, 0:HEAD_DIM]], axis=1)
                else:
                    dk = dk[:, 0:HEAD_DIM] + att[h, at, 0:HEAD_DIM]
                    dv = dv[:, 0:HEAD_DIM] + att[h, at, HEAD_DIM:LANES]
                    finish_keys(kb, h, dv, dk)
                act(kb, 2, first + h)
            return 0

        lax.fori_loop(2, N_IN, run, 0)
        for h in range(HP):
            cs = slice(half * CQ, (half + 1) * CQ)
            d_all[cs, head_cols(0, h)] = dqt_ref[h, :, cs].T.astype(BF16)

    def input_grad(i):
        at = pl.ds(i * rows, rows)
        feeds[i][0].wait()
        value = product_nt(d_all[at, :], wq_ref[...])
        gain_sum = jnp.sum(value * n_ref[i % 2].astype(F32), axis=0, keepdims=True)
        shift_sum = jnp.sum(value, axis=0, keepdims=True)
        return value.astype(BF16), gain_sum, shift_sum

    def weight_grad(i):
        at = pl.ds(i * rows, rows)
        feeds[i][1].wait()
        return product_tn(h_ref[i % 2], d_all[at, :])

    one_half(0, 2 * HP)
    loads["wq"].wait()
    value, gain_sum, shift_sum = input_grad(DIAG)
    dh_diag[...] = value
    give_diag.start()
    value, g_sum, s_sum = input_grad(FAR)
    dh_far[...] = value
    norm_sums[0:1, :] = gain_sum + g_sum
    norm_sums[1:2, :] = shift_sum + s_sum
    g_w[...] = weight_grad(DIAG) + weight_grad(FAR)
    for feed in feeds[2:4]:
        start(feed)
    packed = unspread(sums[...], n_dev, lens[GAIN_ONE])
    row = lax.broadcasted_iota(jnp.int32, (8, D), 0)
    for c in range(sum_up.shape[1] // D):
        line = jnp.where(row == BIAS_UP, sum_up[:, c * D : (c + 1) * D], 0.0)
        packed = packed + unspread(line, n_dev, lens[BIAS_UP], c * D)
    v_own[...] = packed.reshape(N_Z, n_x, N_IN, 8, LANES)
    give_diag.wait_recv()
    add_rows(dh_far, [t_core.at[1]])
    across.start()
    up0.step(3)
    up1.step(3)
    one_half(1, 4 * HP)
    w_rows = D // n_dp
    wide = weight_grad(SIB) + weight_grad(OWN) + g_w[...]
    for t in range(3):
        value = wide[:, t * CW : (t + 1) * CW]
        value = value.astype(BF16) if packs(w_rows) else value
        for d in range(n_dp):
            block = value[d * w_rows : (d + 1) * w_rows]
            block = pack(block) if packs(w_rows) else block.astype(BF16)
            w_own[d // n_x, d % n_x, t] = block
    for kz in w_order:
        start(w_to_x[kz])
    def add_w(kz):
        wait_recv(w_to_x[kz])
        at = (p.z + kz) % N_Z
        value = w_own[at, p.x]
        for k in range(n_x - 1):
            value = value + w_x[k, kz]
        w_own[at, p.x] = value
        for t in range(3):
            stays, r, away = unit(t, kz)
            if kz:
                away.start()
            else:

                @pl.when(jnp.logical_not(stays))
                def _():
                    away.start()

                @pl.when(stays)
                def _():
                    w_in[r, 0] = value[t]

    value, gain_sum, shift_sum = input_grad(SIB)
    dh_sib[...] = value
    give_sib.start()
    loads["tok"].start()
    add_w(1)
    value, g_sum, s_sum = input_grad(OWN)
    dh_own[...] = value
    gain_sum = gain_sum + g_sum + norm_sums[0:1, :]
    shift_sum = shift_sum + s_sum + norm_sums[1:2, :]

    row = lax.broadcasted_iota(jnp.int32, (8, D), 0)
    wide = jnp.where(row == GAIN_ONE, gain_sum, jnp.where(row == SHIFT_ONE, shift_sum, 0.0))
    packed = unspread(wide, n_dev, lens[GAIN_ONE])
    row = lax.broadcasted_iota(jnp.int32, (8, CW), 0)
    for t, first in ((0, 0), (2, D)):
        line = d_all[:, t * CW : (t + 1) * CW].astype(F32)
        line = jnp.sum(line, axis=0, keepdims=True)
        line = jnp.where(row == BIAS_QV, line, 0.0)
        packed = packed + unspread(line, n_dev, lens[BIAS_QV], first + p.inn * CW)
    v_own[...] = v_own[...] + packed.reshape(N_Z, n_x, N_IN, 8, LANES)
    start(v_to_c)
    add_w(2)
    wait_recv(v_to_c)
    for yy in range(2):
        v_own[:, :, 2 * yy + p.c] = v_own[:, :, 2 * yy + p.c] + v_c[yy]
    v_to_y.start()
    add_w(3)
    v_to_y.wait_recv()
    v_own[:, :, p.inn] = v_own[:, :, p.inn] + v_y[...]
    start(v_to_all)
    up0.step(4)
    up1.step(4)
    add_w(0)
    give_sib.wait_recv()
    add_rows(dh_own, [t_core.at[0]])
    blocks = vec_all[...].reshape(n_dev * 8, LANES)
    gain = spread(blocks, lens[GAIN_ONE], D)[GAIN_ONE : GAIN_ONE + 1]
    loads["tok"].wait()
    loads["res"].wait()
    normed, factor = norm_parts(tok[...].astype(F32))
    for r in range(3):
        value = None
        for kz in range(N_Z):
            stays, bring = arrival(r, kz)
            if kz:
                bring.wait_recv()
            else:

                @pl.when(jnp.logical_not(stays))
                def _():
                    bring.wait_recv()

            term = w_in[r, kz].astype(F32)
            value = term if value is None else value + term
        cols = slice(r * CW, (r + 1) * CW)
        if packs(w_rows):
            g_qkv[0 : w_rows // 2, cols] = value[:, 0:CW]
            g_qkv[w_rows // 2 :, cols] = value[:, CW:]
        else:
            g_qkv[:, cols] = value
    wait_recv(v_to_all)
    final = v_own[p.z, p.x, p.inn]
    for k in range(n_dp - 1):
        final = final + v_all[k]
    for r, length in enumerate(lens):
        vec_outs[r][...] = final[r : r + 1, 0:length]
    across.wait_recv()
    grad = dh_own[...].astype(F32) + t_far[...].astype(F32)
    grad_tokens[...] = (d_res[...] + norm_backward(grad, normed, factor, gain)).astype(BF16)
    for t in range(3):
        for kz in range(N_Z):
            stays, _, away = unit(t, kz)
            if kz:
                away.wait_send()
            else:

                @pl.when(jnp.logical_not(stays))
                def _():
                    away.wait_send()

    wait_send([give_diag, give_sib, across, v_to_y])
    wait_send(v_to_c + v_to_all)
    for kz in w_order:
        wait_send(w_to_x[kz])
    for item in pieces:
        item.finish()


def backward(n_dp, lens, like_out, like_down, tokens, seen, att, e_all, q, v, kt, h_one, n_one, wq, d_res, *grads):
    t_out, t_up, t_down, vec_all, sums, sum_up = grads
    n_x = n_dp // N_Z
    rows = tokens.shape[0]
    total = N_IN * rows
    w_rows = D // n_dp
    w_block = packed_shape(w_rows, CW)
    r_down, c_down = t_down.shape[3:]
    r_up, c_up = t_up.shape[3:]
    r_first = first_rows(r_down)
    sizes = [(r_first, c_down), (r_down - r_first, c_down)]
    sizes += [(r_up, c_up // 2)] * 2 + [t_out.shape[3:]]
    scratch = [
        pltpu.VMEM((N_IN,) + packed_shape(rows, CW), BF16),
        pltpu.VMEM((HP, total, LANES), F32),
        pltpu.VMEM((HP, total, LANES), BF16),
        pltpu.VMEM((HP, total, LANES), BF16),
        pltpu.VMEM((HP, HEAD_DIM, total), BF16),
        pltpu.VMEM((2, rows, D), BF16),
        pltpu.VMEM((2, rows, D), BF16),
        pltpu.VMEM((D, 3 * CW), BF16),
        pltpu.VMEM((rows, D), F32),
        pltpu.VMEM((HP, total, LANES), BF16),
        pltpu.VMEM((HP, HEAD_DIM, total), F32),
        pltpu.VMEM((4, BK, CQ), BF16),
        pltpu.VMEM((total, 3 * CW), BF16),
        pltpu.VMEM((2, rows, D), BF16),
        pltpu.VMEM((rows, D), BF16),
        pltpu.VMEM((D, 3 * CW), F32),
        pltpu.VMEM((2, D), F32),
        pltpu.VMEM((N_Z, n_x, 3) + w_block, BF16),
        pltpu.VMEM((n_x - 1, N_Z, 3) + w_block, BF16),
        pltpu.VMEM((3, N_Z) + w_block, BF16),
        pltpu.VMEM((N_Z, n_x, N_IN, 8, LANES), F32),
        pltpu.VMEM((n_dp - 1, 8, LANES), F32),
        pltpu.VMEM((N_Z, n_x, 8, LANES), F32),
        pltpu.VMEM((2, N_Z, n_x, 8, LANES), F32),
    ]
    for (r, c), order in zip(sizes, SCATTER_ORDERS):
        scratch += scatter_buffers(n_x, r, c, order)
    n_remote = 5 * scatter_count(n_x) + 3 + N_Z * (n_x - 1) + (n_dp - 1) + 3 + 3 * N_Z
    return pl.pallas_call(
        functools.partial(backward_kernel, n_dp, lens),
        out_shape=(
            jax.ShapeDtypeStruct((rows, D), BF16),
            jax.ShapeDtypeStruct((w_rows, 3 * CW), F32),
            jax.ShapeDtypeStruct(like_out.shape, F32),
            jax.ShapeDtypeStruct(t_up.shape[3:], F32),
            jax.ShapeDtypeStruct(like_down.shape, F32),
        )
        + tuple(jax.ShapeDtypeStruct((1, length), F32) for length in lens),
        in_specs=[ANY] * 14 + [VMEM] * 3,
        out_specs=(VMEM,) * 13,
        scratch_shapes=scratch + [pltpu.SemaphoreType.DMA((4,))] + sem_shapes(n_remote, 21),
        compiler_params=params(2, VMEM_LIMIT if n_dp <= 8 else VMEM_LIMIT + (1 << 20)),
        name="backward",
    )(
        tokens,
        seen,
        att,
        e_all,
        q,
        v,
        kt,
        h_one,
        n_one,
        wq,
        d_res,
        t_out,
        t_up,
        t_down,
        vec_all,
        sums,
        sum_up,
    )


def finish_kernel(n, *rest):
    for source, result in zip(rest[:n], rest[n:]):
        result[...] = source[...]


def finish(*arrays):
    n = len(arrays)
    return pl.pallas_call(
        functools.partial(finish_kernel, n),
        out_shape=tuple(jax.ShapeDtypeStruct(array.shape, array.dtype) for array in arrays),
        in_specs=[VMEM] * n,
        out_specs=(VMEM,) * n,
        compiler_params=pltpu.CompilerParams(vmem_limit_bytes=VMEM_LIMIT),
        name="finish",
    )(*arrays)


def on_device(
    tokens,
    lengths,
    w_qkv,
    bias_qv,
    w_out,
    bias_out,
    w_up,
    bias_up,
    w_down,
    bias_down,
    gain_one,
    shift_one,
    gain_two,
    shift_two,
    cotangent,
):
    n_dp = lax.axis_size("dp")
    n_x = n_dp // N_Z
    vectors = (
        bias_qv,
        bias_out,
        bias_up,
        bias_down,
        gain_one,
        shift_one,
        gain_two,
        shift_two,
    )
    lens = tuple(v.shape[0] for v in vectors)
    h_one, n_one, q, v, kt, att, e_all, mixed, a_out, a_up, a_down, vec_all, wq = forward(
        n_dp, tokens, lengths, w_qkv, vectors, w_out, w_up, w_down.T
    )

    def by_dp(blocks):
        return blocks.reshape((N_IN, n_dp) + blocks.shape[3:])

    output, d_res, seen, t_out, t_up, t_down, sums, sum_up = middle(
        n_dp,
        lens,
        tokens,
        mixed,
        by_dp(a_out) if packs(w_out.shape[0]) else a_out.reshape(N_IN, D, CW),
        a_up.reshape(N_IN, D, -1),
        by_dp(a_down),
        vec_all,
        cotangent,
    )

    def blocks(grads, like):
        return grads.reshape((2, N_Z, n_x) + like.shape[3:])

    grad_tokens, g_qkv, g_out, g_up, g_down, *vecs = backward(
        n_dp,
        lens,
        w_out,
        w_down.T,
        tokens,
        seen,
        att,
        e_all,
        q,
        v,
        kt,
        h_one,
        n_one,
        wq,
        d_res,
        blocks(t_out, a_out),
        blocks(t_up, a_up),
        blocks(t_down, a_down),
        vec_all,
        sums,
        sum_up,
    )
    output, grad_tokens, g_qkv, g_out, g_up, g_down, *vecs = finish(
        output, grad_tokens, g_qkv, g_out, g_up, g_down, *vecs
    )
    vecs = [vec.reshape(-1) for vec in vecs]
    return (
        output,
        grad_tokens,
        g_qkv,
        vecs[BIAS_QV],
        g_out,
        vecs[BIAS_OUT],
        g_up,
        vecs[BIAS_UP],
        g_down.T,
        vecs[BIAS_DOWN],
        vecs[GAIN_ONE],
        vecs[SHIFT_ONE],
        vecs[GAIN_TWO],
        vecs[SHIFT_TWO],
    )


def solution(mesh):
    rows = P(("dp", "inner"), None)
    mat = P("dp", "inner")
    vec = P(("dp", "inner"))
    return jax.shard_map(
        on_device,
        mesh=mesh,
        in_specs=(
            rows,
            P("dp", None),
            mat,
            vec,
            mat,
            vec,
            mat,
            vec,
            mat,
            vec,
            vec,
            vec,
            vec,
            vec,
            rows,
        ),
        out_specs=(rows, rows, mat, vec, mat, vec, mat, vec, mat, vec, vec, vec, vec, vec),
        check_vma=False,
    )
```

```python
import functools

import jax
import jax.numpy as jnp
from jax import lax
from jax.experimental import pallas as pl
from jax.experimental.pallas import tpu as pltpu
from jax.sharding import PartitionSpec as P

D = 768
HEADS = 12
HEAD_DIM = 64
EPS = 1e-06
NEG = -1e30
LANES = 128
N_Z = 4
N_IN = 4
HP = HEADS // N_IN
CW = HP * HEAD_DIM
SCALE = HEAD_DIM**-0.5
MESH = pl.DeviceIdType.MESH
NT = (((1,), (1,)), ((), ()))
TN = (((0,), (0,)), ((), ()))
F32, BF16 = jnp.float32, jnp.bfloat16
ANY = pl.BlockSpec(memory_space=pl.ANY)
VMEM = pl.BlockSpec(memory_space=pltpu.VMEM)
SMEM = pl.BlockSpec(memory_space=pltpu.SMEM)
VMEM_LIMIT = 62 << 20
BIAS_QV, BIAS_OUT, BIAS_UP, BIAS_DOWN, GAIN_ONE, SHIFT_ONE, GAIN_TWO, SHIFT_TWO = range(8)


def product(left, right):
    return jnp.dot(left, right, preferred_element_type=F32)


def product_tn(left, right):
    return lax.dot_general(left, right, TN, preferred_element_type=F32)


def product_nt(left, right):
    return lax.dot_general(left, right, NT, preferred_element_type=F32)


class Place:
    def __init__(self, n_dp):
        self.n_x = n_dp // N_Z
        self.dp = lax.axis_index("dp")
        self.inn = lax.axis_index("inner")
        self.x, self.z = self.dp % self.n_x, self.dp // self.n_x
        self.c, self.y = self.inn % 2, self.inn // 2
        self.sib = self.y * 2 + 1 - self.c
        self.far = (1 - self.y) * 2 + self.c
        self.diag = (1 - self.y) * 2 + 1 - self.c
        self.slots = (self.diag, self.far, self.sib, self.inn)

    def size(self, axis):
        return {"z": N_Z, "x": self.n_x, "y": 2, "c": 2}[axis]

    def peer(self, axis, k):
        if axis == "z":
            at = (self.z + k) % N_Z
            return at, (at * self.n_x + self.x, self.inn)
        if axis == "x":
            at = (self.x + k) % self.n_x
            return at, (self.z * self.n_x + at, self.inn)
        if axis == "y":
            return 1 - self.y, (self.dp, self.far)
        return 1 - self.c, (self.dp, self.sib)

    def peers(self, axis):
        return [self.peer(axis, k) + (k,) for k in range(1, self.size(axis))]


class Sems:
    def __init__(self, send, recv, local):
        self.send, self.recv, self.local = send, recv, local
        self.n = self.m = 0

    def remote(self, src, dst, device):
        i = self.n
        self.n += 1
        return pltpu.make_async_remote_copy(
            src_ref=src,
            dst_ref=dst,
            send_sem=self.send.at[i],
            recv_sem=self.recv.at[i],
            device_id=device,
            device_id_type=MESH,
        )

    def copy(self, src, dst):
        i = self.m
        self.m += 1
        return pltpu.make_async_copy(src, dst, self.local.at[i])


def sem_shapes(n_remote, n_local):
    return [
        pltpu.SemaphoreType.DMA((n_remote,)),
        pltpu.SemaphoreType.DMA((n_remote,)),
        pltpu.SemaphoreType.DMA((n_local,)),
    ]


def partners(place, axes, diagonal=False):
    devices = [device for axis in axes for _, device, _ in place.peers(axis)]
    if diagonal:
        devices.append((place.dp, place.diag))
    return devices


def arrive(devices):
    barrier = pltpu.get_barrier_semaphore()
    for device in devices:
        pl.semaphore_signal(barrier, inc=1, device_id=device, device_id_type=MESH)


def all_in(devices):
    pl.semaphore_wait(pltpu.get_barrier_semaphore(), len(devices))


def start(copies):
    for copy in copies:
        copy.start()


def wait_recv(copies):
    for copy in copies:
        copy.wait_recv()


def wait_send(copies):
    for copy in copies:
        copy.wait_send()


def wait(copies):
    for copy in copies:
        copy.wait()


def params(collective_id, limit=VMEM_LIMIT):
    return pltpu.CompilerParams(
        collective_id=collective_id, has_side_effects=True, vmem_limit_bytes=limit
    )


def part(ref, first, size, axis):
    cut = pl.ds(first, size)
    lead = (slice(None),) * (len(ref.shape) - 2)
    return ref.at[lead + ((cut, slice(None)) if axis == 0 else (slice(None), cut))]


def pack(value):
    half = value.shape[0] // 2
    return jnp.concatenate([value[:half], value[half:]], axis=1)


def packs(rows):
    return rows % 32 == 0


def packed_shape(rows, cols):
    return (rows // 2, 2 * cols) if packs(rows) else (rows, cols)


def first_rows(rows):
    return -(-rows // 32) * 16


DIAG, FAR, SIB, OWN = range(N_IN)


def place_mask(n_dev, length, size, first):
    column = lax.broadcasted_iota(jnp.int32, (n_dev * 8, size), 1) + first
    row = lax.broadcasted_iota(jnp.int32, (n_dev * 8, size), 0)
    begin = (row // 8) * length
    owned = jnp.logical_and(column >= begin, column < begin + length)
    column = lax.broadcasted_iota(jnp.int32, (LANES, size), 1) + first
    lane = lax.broadcasted_iota(jnp.int32, (LANES, size), 0)
    return owned, jnp.where(column % length == lane, 1.0, 0.0).astype(BF16)


def spread(blocks, length, size, first=0):
    n_dev = blocks.shape[0] // 8
    owned, lanes = place_mask(n_dev, length, size, first)
    wide = jnp.where(owned, product(blocks.astype(BF16), lanes), 0.0)
    return jnp.sum(wide.reshape(n_dev, 8, size), axis=0)


def unspread(rows, n_dev, length, first=0):
    size = rows.shape[1]
    if size > 2 * LANES and n_dev * size > 32 * D:
        cut = size // 3
        parts = [
            unspread(rows[:, at : at + cut], n_dev, length, first + at)
            for at in range(0, size, cut)
        ]
        return parts[0] + parts[1] + parts[2]
    owned, lanes = place_mask(n_dev, length, size, first)
    total = None
    for _ in range(2):
        low = rows.astype(BF16)
        rows = rows - low.astype(F32)
        many = jnp.broadcast_to(low.astype(F32)[None], (n_dev,) + low.shape)
        many = jnp.where(owned, many.reshape(n_dev * 8, low.shape[1]), 0.0).astype(BF16)
        term = product_nt(many, lanes)
        total = term if total is None else total + term
    return total


def norm_parts(value):
    mean = jnp.mean(value, axis=-1, keepdims=True)
    centred = value - mean
    spread_of = jnp.mean(centred * centred, axis=-1, keepdims=True)
    factor = lax.rsqrt(spread_of + EPS)
    return centred * factor, factor


def norm_backward(grad, normed, factor, gain):
    scaled = grad * gain
    inner_mean = jnp.mean(scaled, axis=-1, keepdims=True)
    cross_mean = jnp.mean(scaled * normed, axis=-1, keepdims=True)
    return factor * (scaled - inner_mean - normed * cross_mean)


class Gather:
    def __init__(self, place, sems, source, out, view, order):
        p = place

        def at(inn, z, x):
            return view(out.at[inn, z, x])

        everything = slice(None)
        zs, xs = p.z, p.x
        self.own = sems.copy(source, at(p.inn, zs, xs))
        inns = [p.inn]
        self.stages = []
        for number, axis in enumerate(order):
            copies = []
            for _, device, _ in p.peers(axis):
                for inn in inns:
                    target = at(inn, zs, xs)
                    copies.append(sems.remote(source if number == 0 else target, target, device))
            self.stages.append(copies)
            if axis == "z":
                zs = everything
            elif axis == "x":
                xs = everything
            elif axis == "y":
                inns = [p.inn, p.far]

    def step(self, number):
        if number == 0:
            self.own.start()
        else:
            if number == 1:
                self.own.wait()
            wait_recv(self.stages[number - 1])
        if number < len(self.stages):
            start(self.stages[number])

    def finish(self):
        for copies in self.stages:
            wait_send(copies)


def gather_count(n_x, order):
    count, inns = 0, 1
    for axis in order:
        count += inns * {"z": N_Z - 1, "x": n_x - 1, "y": 1, "c": 1}[axis]
        inns = 2 if axis == "y" else inns
    return count


BQ = 640
CK = 256
GATHER_ORDERS = {"down0": "xyzc", "down1": "zyxc", "up0": "zyxc", "up1": "zxyc", "out": "xyzc"}


def forward_kernel(
    n_dp,
    lens,
    tokens,
    lengths,
    w_qkv,
    *rest,
):
    vec_in, rest = rest[:8], rest[8:]
    (
        w_out,
        w_up,
        w_down,
        h_out,
        n_out,
        q_out,
        v_out,
        kt_out,
        att_out,
        e_out,
        mixed,
        all_out,
        all_up,
        all_down,
        vec_all,
        wq_full,
        tok,
        h_ref,
        n_ref,
        q_ref,
        v_ref,
        kt_ref,
        att_ref,
        k_ref,
        vt_ref,
        s_ref,
        e_ref,
        low_ref,
        units,
        unit_in,
        w_wide,
        wq_all,
        vec_own,
        out_pack,
        e_sem,
        send,
        recv,
        local,
    ) = rest
    p = Place(n_dp)
    n_dev = n_dp * N_IN
    sems = Sems(send, recv, local)
    rows = tokens.shape[0]
    total = N_IN * rows
    n_down = w_down.shape[0]
    half_down = first_rows(n_down)
    half_up = w_up.shape[1] // 2

    def piece(name, ref, out, first, size, axis):
        view = functools.partial(part, first=first, size=size, axis=axis)
        return Gather(p, sems, view(ref), out, view, GATHER_ORDERS[name])

    down0 = piece("down0", w_down, all_down, 0, half_down, 0)
    down1 = piece("down1", w_down, all_down, half_down, n_down - half_down, 0)
    up0 = piece("up0", w_up, all_up, 0, half_up, 1)
    up1 = piece("up1", w_up, all_up, half_up, half_up, 1)
    small = Gather(p, sems, out_pack, all_out, lambda ref: ref, GATHER_ORDERS["out"])
    pieces = [down0, down1, up0, up1, small]

    own_tok = sems.copy(tokens, tok.at[OWN])
    tok_sib = sems.remote(tokens, tok.at[SIB], (p.dp, p.sib))
    half_rows = rows // 2
    halves = [pl.ds(i * half_rows, half_rows) for i in range(2)]
    tok_far = [sems.remote(tokens.at[at], tok.at[FAR, at], (p.dp, p.far)) for at in halves]
    tok_on = [sems.remote(tok.at[FAR, at], tok.at[DIAG, at], (p.dp, p.sib)) for at in halves]
    block = vec_all.at[p.z, p.x, p.inn]
    vec_i = [
        sems.remote(vec_own, block, (p.dp, other)) for other in (p.sib, p.far, p.diag)
    ]
    mine = vec_all.at[p.z, p.x]
    vec_x = [sems.remote(mine, mine, device) for _, device, _ in p.peers("x")]
    column = vec_all.at[p.z]
    vec_z = [sems.remote(column, column, device) for _, device, _ in p.peers("z")]
    unit_base = sems.n
    sems.n += 3

    def unit(r):
        u = 3 * p.inn + r
        away = pltpu.make_async_remote_copy(
            src_ref=units.at[r],
            dst_ref=unit_in.at[u // N_IN],
            send_sem=send.at[unit_base + r],
            recv_sem=recv.at[unit_base + u // N_IN],
            device_id=(p.dp, u % N_IN),
            device_id_type=MESH,
        )
        return u % N_IN == p.inn, u // N_IN, away

    def arrival(t):
        u = p.inn + N_IN * t
        bring = pltpu.make_async_remote_copy(
            src_ref=units.at[0],
            dst_ref=unit_in.at[t],
            send_sem=send.at[unit_base],
            recv_sem=recv.at[unit_base + t],
            device_id=(p.dp, p.far),
            device_id_type=MESH,
        )
        return u // 3 == p.inn, bring

    wq_block = wq_all.at[p.z, p.x]
    wq_z = [sems.remote(wq_block, wq_block, device) for _, device, _ in p.peers("z")]
    wq_x = []
    for k in range(N_Z):
        spot = wq_all.at[(p.z + N_Z - k) % N_Z, p.x]
        wq_x.append([sems.remote(spot, spot, device) for _, device, _ in p.peers("x")])
    swap = [
        sems.remote(low_ref.at[s], mixed.at[p.inn], (p.dp, p.slots[s])) for s in (DIAG, FAR, SIB)
    ]
    swap_own = sems.copy(low_ref.at[OWN], mixed.at[p.inn])
    saves = [
        sems.copy(ref, out)
        for ref, out in (
            (h_ref, h_out),
            (n_ref, n_out),
            (q_ref, q_out),
            (v_ref, v_out),
        )
    ]
    late_saves = [sems.copy(att_ref, att_out), sems.copy(kt_ref, kt_out)]

    near = partners(p, "zxyc", diagonal=True)
    arrive(near)
    own_tok.start()
    vec_own[...] = jnp.zeros_like(vec_own)
    for r, length in enumerate(lens):
        vec_own[r : r + 1, 0:length] = vec_in[r][...].astype(F32)
    for r in range(3):
        units[r] = w_qkv[:, r * CW : (r + 1) * CW]

    all_in(near)
    start(vec_i)
    for r in range(3):
        stays, t, away = unit(r)

        @pl.when(jnp.logical_not(stays))
        def _():
            away.start()

        @pl.when(stays)
        def _():
            unit_in[t] = units[r]

    start(tok_far)
    tok_sib.start()
    vec_all[p.z, p.x, p.inn] = vec_own[...]
    down0.step(0)
    out_pack[...] = pack(w_out[...]) if packs(w_out.shape[0]) else w_out[...]
    small.step(0)
    for t in range(3):
        stays, bring = arrival(t)

        @pl.when(jnp.logical_not(stays))
        def _():
            bring.wait_recv()

        wq_all[p.z, p.x, :, t * CW : (t + 1) * CW] = unit_in[t]
    start(wq_z)
    start(wq_x[0])
    wait_recv(vec_i)
    start(vec_x)
    wait_recv(vec_x)
    start(vec_z)
    for k in range(1, N_Z):
        wq_z[k - 1].wait_recv()
        start(wq_x[k])
    up1.step(0)
    up0.step(0)
    down1.step(0)
    wait_recv(vec_z)

    blocks = vec_all[...].reshape(n_dev * 8, LANES)
    shared = spread(blocks, lens[GAIN_ONE], D)
    gain, shift = shared[GAIN_ONE : GAIN_ONE + 1], shared[SHIFT_ONE : SHIFT_ONE + 1]
    bias_q = spread(blocks, lens[BIAS_QV], CW, p.inn * CW)[BIAS_QV : BIAS_QV + 1] * SCALE
    bias_v = spread(blocks, lens[BIAS_QV], CW, D + p.inn * CW)[BIAS_QV : BIAS_QV + 1]
    blank = jnp.zeros((1, HEAD_DIM), F32)

    def beside(row, h):
        return jnp.concatenate([row[:, h * HEAD_DIM : (h + 1) * HEAD_DIM], blank], axis=1)

    def norm(s, first=0, size=rows):
        here = pl.ds(s * rows + first, size)
        normed, _ = norm_parts(tok[s, first : first + size, :].astype(F32))
        h_ref[here, :] = (normed * gain + shift).astype(BF16)
        n_ref[here, :] = normed.astype(BF16)

    def heads(s, first=0, size=rows):
        here = pl.ds(s * rows + first, size)
        place_of = p.slots[s] * rows + first
        end_one = lengths[0, 0]
        end_two = end_one + lengths[0, 1]
        index = lax.broadcasted_iota(jnp.int32, (size, LANES), 0) + place_of
        lane = lax.broadcasted_iota(jnp.int32, (size, LANES), 1) - HEAD_DIM
        item = jnp.where(index >= end_one, 1, 0) + jnp.where(index >= end_two, 1, 0)
        same = jnp.where(lane == item, 1.0, 0.0)
        inside = jnp.logical_and(lane >= 0, lane < 3)
        other = jnp.where(jnp.logical_and(lane != item, inside), NEG, 0.0)
        ones = jnp.where(jnp.logical_and(lane >= 0, lane < 2), 1.0, 0.0)
        qkv = product(h_ref[here, :], w_wide[...])
        for h in range(HP):
            q, k, v = (qkv[:, (t * HP + h) * LANES : (t * HP + h + 1) * LANES] for t in range(3))
            q_ref[h, here, :] = (q + (same + beside(bias_q, h))).astype(BF16)
            k_ref[h, here, :] = (k + other).astype(BF16)
            v_aug = (v + (ones + beside(bias_v, h))).astype(BF16)
            v_ref[h, here, :] = v_aug
            vt_ref[h, :, here] = v_aug.T

    own_tok.wait()
    norm(OWN)
    tok_sib.wait_recv()
    norm(SIB)
    tok_far[0].wait_recv()
    tok_on[0].start()
    norm(FAR, 0, half_rows)
    for copies in wq_x:
        wait_recv(copies)
    down0.step(1)
    small.step(1)
    if w_qkv.shape[0] % 16 == 0:
        wq_full[...] = wq_all[...].reshape(D, 3 * CW)
    else:
        rows_of = [wq_all[z, x].astype(F32) for z in range(N_Z) for x in range(p.n_x)]
        wq_full[...] = jnp.concatenate(rows_of, axis=0).astype(BF16)
    for i in range(3 * HP):
        value = wq_full[:, i * HEAD_DIM : (i + 1) * HEAD_DIM]
        if i < HP:
            value = value * BF16(SCALE)
        w_wide[:, i * LANES : (i + 1) * LANES] = jnp.concatenate(
            [value, jnp.zeros_like(value)], axis=1
        )
    heads(OWN)
    up1.step(1)
    heads(SIB)
    tok_far[1].wait_recv()
    tok_on[1].start()
    norm(FAR, half_rows, half_rows)
    heads(FAR)
    up0.step(1)
    for i in range(2):
        tok_on[i].wait_recv()
        norm(DIAG, i * half_rows, half_rows)
    heads(DIAG)
    down0.step(2)
    start(saves)

    items = N_IN * HP

    def spill(it, slot):
        h, qb = it % HP, it // HP
        return pltpu.make_async_copy(
            e_ref.at[slot],
            e_out.at[h, :, pl.ds(pl.multiple_of(qb * BQ, BQ), BQ)],
            e_sem.at[slot],
        )

    actions = {
        0: [(down1, 1), (small, 2)],
        1: [(up0, 2), (up1, 2)],
        3: [(down1, 2)],
        7: [(up0, 3)],
        9: [(up1, 3), (up0, 4)],
    }

    def body(it, _):
        slot = it % 2
        h, qb = it % HP, it // HP
        here = pl.ds(pl.multiple_of(qb * BQ, BQ), BQ)

        @pl.when(it >= 2)
        def _():
            spill(it - 2, slot).wait()

        kt_ref[h, :, here] = k_ref[h, here, :].T[0:HEAD_DIM]
        q = q_ref[h, here, :]
        top = None
        for c in range(total // CK):
            cs = slice(c * CK, (c + 1) * CK)
            scores = product_nt(k_ref[h, cs, :], q)
            s_ref[cs, :] = scores
            peak = jnp.max(scores, axis=0, keepdims=True)
            top = peak if top is None else jnp.maximum(top, peak)
        acc = None
        for c in range(total // CK):
            cs = slice(c * CK, (c + 1) * CK)
            expo = jnp.exp(s_ref[cs, :] - top).astype(BF16)
            e_ref[slot, cs, :] = expo
            term = product(vt_ref[h, :, cs], expo)
            acc = term if acc is None else acc + term
        spill(it, slot).start()
        wide = acc.T
        sums = wide[:, HEAD_DIM : HEAD_DIM + 1]
        lane = lax.broadcasted_iota(jnp.int32, wide.shape, 1)
        att_ref[h, here, :] = jnp.where(lane < HEAD_DIM, wide / sums, wide)

        @pl.when(h == HP - 1)
        def _():
            low_ref[qb] = pack(
                jnp.concatenate([att_ref[i, here, 0:HEAD_DIM] for i in range(HP)], axis=1)
            ).astype(BF16)

        for when, acts in actions.items():

            @pl.when(it == when)
            def _():
                for which, number in acts:
                    which.step(number)

        for s in range(N_IN - 1):

            @pl.when(it == s * HP + HP - 1)
            def _():
                swap[s].start()

        return 0

    lax.fori_loop(0, items, body, 0)
    swap_own.start()
    start(late_saves)
    down0.step(3)
    down1.step(3)
    small.step(3)
    up1.step(4)
    down1.step(4)
    down0.step(4)
    small.step(4)
    wait(swap)
    swap_own.wait()
    wait(saves)
    wait(late_saves)
    for it in (items - 2, items - 1):
        spill(it, it % 2).wait()
    for item in pieces:
        item.finish()
    for r in range(3):
        stays, _, away = unit(r)

        @pl.when(jnp.logical_not(stays))
        def _():
            away.wait_send()

    wait_send(tok_far + tok_on + [tok_sib] + vec_i + vec_x + vec_z + wq_z)
    for copies in wq_x:
        wait_send(copies)


def forward(n_dp, tokens, lengths, w_qkv, vectors, w_out, w_up, w_down):
    n_x = n_dp // N_Z
    rows = tokens.shape[0]
    total = N_IN * rows
    lens = tuple(v.shape[0] for v in vectors)
    w_rows = w_qkv.shape[0]
    wide = (HP, total, LANES)

    def whole(shape):
        return jax.ShapeDtypeStruct((N_IN, N_Z, n_x) + shape, BF16)

    out_shape = packed_shape(*w_out.shape)

    n_remote = 5 + 3 + 3 + (1 + N_Z) * (n_x - 1) + 2 * (N_Z - 1) + 3
    n_remote += sum(gather_count(n_x, order) for order in GATHER_ORDERS.values())
    return pl.pallas_call(
        functools.partial(forward_kernel, n_dp, lens),
        out_shape=(
            jax.ShapeDtypeStruct((total, D), BF16),
            jax.ShapeDtypeStruct((total, D), BF16),
            jax.ShapeDtypeStruct(wide, BF16),
            jax.ShapeDtypeStruct(wide, BF16),
            jax.ShapeDtypeStruct((HP, HEAD_DIM, total), BF16),
            jax.ShapeDtypeStruct(wide, F32),
            jax.ShapeDtypeStruct((HP, total, total), BF16),
            jax.ShapeDtypeStruct((N_IN,) + packed_shape(rows, CW), BF16),
            whole(out_shape),
            whole(w_up.shape),
            whole(w_down.shape),
            jax.ShapeDtypeStruct((N_Z, n_x, N_IN, 8, LANES), F32),
            jax.ShapeDtypeStruct((D, 3 * CW), BF16),
        ),
        in_specs=[ANY, SMEM, VMEM] + [VMEM] * 8 + [VMEM, ANY, VMEM],
        out_specs=(ANY,) * 11 + (VMEM,) * 2,
        scratch_shapes=[
            pltpu.VMEM((N_IN, rows, D), BF16),
            pltpu.VMEM((total, D), BF16),
            pltpu.VMEM((total, D), BF16),
            pltpu.VMEM(wide, BF16),
            pltpu.VMEM(wide, BF16),
            pltpu.VMEM((HP, HEAD_DIM, total), BF16),
            pltpu.VMEM(wide, F32),
            pltpu.VMEM(wide, BF16),
            pltpu.VMEM((HP, LANES, total), BF16),
            pltpu.VMEM((total, BQ), F32),
            pltpu.VMEM((2, total, BQ), BF16),
            pltpu.VMEM((N_IN,) + packed_shape(rows, CW), BF16),
            pltpu.VMEM((3, w_rows, CW), BF16),
            pltpu.VMEM((3, w_rows, CW), BF16),
            pltpu.VMEM((D, 3 * HP * LANES), BF16),
            pltpu.VMEM((N_Z, n_x, w_rows, 3 * CW), BF16),
            pltpu.VMEM((8, LANES), F32),
            pltpu.VMEM(out_shape, BF16),
            pltpu.SemaphoreType.DMA((2,)),
        ]
        + sem_shapes(n_remote, 13),
        compiler_params=params(0),
        name="forward",
    )(tokens, lengths, w_qkv, *[v.reshape(1, -1) for v in vectors], w_out, w_up, w_down)


HC = 768
GC = 768


def add_rows(total, terms, out=None):
    step = 128

    def one(i, _):
        at = pl.ds(pl.multiple_of(i * step, step), step)
        if out is None:
            value = total[at, :]
            for term in terms:
                value = value + term[at, :]
            total[at, :] = value
        else:
            value = total[at, :].astype(F32)
            for term in terms:
                value = value + term[at, :].astype(F32)
            out[at, :] = value
        return 0

    lax.fori_loop(0, total.shape[0] // step, one, 0)


def add_blocks(total, term):
    if len(total.shape) == 2:
        add_rows(total, [term])
        return

    def one(i, _):
        total[i] = total[i] + term[i]
        return 0

    lax.fori_loop(0, total.shape[0], one, 0)


def unpack_into(out, parts, rows):
    half = rows // 2
    packed = parts.shape[-1] == 2 * CW

    def one(d, _):
        for i in range(N_IN):
            cols = slice(i * CW, (i + 1) * CW)
            if packed:
                first = pl.ds(pl.multiple_of(d * rows, 16), half)
                second = pl.ds(pl.multiple_of(d * rows + half, 16), half)
                out[first, cols] = parts[i, d, :, 0:CW]
                out[second, cols] = parts[i, d, :, CW : 2 * CW]
            else:
                at = pl.ds(pl.multiple_of(d * LANES, LANES), LANES)
                out[at, cols] = parts[i, at, :]
        return 0

    lax.fori_loop(0, out.shape[0] // (rows if packed else LANES), one, 0)


def pack_into(parts, value, rows, first):
    for i in range(N_IN):
        cols = slice(i * CW, (i + 1) * CW)
        if parts.shape[-1] == 2 * CW:
            for b in range(value.shape[0] // rows):
                parts[i, first + b] = pack(value[b * rows : (b + 1) * rows, cols])
        else:
            parts[i] = value[:, cols]


def middle_kernel(
    n_dp,
    lens,
    tokens,
    mixed,
    a_out,
    a_up,
    a_down,
    vec_all,
    cotangent,
    output,
    d_res_out,
    seen,
    t_out,
    t_up,
    t_down,
    sums,
    sum_up,
    tok,
    mix,
    po,
    pu,
    pd,
    cot,
    fo,
    fd,
    att,
    res,
    n_two,
    h_two,
    act,
    d_up,
    b_up,
    d_mixed,
    d_res,
    out_ref,
    d_att,
    co,
    cu,
    cd,
    h_turned,
    cot_turned,
    send,
    recv,
    local,
):
    p = Place(n_dp)
    n_dev = n_dp * N_IN
    sems = Sems(send, recv, local)
    rows = tokens.shape[0]
    ff = a_up.shape[0] * a_up.shape[2]
    r_out, r_down = D // n_dp, a_down.shape[3]
    loads = {
        name: sems.copy(src, dst)
        for name, src, dst in (
            ("out", a_out, po),
            ("mix", mixed, mix),
            ("tok", tokens, tok),
            ("up", a_up, pu),
            ("cot", cotangent, cot),
        )
    }
    direct = r_down % LANES == 0
    if direct:
        down_loads = [
            sems.copy(a_down.at[i, d], fd.at[pl.ds(i * CW, CW), pl.ds(d * r_down, r_down)])
            for i in range(N_IN)
            for d in range(n_dp)
        ]
    else:
        down_loads = [sems.copy(a_down, pd)]
    start(list(loads.values()) + down_loads)
    swap = [
        sems.remote(d_att.at[p.slots[s]], seen.at[s], (p.dp, p.slots[s])) for s in (DIAG, FAR, SIB)
    ]
    swap_own = sems.copy(d_att.at[p.inn], seen.at[OWN])

    def across(parts, buffer):
        return [
            sems.remote(parts.at[2 * yy + 1 - p.c], buffer.at[yy], (p.dp, p.sib))
            for yy in range(2)
        ]

    core_up, core_down, core_out = across(pu, cu), across(pd, cd), across(po, co)
    keeps = {
        name: [sems.copy(parts.at[2 * yy + p.c], out.at[yy]) for yy in range(2)]
        for name, parts, out in (("up", pu, t_up), ("down", pd, t_down), ("out", po, t_out))
    }
    out_save = sems.copy(out_ref, output)
    res_save = sems.copy(d_res, d_res_out)

    near = partners(p, "yc", diagonal=True)
    arrive(near)
    blocks = vec_all[...].reshape(n_dev * 8, LANES)
    shared = spread(blocks, lens[BIAS_OUT], D)
    for c in range(ff // D):
        b_up[:, c * D : (c + 1) * D] = spread(blocks, lens[BIAS_UP], D, c * D)[
            BIAS_UP : BIAS_UP + 1
        ]

    loads["out"].wait()
    loads["mix"].wait()
    unpack_into(fo, po, r_out)
    half = rows // 2
    for i in range(N_IN):
        cols = slice(i * CW, (i + 1) * CW)
        att[0:half, cols] = mix[i, :, 0:CW]
        att[half:rows, cols] = mix[i, :, CW : 2 * CW]
    loads["tok"].wait()
    residual = (
        tok[...].astype(F32) + product(att[...], fo[...]) + shared[BIAS_OUT : BIAS_OUT + 1]
    )
    res[...] = residual
    normed, factor = norm_parts(residual)
    n_two[...] = normed
    gain = shared[GAIN_TWO : GAIN_TWO + 1]
    h_two[...] = (normed * gain + shared[SHIFT_TWO : SHIFT_TWO + 1]).astype(BF16)
    wait(down_loads)
    if not direct:
        for i in range(N_IN):
            for d in range(n_dp):
                fd[i * CW : (i + 1) * CW, d * r_down : (d + 1) * r_down] = pd[i, d]
    loads["up"].wait()
    loads["cot"].wait()

    def hidden(it, _):
        hid = pl.ds(pl.multiple_of(it * HC, HC), HC)
        inside = pl.ds(pl.multiple_of(it % (D // HC) * HC, HC), HC)
        up = product(h_two[...], pu[it // (D // HC), :, inside]) + b_up[:, hid]
        d_act = product(cot[...], fd[:, hid])
        cdf = 0.5 * (1.0 + lax.erf(up * 0.7071067811865476))
        pdf = jnp.exp(-0.5 * up * up) * 0.3989422804014327
        act[:, hid] = (up * cdf).astype(BF16)
        grad = (d_act * (cdf + up * pdf)).astype(BF16)
        d_up[:, hid] = grad
        sum_up[:, hid] = jnp.sum(grad.astype(F32), axis=0, keepdims=True)
        return 0

    lax.fori_loop(0, ff // HC, hidden, 0)

    dh_two = None
    for i in range(N_IN):
        term = product_nt(d_up[:, i * D : (i + 1) * D], pu[i])
        dh_two = term if dh_two is None else dh_two + term
    normed = n_two[...]
    upstream = cot[...].astype(F32)
    value = upstream + norm_backward(dh_two, normed, factor, gain)
    d_res[...] = value
    res_save.start()
    low = value.astype(BF16)
    d_mixed[...] = low
    grad_att = product_nt(low, fo[...]).astype(BF16)
    for i in range(N_IN):
        d_att[i] = pack(grad_att[:, i * CW : (i + 1) * CW])
    all_in(near)
    start(swap)
    swap_own.start()

    def grad_up(i):
        cols = pl.ds(pl.multiple_of(i * D, D), D)
        pu[i] = product(h_turned[...], d_up[:, cols]).astype(BF16)

    h_turned[...] = h_two[...].T
    cot_turned[...] = cot[...].T
    for yy in range(2):
        grad_up(2 * yy + 1 - p.c)
    start(core_up)

    def grad_down(it, _):
        hid = pl.ds(pl.multiple_of(it * GC, GC), GC)
        value = product(cot_turned[...], act[:, hid]).astype(BF16)
        for i in range(N_IN):
            for b in range(GC // r_down):
                cols = slice(b * r_down, (b + 1) * r_down)
                pd[i, it * (GC // r_down) + b] = value[i * CW : (i + 1) * CW, cols]
        return 0

    lax.fori_loop(0, ff // GC, grad_down, 0)
    start(core_down)
    pack_into(po, product_tn(att[...], d_mixed[...]).astype(BF16), r_out, 0)
    start(core_out)
    for yy in range(2):
        grad_up(2 * yy + p.c)

    def output_part(n, _):
        cols = pl.ds(pl.multiple_of(n * HC, HC), HC)
        value = product_nt(act[...], fd[cols, :]) + res[:, cols]
        out_ref[:, cols] = value.astype(BF16)
        return 0

    res[...] = res[...] + shared[BIAS_DOWN : BIAS_DOWN + 1]
    lax.fori_loop(0, D // HC, output_part, 0)
    out_save.start()

    sums[...] = jnp.zeros_like(sums)
    sums[BIAS_OUT : BIAS_OUT + 1, :] = jnp.sum(low.astype(F32), axis=0, keepdims=True)
    sums[BIAS_DOWN : BIAS_DOWN + 1, :] = jnp.sum(upstream, axis=0, keepdims=True)
    sums[GAIN_TWO : GAIN_TWO + 1, :] = jnp.sum(dh_two * normed, axis=0, keepdims=True)
    sums[SHIFT_TWO : SHIFT_TWO + 1, :] = jnp.sum(dh_two, axis=0, keepdims=True)
    for copies, parts, buffer, name in (
        (core_up, pu, cu, "up"),
        (core_down, pd, cd, "down"),
        (core_out, po, co, "out"),
    ):
        wait_recv(copies)
        for yy in range(2):
            add_blocks(parts.at[2 * yy + p.c], buffer.at[yy])
        start(keeps[name])
    wait(swap)
    swap_own.wait()
    for copies in (core_up, core_down, core_out):
        wait_send(copies)
    for copies in keeps.values():
        wait(copies)
    out_save.wait()
    res_save.wait()


def middle(n_dp, lens, tokens, mixed, a_out, a_up, a_down, vec_all, cotangent):
    rows = tokens.shape[0]
    ff = a_up.shape[0] * a_up.shape[2]
    out_parts, up_parts, down_parts = a_out.shape[1:], a_up.shape[1:], a_down.shape[1:]
    return pl.pallas_call(
        functools.partial(middle_kernel, n_dp, lens),
        out_shape=(
            jax.ShapeDtypeStruct((rows, D), BF16),
            jax.ShapeDtypeStruct((rows, D), F32),
            jax.ShapeDtypeStruct((N_IN,) + packed_shape(rows, CW), BF16),
            jax.ShapeDtypeStruct((2,) + out_parts, BF16),
            jax.ShapeDtypeStruct((2,) + up_parts, BF16),
            jax.ShapeDtypeStruct((2,) + down_parts, BF16),
            jax.ShapeDtypeStruct((8, D), F32),
            jax.ShapeDtypeStruct((1, ff), F32),
        ),
        in_specs=[ANY] * 5 + [VMEM, ANY],
        out_specs=(ANY,) * 6 + (VMEM,) * 2,
        scratch_shapes=[
            pltpu.VMEM((rows, D), BF16),
            pltpu.VMEM((N_IN,) + packed_shape(rows, CW), BF16),
            pltpu.VMEM((N_IN,) + out_parts, BF16),
            pltpu.VMEM((N_IN,) + up_parts, BF16),
            pltpu.VMEM((N_IN,) + down_parts, BF16),
            pltpu.VMEM((rows, D), BF16),
            pltpu.VMEM((D, D), BF16),
            pltpu.VMEM((D, ff), BF16),
            pltpu.VMEM((rows, D), BF16),
            pltpu.VMEM((rows, D), F32),
            pltpu.VMEM((rows, D), F32),
            pltpu.VMEM((rows, D), BF16),
            pltpu.VMEM((rows, ff), BF16),
            pltpu.VMEM((rows, ff), BF16),
            pltpu.VMEM((1, ff), F32),
            pltpu.VMEM((rows, D), BF16),
            pltpu.VMEM((rows, D), F32),
            pltpu.VMEM((rows, D), BF16),
            pltpu.VMEM((N_IN,) + packed_shape(rows, CW), BF16),
            pltpu.VMEM((2,) + out_parts, BF16),
            pltpu.VMEM((2,) + up_parts, BF16),
            pltpu.VMEM((2,) + down_parts, BF16),
            pltpu.VMEM((D, rows), BF16),
            pltpu.VMEM((D, rows), BF16),
        ]
        + sem_shapes(9, 14 + N_IN * n_dp),
        compiler_params=params(1),
        name="middle",
    )(tokens, mixed, a_out, a_up, a_down, vec_all, cotangent)


BK = 640
CQ = 1280
SCATTER_ORDERS = ("yxz", "xyz", "yxz", "xyz", "zyx")


class Scatter:
    def __init__(self, place, sems, blocks, order, buffers, out):
        self.order, self.out = order, out
        p = place
        self.total, self.buffers = buffers[0], dict(zip(order, buffers[1:]))
        self.load = sems.copy(blocks, self.total)
        _, _, n_x, _, _ = self.total.shape
        where = {"y": pl.ds(0, 2), "z": pl.ds(0, N_Z), "x": pl.ds(0, n_x)}
        own = {"y": p.y, "z": p.z, "x": p.x}
        self.copies, self.regions = {}, {}
        for axis in order:
            copies = []
            for at, device, k in p.peers(axis):
                there = dict(where)
                there[axis] = pl.ds(at, 1)
                src = self.total.at[there["y"], there["z"], there["x"]]
                copies.append(sems.remote(src, self.buffers[axis].at[k - 1], device))
            self.copies[axis] = copies
            where[axis] = pl.ds(own[axis], 1)
            self.regions[axis] = (where["y"], where["z"], where["x"])

    def step(self, number):
        if number == 0:
            self.load.start()
            return
        if number == 1:
            self.load.wait()
        else:
            axis = self.order[number - 2]
            wait_recv(self.copies[axis])
            region, buffer = self.total.at[self.regions[axis]], self.buffers[axis]
            if number - 1 == len(self.order):
                value = region[0, 0, 0].astype(F32)
                for k in range(buffer.shape[0]):
                    value = value + buffer[k, 0, 0, 0].astype(F32)
                self.out(value)
                return
            _, n_y, n_z, n_x, _, _ = buffer.shape

            def one(i, _):
                for y in range(n_y):
                    for x in range(n_x):
                        value = region[y, i, x]
                        for k in range(buffer.shape[0]):
                            value = value + buffer[k, y, i, x]
                        region[y, i, x] = value
                return 0

            lax.fori_loop(0, n_z, one, 0)
        start(self.copies[self.order[number - 1]])

    def finish(self):
        for axis in self.order:
            wait_send(self.copies[axis])


def scatter_buffers(n_x, rows, cols, order):
    sizes = {"y": 2, "z": N_Z, "x": n_x}
    shapes = [(2, N_Z, n_x, rows, cols)]
    left = dict(sizes)
    for axis in order:
        left[axis] = 1
        shapes.append((sizes[axis] - 1, left["y"], left["z"], left["x"], rows, cols))
    return [pltpu.VMEM(shape, BF16) for shape in shapes]


def scatter_count(n_x):
    return 1 + (N_Z - 1) + (n_x - 1)


def backward_kernel(n_dp, lens, *rest):
    (
        tokens,
        seen_in,
        att_in,
        e_all,
        q_in,
        v_in,
        kt_in,
        h_in,
        n_in,
        wq_in,
        d_res_in,
        t_out,
        t_up,
        t_down,
        vec_all,
        sums,
        sum_up,
    ) = rest[:17]
    grad_tokens, g_qkv, s_out, s_up, s_down = rest[17:22]
    vec_outs = rest[22:30]
    (
        seen,
        att,
        q_ref,
        v_ref,
        kt_ref,
        h_ref,
        n_ref,
        wq_ref,
        d_res,
        do_ref,
        dqt_ref,
        e_ref,
        d_all,
        t_core,
        t_far,
        g_w,
        norm_sums,
        w_own,
        w_x,
        w_in,
        v_own,
        v_all,
        v_y,
        v_c,
    ) = rest[30:54]
    buffers = rest[54:74]
    e_sem, send, recv, local = rest[74:]
    p = Place(n_dp)
    n_dev, n_x = n_dp * N_IN, n_dp // N_Z
    sems = Sems(send, recv, local)
    rows = tokens.shape[0]
    total = N_IN * rows
    n_down = t_down.shape[3]
    half_down = first_rows(n_down)
    half_up = t_up.shape[4] // 2

    def put(out, first):
        def write(value):
            size, cols = value.shape
            if cols == 2 * CW and out.shape[1] == CW:
                out[0:size, :] = value[:, 0:CW]
                out[size:, :] = value[:, CW:]
            elif cols == out.shape[1]:
                out[first : first + size, :] = value
            else:
                out[:, first : first + cols] = value

        return write

    near = partners(p, "yc", diagonal=True)
    others = [(p.dp + k) % n_dp for k in range(1, n_dp)]
    for k, dp in enumerate(others, 1):
        near += [(dp, inn) for inn in range(N_IN)] if k % n_x == 0 else [(dp, p.inn)]
    arrive(near)
    loads = {
        name: sems.copy(src, dst)
        for name, src, dst in (
            ("seen", seen_in, seen),
            ("att", att_in, att),
            ("v", v_in, v_ref),
            ("kt", kt_in, kt_ref),
            ("q", q_in, q_ref),
            ("wq", wq_in, wq_ref),
            ("res", d_res_in, d_res),
        )
    }
    for name in ("seen", "att"):
        loads[name].start()
    pieces = []
    for number, (ref, out, first, size, axis) in enumerate(
        (
            (t_down, s_down, 0, half_down, 0),
            (t_down, s_down, half_down, n_down - half_down, 0),
            (t_up, s_up, 0, half_up, 1),
            (t_up, s_up, half_up, half_up, 1),
            (t_out, s_out, 0, t_out.shape[3], 0),
        )
    ):
        pieces.append(
            Scatter(
                p,
                sems,
                part(ref, first, size, axis),
                SCATTER_ORDERS[number],
                buffers[4 * number : 4 * number + 4],
                put(out, first),
            )
        )
    down0, down1, up0, up1, small = pieces

    def room(i):
        return e_ref.at[i, :, pl.ds(0, D)]

    dh_far, dh_diag, dh_sib, dh_own = room(2), room(3), room(0), room(1)
    tok = n_ref.at[0]
    loads["tok"] = sems.copy(tokens, tok)

    def fetch(kb, h, half, slot):
        at = pl.ds(pl.multiple_of(kb * BK, BK), BK)
        src = e_all.at[h, at, pl.ds(half * CQ, CQ)]
        return pltpu.make_async_copy(src, e_ref.at[slot], e_sem.at[slot])

    fetch(0, 0, 0, 0).start()
    fetch(0, 0, 1, 1).start()
    feeds = []
    for s in range(N_IN):
        at = pl.ds(s * rows, rows)
        feeds.append(
            [sems.copy(n_in.at[at], n_ref.at[s % 2]), sems.copy(h_in.at[at], h_ref.at[s % 2])]
        )
    for name in ("v", "kt", "q"):
        loads[name].start()
    for item in (down0, down1, small, up0, up1):
        item.step(0)
    for feed in feeds[0:2]:
        start(feed)
    for name in ("wq", "res"):
        loads[name].start()
    here, there = (p.dp, p.sib), (p.dp, p.far)
    give_diag = sems.remote(dh_diag, t_core.at[1], here)
    give_sib = sems.remote(dh_sib, t_core.at[0], here)
    across = sems.remote(dh_far, t_far, there)
    w_order = tuple(range(1, N_Z)) + (0,)
    w_to_x = {}
    for kz in w_order:
        w_to_x[kz] = [
            sems.remote(w_own.at[(p.z + kz) % N_Z, at], w_x.at[k - 1, kz], device)
            for at, device, k in p.peers("x")
        ]
    v_to_c = [
        sems.remote(v_own.at[:, :, 2 * yy + 1 - p.c], v_c.at[yy], here) for yy in range(2)
    ]
    v_to_y = sems.remote(v_own.at[:, :, p.far], v_y, there)
    v_to_all = [
        sems.remote(v_own.at[dp // n_x, dp % n_x, p.inn], v_all.at[k], (dp, p.inn))
        for k, dp in enumerate(others)
    ]
    unit_base = sems.n

    def unit(t, kz):
        u = p.inn + N_IN * t
        owner, r = u // 3, u % 3
        at = (p.z + kz) % N_Z
        away = pltpu.make_async_remote_copy(
            src_ref=w_own.at[at, p.x, t],
            dst_ref=w_in.at[r, kz],
            send_sem=send.at[unit_base + t * N_Z + kz],
            recv_sem=recv.at[unit_base + r * N_Z + kz],
            device_id=(at * n_x + p.x, owner),
            device_id_type=MESH,
        )
        return owner == p.inn, r, away

    def arrival(r, kz):
        bring = pltpu.make_async_remote_copy(
            src_ref=w_own.at[p.z, p.x, 0],
            dst_ref=w_in.at[r, kz],
            send_sem=send.at[unit_base],
            recv_sem=recv.at[unit_base + r * N_Z + kz],
            device_id=(p.dp, p.far),
            device_id_type=MESH,
        )
        return (3 * p.inn + r) % N_IN == p.inn, bring

    dqt_ref[...] = jnp.zeros_like(dqt_ref)
    loads["seen"].wait()
    loads["att"].wait()
    for s in range(N_IN):
        if s == 1:
            all_in(near)
            for item in (down0, down1, small, up0, up1):
                item.step(1)
        at = pl.ds(s * rows, rows)
        for h in range(HP):
            grad = jnp.concatenate(
                [
                    seen[s, :, side * CW + h * HEAD_DIM : side * CW + (h + 1) * HEAD_DIM]
                    for side in range(2)
                ],
                axis=0,
            ).astype(F32)
            both = att[h, at, :]
            scale = SCALE / both[:, HEAD_DIM : HEAD_DIM + 1]
            delta = jnp.sum(grad * both[:, 0:HEAD_DIM], axis=-1, keepdims=True) * -scale
            high = delta.astype(BF16).astype(F32)
            lane = lax.broadcasted_iota(jnp.int32, (rows, HEAD_DIM), 1)
            tail = jnp.where(lane == 0, high, jnp.where(lane == 1, delta - high, 0.0))
            do_ref[h, at, :] = jnp.concatenate([grad * scale, tail], axis=1).astype(BF16)
    for name in ("v", "kt", "q"):
        loads[name].wait()

    actions = {
        3: [(small, 2), (down0, 2), (down1, 2)],
        7: [(small, 3), (up0, 2), (up1, 2)],
        9: [(down0, 3), (down1, 3), (small, 4)],
        14: [(down0, 4), (down1, 4)],
    }
    last = N_IN - 1
    root = HEAD_DIM**0.5

    def act(kb, first, number):
        for when, acts in actions.items():
            if when in (number, number + HP):

                @pl.when(kb == first + (when - number) // HP)
                def _():
                    for which, stage in acts:
                        which.step(stage)

    def piece(kb, h, half, slot):
        at = pl.ds(pl.multiple_of(kb * BK, BK), BK)
        cs = slice(half * CQ, (half + 1) * CQ)
        expo, do = e_ref[slot], do_ref[h, cs, :]
        ds = (expo.astype(F32) * product_nt(v_ref[h, at, :], do)).astype(BF16)
        dv, dk = product(expo, do), product(ds, q_ref[h, cs, :])
        dqt_ref[h, :, cs] += product(kt_ref[h, :, at], ds)
        return dv, dk

    def head_cols(t, h):
        return slice(t * CW + h * HEAD_DIM, t * CW + (h + 1) * HEAD_DIM)

    def finish_keys(kb, h, dv, dk):
        at = pl.ds(pl.multiple_of(kb * BK, BK), BK)
        d_all[at, head_cols(1, h)] = (dk * root).astype(BF16)
        d_all[at, head_cols(2, h)] = (dv * root).astype(BF16)

    def both_halves(kb, _):
        for h in range(HP):
            slot = (kb * HP + h) % 2 * 2
            other = 2 - slot
            if h < HP - 1:
                for half in range(2):
                    fetch(kb, h + 1, half, other + half).start()
            else:

                @pl.when(kb == 0)
                def _():
                    for half in range(2):
                        fetch(1, 0, half, other + half).start()

                @pl.when(kb == 1)
                def _():
                    fetch(2, 0, 0, 0).start()

            for half in range(2):
                fetch(kb, h, half, slot + half).wait()
            dv0, dk0 = piece(kb, h, 0, slot)
            dv1, dk1 = piece(kb, h, 1, slot + 1)
            dv, dk = dv0 + dv1, dk0 + dk1
            finish_keys(kb, h, dv[:, 0:HEAD_DIM], dk[:, 0:HEAD_DIM])
            act(kb, 0, h)
        return 0

    lax.fori_loop(0, 2, both_halves, 0)

    def one_half(half, first):
        def run(kb, _):
            for h in range(HP):
                slot = ((kb - 2) * HP + h) % 2
                other = 1 - slot
                if h < HP - 1:
                    fetch(kb, h + 1, half, other).start()
                else:

                    @pl.when(kb == 2)
                    def _():
                        fetch(3, 0, half, other).start()

                    if half == 0:

                        @pl.when(kb == last)
                        def _():
                            fetch(2, 0, 1, other).start()

                fetch(kb, h, half, slot).wait()
                dv, dk = piece(kb, h, half, slot)
                at = pl.ds(pl.multiple_of(kb * BK, BK), BK)
                if half == 0:
                    att[h, at, :] = jnp.concatenate([dk[:, 0:HEAD_DIM], dv[:, 0:HEAD_DIM]], axis=1)
                else:
                    dk = dk[:, 0:HEAD_DIM] + att[h, at, 0:HEAD_DIM]
                    dv = dv[:, 0:HEAD_DIM] + att[h, at, HEAD_DIM:LANES]
                    finish_keys(kb, h, dv, dk)
                act(kb, 2, first + h)
            return 0

        lax.fori_loop(2, N_IN, run, 0)
        for h in range(HP):
            cs = slice(half * CQ, (half + 1) * CQ)
            d_all[cs, head_cols(0, h)] = dqt_ref[h, :, cs].T.astype(BF16)

    def input_grad(i):
        at = pl.ds(i * rows, rows)
        feeds[i][0].wait()
        value = product_nt(d_all[at, :], wq_ref[...])
        gain_sum = jnp.sum(value * n_ref[i % 2].astype(F32), axis=0, keepdims=True)
        shift_sum = jnp.sum(value, axis=0, keepdims=True)
        return value.astype(BF16), gain_sum, shift_sum

    def weight_grad(i):
        at = pl.ds(i * rows, rows)
        feeds[i][1].wait()
        return product_tn(h_ref[i % 2], d_all[at, :])

    one_half(0, 2 * HP)
    loads["wq"].wait()
    value, gain_sum, shift_sum = input_grad(DIAG)
    dh_diag[...] = value
    give_diag.start()
    value, g_sum, s_sum = input_grad(FAR)
    dh_far[...] = value
    norm_sums[0:1, :] = gain_sum + g_sum
    norm_sums[1:2, :] = shift_sum + s_sum
    g_w[...] = weight_grad(DIAG) + weight_grad(FAR)
    for feed in feeds[2:4]:
        start(feed)
    packed = unspread(sums[...], n_dev, lens[GAIN_ONE])
    row = lax.broadcasted_iota(jnp.int32, (8, D), 0)
    for c in range(sum_up.shape[1] // D):
        line = jnp.where(row == BIAS_UP, sum_up[:, c * D : (c + 1) * D], 0.0)
        packed = packed + unspread(line, n_dev, lens[BIAS_UP], c * D)
    v_own[...] = packed.reshape(N_Z, n_x, N_IN, 8, LANES)
    give_diag.wait_recv()
    add_rows(dh_far, [t_core.at[1]])
    across.start()
    up0.step(3)
    up1.step(3)
    one_half(1, 4 * HP)
    w_rows = D // n_dp
    wide = weight_grad(SIB) + weight_grad(OWN) + g_w[...]
    for t in range(3):
        value = wide[:, t * CW : (t + 1) * CW]
        value = value.astype(BF16) if packs(w_rows) else value
        for d in range(n_dp):
            block = value[d * w_rows : (d + 1) * w_rows]
            block = pack(block) if packs(w_rows) else block.astype(BF16)
            w_own[d // n_x, d % n_x, t] = block
    for kz in w_order:
        start(w_to_x[kz])
    def add_w(kz):
        wait_recv(w_to_x[kz])
        at = (p.z + kz) % N_Z
        value = w_own[at, p.x]
        for k in range(n_x - 1):
            value = value + w_x[k, kz]
        w_own[at, p.x] = value
        for t in range(3):
            stays, r, away = unit(t, kz)
            if kz:
                away.start()
            else:

                @pl.when(jnp.logical_not(stays))
                def _():
                    away.start()

                @pl.when(stays)
                def _():
                    w_in[r, 0] = value[t]

    value, gain_sum, shift_sum = input_grad(SIB)
    dh_sib[...] = value
    give_sib.start()
    loads["tok"].start()
    add_w(1)
    value, g_sum, s_sum = input_grad(OWN)
    dh_own[...] = value
    gain_sum = gain_sum + g_sum + norm_sums[0:1, :]
    shift_sum = shift_sum + s_sum + norm_sums[1:2, :]

    row = lax.broadcasted_iota(jnp.int32, (8, D), 0)
    wide = jnp.where(row == GAIN_ONE, gain_sum, jnp.where(row == SHIFT_ONE, shift_sum, 0.0))
    packed = unspread(wide, n_dev, lens[GAIN_ONE])
    row = lax.broadcasted_iota(jnp.int32, (8, CW), 0)
    for t, first in ((0, 0), (2, D)):
        line = d_all[:, t * CW : (t + 1) * CW].astype(F32)
        line = jnp.sum(line, axis=0, keepdims=True)
        line = jnp.where(row == BIAS_QV, line, 0.0)
        packed = packed + unspread(line, n_dev, lens[BIAS_QV], first + p.inn * CW)
    v_own[...] = v_own[...] + packed.reshape(N_Z, n_x, N_IN, 8, LANES)
    start(v_to_c)
    add_w(2)
    wait_recv(v_to_c)
    for yy in range(2):
        v_own[:, :, 2 * yy + p.c] = v_own[:, :, 2 * yy + p.c] + v_c[yy]
    v_to_y.start()
    add_w(3)
    v_to_y.wait_recv()
    v_own[:, :, p.inn] = v_own[:, :, p.inn] + v_y[...]
    start(v_to_all)
    up0.step(4)
    up1.step(4)
    add_w(0)
    give_sib.wait_recv()
    add_rows(dh_own, [t_core.at[0]])
    blocks = vec_all[...].reshape(n_dev * 8, LANES)
    gain = spread(blocks, lens[GAIN_ONE], D)[GAIN_ONE : GAIN_ONE + 1]
    loads["tok"].wait()
    loads["res"].wait()
    normed, factor = norm_parts(tok[...].astype(F32))
    for r in range(3):
        value = None
        for kz in range(N_Z):
            stays, bring = arrival(r, kz)
            if kz:
                bring.wait_recv()
            else:

                @pl.when(jnp.logical_not(stays))
                def _():
                    bring.wait_recv()

            term = w_in[r, kz].astype(F32)
            value = term if value is None else value + term
        cols = slice(r * CW, (r + 1) * CW)
        if packs(w_rows):
            g_qkv[0 : w_rows // 2, cols] = value[:, 0:CW]
            g_qkv[w_rows // 2 :, cols] = value[:, CW:]
        else:
            g_qkv[:, cols] = value
    wait_recv(v_to_all)
    final = v_own[p.z, p.x, p.inn]
    for k in range(n_dp - 1):
        final = final + v_all[k]
    for r, length in enumerate(lens):
        vec_outs[r][...] = final[r : r + 1, 0:length]
    across.wait_recv()
    grad = dh_own[...].astype(F32) + t_far[...].astype(F32)
    grad_tokens[...] = (d_res[...] + norm_backward(grad, normed, factor, gain)).astype(BF16)
    for t in range(3):
        for kz in range(N_Z):
            stays, _, away = unit(t, kz)
            if kz:
                away.wait_send()
            else:

                @pl.when(jnp.logical_not(stays))
                def _():
                    away.wait_send()

    wait_send([give_diag, give_sib, across, v_to_y])
    wait_send(v_to_c + v_to_all)
    for kz in w_order:
        wait_send(w_to_x[kz])
    for item in pieces:
        item.finish()


def backward(n_dp, lens, like_out, like_down, tokens, seen, att, e_all, q, v, kt, h_one, n_one, wq, d_res, *grads):
    t_out, t_up, t_down, vec_all, sums, sum_up = grads
    n_x = n_dp // N_Z
    rows = tokens.shape[0]
    total = N_IN * rows
    w_rows = D // n_dp
    w_block = packed_shape(w_rows, CW)
    r_down, c_down = t_down.shape[3:]
    r_up, c_up = t_up.shape[3:]
    r_first = first_rows(r_down)
    sizes = [(r_first, c_down), (r_down - r_first, c_down)]
    sizes += [(r_up, c_up // 2)] * 2 + [t_out.shape[3:]]
    scratch = [
        pltpu.VMEM((N_IN,) + packed_shape(rows, CW), BF16),
        pltpu.VMEM((HP, total, LANES), F32),
        pltpu.VMEM((HP, total, LANES), BF16),
        pltpu.VMEM((HP, total, LANES), BF16),
        pltpu.VMEM((HP, HEAD_DIM, total), BF16),
        pltpu.VMEM((2, rows, D), BF16),
        pltpu.VMEM((2, rows, D), BF16),
        pltpu.VMEM((D, 3 * CW), BF16),
        pltpu.VMEM((rows, D), F32),
        pltpu.VMEM((HP, total, LANES), BF16),
        pltpu.VMEM((HP, HEAD_DIM, total), F32),
        pltpu.VMEM((4, BK, CQ), BF16),
        pltpu.VMEM((total, 3 * CW), BF16),
        pltpu.VMEM((2, rows, D), BF16),
        pltpu.VMEM((rows, D), BF16),
        pltpu.VMEM((D, 3 * CW), F32),
        pltpu.VMEM((2, D), F32),
        pltpu.VMEM((N_Z, n_x, 3) + w_block, BF16),
        pltpu.VMEM((n_x - 1, N_Z, 3) + w_block, BF16),
        pltpu.VMEM((3, N_Z) + w_block, BF16),
        pltpu.VMEM((N_Z, n_x, N_IN, 8, LANES), F32),
        pltpu.VMEM((n_dp - 1, 8, LANES), F32),
        pltpu.VMEM((N_Z, n_x, 8, LANES), F32),
        pltpu.VMEM((2, N_Z, n_x, 8, LANES), F32),
    ]
    for (r, c), order in zip(sizes, SCATTER_ORDERS):
        scratch += scatter_buffers(n_x, r, c, order)
    n_remote = 5 * scatter_count(n_x) + 3 + N_Z * (n_x - 1) + (n_dp - 1) + 3 + 3 * N_Z
    return pl.pallas_call(
        functools.partial(backward_kernel, n_dp, lens),
        out_shape=(
            jax.ShapeDtypeStruct((rows, D), BF16),
            jax.ShapeDtypeStruct((w_rows, 3 * CW), F32),
            jax.ShapeDtypeStruct(like_out.shape, F32),
            jax.ShapeDtypeStruct(t_up.shape[3:], F32),
            jax.ShapeDtypeStruct(like_down.shape, F32),
        )
        + tuple(jax.ShapeDtypeStruct((1, length), F32) for length in lens),
        in_specs=[ANY] * 14 + [VMEM] * 3,
        out_specs=(VMEM,) * 13,
        scratch_shapes=scratch + [pltpu.SemaphoreType.DMA((4,))] + sem_shapes(n_remote, 21),
        compiler_params=params(2, VMEM_LIMIT if n_dp <= 8 else VMEM_LIMIT + (1 << 20)),
        name="backward",
    )(
        tokens,
        seen,
        att,
        e_all,
        q,
        v,
        kt,
        h_one,
        n_one,
        wq,
        d_res,
        t_out,
        t_up,
        t_down,
        vec_all,
        sums,
        sum_up,
    )


def finish_kernel(n, *rest):
    for source, result in zip(rest[:n], rest[n:]):
        result[...] = source[...]


def finish(*arrays):
    n = len(arrays)
    return pl.pallas_call(
        functools.partial(finish_kernel, n),
        out_shape=tuple(jax.ShapeDtypeStruct(array.shape, array.dtype) for array in arrays),
        in_specs=[VMEM] * n,
        out_specs=(VMEM,) * n,
        compiler_params=pltpu.CompilerParams(vmem_limit_bytes=VMEM_LIMIT),
        name="finish",
    )(*arrays)


def on_device(
    tokens,
    lengths,
    w_qkv,
    bias_qv,
    w_out,
    bias_out,
    w_up,
    bias_up,
    w_down,
    bias_down,
    gain_one,
    shift_one,
    gain_two,
    shift_two,
    cotangent,
):
    n_dp = lax.axis_size("dp")
    n_x = n_dp // N_Z
    vectors = (
        bias_qv,
        bias_out,
        bias_up,
        bias_down,
        gain_one,
        shift_one,
        gain_two,
        shift_two,
    )
    lens = tuple(v.shape[0] for v in vectors)
    h_one, n_one, q, v, kt, att, e_all, mixed, a_out, a_up, a_down, vec_all, wq = forward(
        n_dp, tokens, lengths, w_qkv, vectors, w_out, w_up, w_down.T
    )

    def by_dp(blocks):
        return blocks.reshape((N_IN, n_dp) + blocks.shape[3:])

    output, d_res, seen, t_out, t_up, t_down, sums, sum_up = middle(
        n_dp,
        lens,
        tokens,
        mixed,
        by_dp(a_out) if packs(w_out.shape[0]) else a_out.reshape(N_IN, D, CW),
        a_up.reshape(N_IN, D, -1),
        by_dp(a_down),
        vec_all,
        cotangent,
    )

    def blocks(grads, like):
        return grads.reshape((2, N_Z, n_x) + like.shape[3:])

    grad_tokens, g_qkv, g_out, g_up, g_down, *vecs = backward(
        n_dp,
        lens,
        w_out,
        w_down.T,
        tokens,
        seen,
        att,
        e_all,
        q,
        v,
        kt,
        h_one,
        n_one,
        wq,
        d_res,
        blocks(t_out, a_out),
        blocks(t_up, a_up),
        blocks(t_down, a_down),
        vec_all,
        sums,
        sum_up,
    )
    output, grad_tokens, g_qkv, g_out, g_up, g_down, *vecs = finish(
        output, grad_tokens, g_qkv, g_out, g_up, g_down, *vecs
    )
    vecs = [vec.reshape(-1) for vec in vecs]
    return (
        output,
        grad_tokens,
        g_qkv,
        vecs[BIAS_QV],
        g_out,
        vecs[BIAS_OUT],
        g_up,
        vecs[BIAS_UP],
        g_down.T,
        vecs[BIAS_DOWN],
        vecs[GAIN_ONE],
        vecs[SHIFT_ONE],
        vecs[GAIN_TWO],
        vecs[SHIFT_TWO],
    )


def solution(mesh):
    rows = P(("dp", "inner"), None)
    mat = P("dp", "inner")
    vec = P(("dp", "inner"))
    return jax.shard_map(
        on_device,
        mesh=mesh,
        in_specs=(
            rows,
            P("dp", None),
            mat,
            vec,
            mat,
            vec,
            mat,
            vec,
            mat,
            vec,
            vec,
            vec,
            vec,
            vec,
            rows,
        ),
        out_specs=(rows, rows, mat, vec, mat, vec, mat, vec, mat, vec, vec, vec, vec, vec),
        check_vma=False,
    )
```
